128 devices in a mesh: section: 2 (over core), ctx: 16 (over y, x), wsh: 4 (over z).
Axes of the slice: x: 4, y: 4, z: 4, core: 2. Of those that a mesh axis runs over, the one named last changes fastest.
Arguments:
- tokens: float32 [2, 4, 2048, 960], P(None, 'wsh', 'ctx'), may hold values from -6 to 6
- cotangent: float32 [2, 4, 2048, 960], P(None, 'wsh', 'ctx'), may hold values from -6 to 6
- block_order: int32 [32], replicated, may hold values from 0 to 31, as said below
- norm_one: bfloat16 [2, 960], P('section', 'wsh'), may hold values from 0.5 to 1.5
- w_query: bfloat16 [2, 960, 960], P('section', 'wsh'), may hold values from -0.1875 to 0.1875
- w_key: bfloat16 [2, 960, 320], P('section', 'wsh'), may hold values from -0.1875 to 0.1875
- w_value: bfloat16 [2, 960, 320], P('section', 'wsh'), may hold values from -0.1875 to 0.1875
- w_out: bfloat16 [2, 960, 960], P('section', 'wsh'), may hold values from -1.5 to 1.5
- norm_two: bfloat16 [2, 960], P('section', 'wsh'), may hold values from 0.5 to 1.5
- w_gate: bfloat16 [2, 960, 2560], P('section', 'wsh'), may hold values from -0.1875 to 0.1875
- w_up: bfloat16 [2, 960, 2560], P('section', 'wsh'), may hold values from -0.1875 to 0.1875
- w_down: bfloat16 [2, 2560, 960], P('section', 'wsh'), may hold values from -0.125 to 0.125
Outputs:
- section_outputs: float32 [2, 2, 4, 2048, 960], P('section', None, 'wsh', 'ctx')
- input_grads: float32 [2, 2, 4, 2048, 960], P('section', None, 'wsh', 'ctx')
- grad_norm_one: float32 [2, 960], P('section', ('ctx', 'wsh'))
- grad_query: float32 [2, 960, 960], P('section', ('ctx', 'wsh'))
- grad_key: float32 [2, 960, 320], P('section', ('ctx', 'wsh'))
- grad_value: float32 [2, 960, 320], P('section', ('ctx', 'wsh'))
- grad_out: float32 [2, 960, 960], P('section', ('ctx', 'wsh'))
- grad_norm_two: float32 [2, 960], P('section', ('ctx', 'wsh'))
- grad_gate: float32 [2, 960, 2560], P('section', ('ctx', 'wsh'))
- grad_up: float32 [2, 960, 2560], P('section', ('ctx', 'wsh'))
- grad_down: float32 [2, 2560, 960], P('section', ('ctx', 'wsh'))
The draws below stay inside these ranges and needn't reach their ends.
Inputs may be any that keep to these rules, and one draw needn't show every extreme that they name: block_order is a permutation of the 32 blocks of a sequence, and entries 2 r and 2 r + 1 sum to 31.
All inputs are finite; a program needn't handle non-finite values.
Results may differ from the reference program's by a relative error of at most 0.028.
Values may be sent and summed in bfloat16 or wider, within the bound.
No kernel may reach another device: no remote copies, remote signals or barrier semaphores. Data moves between devices by JAX's collectives and lax.ppermute only.
A program may use at most 256 MiB of HBM per device.

```python
import math
from functools import partial
import jax
import jax.numpy as jnp
from jax import lax

D = 960
HEADS = 15
KV_HEADS = 5
HEAD = 64
FF = 2560
MB = 2
QW = 960
KW = 320
SEQ = 2048
BLK = 64
SEQS = 4
N_SECTION = 2


def draw_block_order(key, part):
    key = jax.random.fold_in(key, 11)
    pair_count = SEQ // (2 * BLK)
    order_key, flip_key = jax.random.split(key)
    pair_order = jax.random.permutation(order_key, pair_count)
    flip_bits = jax.random.randint(flip_key, (pair_count,), 0, 2)
    last_block = 2 * pair_count - 1
    first_block = jnp.where(flip_bits == 1, last_block - pair_order, pair_order)
    return jnp.stack([first_block, last_block - first_block], axis=1).reshape(2 * pair_count).astype(jnp.int32)


def level_of(rng, shape, cuts, least, largest):
    def one(dim, parts):
        heights = jax.random.uniform(jax.random.fold_in(jax.random.fold_in(rng, 6), dim), (parts,), jnp.float32, least / len(cuts), largest / len(cuts))
        return jnp.repeat(jnp.exp(heights), shape[dim] // parts).reshape((-1,) + (1,) * (len(shape) - dim - 1))

    loudness = one(*cuts[0])
    for cut in cuts[1:]:
        loudness = loudness * one(*cut)
    return loudness


def gaussian(stream_key, extent, deviation, bound, shards=(), kind=jnp.bfloat16):
    values = deviation * jax.random.normal(stream_key, extent, jnp.float32)
    if shards:
        values = values * level_of(stream_key, extent, shards, -0.22, 0.18)
    return jnp.clip(values, -bound, bound).astype(kind)


def setup_inputs(seed: int = 0) -> dict:
    keys = jax.random.split(jax.random.key(seed), 13)
    tokens = gaussian(keys[0], (MB, SEQS, SEQ, D), 1.0, 6.0, ((1, 4), (2, 16)), jnp.float32)
    cotangent = gaussian(keys[1], (MB, SEQS, SEQ, D), 1.0, 6.0, ((1, 4), (2, 16)), jnp.float32)
    block_order = draw_block_order(jax.random.fold_in(keys[12], 71), 0)
    norm_one = jnp.clip(1.0 + 0.1 * jax.random.normal(keys[3], (N_SECTION, D), jnp.float32), 0.5, 1.5).astype(jnp.bfloat16)
    w_query = gaussian(keys[4], (N_SECTION, D, QW), D ** -0.5, 0.1875, ((0, 2), (1, 4)))
    w_key = gaussian(keys[5], (N_SECTION, D, KW), D ** -0.5, 0.1875, ((0, 2), (1, 4)))
    w_value = gaussian(keys[6], (N_SECTION, D, KW), D ** -0.5, 0.1875, ((0, 2), (1, 4)))
    w_out = gaussian(keys[7], (N_SECTION, QW, D), 16 ** -0.5, 1.5, ((0, 2), (1, 4)))
    norm_two = jnp.clip(1.0 + 0.1 * jax.random.normal(keys[8], (N_SECTION, D), jnp.float32), 0.5, 1.5).astype(jnp.bfloat16)
    w_gate = gaussian(keys[9], (N_SECTION, D, FF), D ** -0.5, 0.1875, ((0, 2), (1, 4)))
    w_up = gaussian(keys[10], (N_SECTION, D, FF), D ** -0.5, 0.1875, ((0, 2), (1, 4)))
    w_down = gaussian(keys[11], (N_SECTION, FF, D), FF ** -0.5, 0.125, ((0, 2), (1, 4)))
    return dict(tokens=tokens, cotangent=cotangent, block_order=block_order, norm_one=norm_one, w_query=w_query, w_key=w_key, w_value=w_value, w_out=w_out, norm_two=norm_two, w_gate=w_gate, w_up=w_up, w_down=w_down)


EPS = 1e-05
ROPE_BASE = 10000.0

@jax.custom_vjp
def low(v):
    return lax.optimization_barrier(v.astype(jnp.bfloat16)).astype(jnp.float32)

@jax.custom_vjp
def low_back(v):
    return v

def low_keep(v):
    return (low(v), None)

def low_pass(kept, grad):
    return (grad,)

def back_keep(v):
    return (v, None)

def back_low(kept, grad):
    return (low(grad),)
low.defvjp(low_keep, low_pass)
low_back.defvjp(back_keep, back_low)

def matmul(left, right):
    return jnp.dot(left, right, preferred_element_type=jnp.float32, precision=lax.Precision.HIGHEST)

def norm_gain(source, gain_vec):
    return source * lax.rsqrt(lax.optimization_barrier(jnp.mean(source * source, axis=-1, keepdims=True)) + EPS) * gain_vec

def angles(positions):
    half_size = HEAD // 2
    frequency = jnp.exp(jnp.arange(half_size).astype(jnp.float32) * (-2.0 * math.log(ROPE_BASE) / HEAD))
    return positions.astype(jnp.float32)[:, None] * frequency[None, :]

def rotate(source, angle):
    half_size = source.shape[-1] // 2
    cosine = jnp.cos(angle)[:, None, :]
    sine = jnp.sin(angle)[:, None, :]
    first_half = source[..., :half_size]
    second_half = source[..., half_size:]
    return jnp.concatenate([first_half * cosine - second_half * sine, second_half * cosine + first_half * sine], axis=-1)

def attend(query, key, value, positions):
    seq_rows = query.shape[0]
    group_size = HEADS // KV_HEADS
    block_rows = math.gcd(seq_rows, 512)
    block_count = seq_rows // block_rows
    grouped = query.reshape(block_count, block_rows, KV_HEADS, group_size, HEAD)
    pos_blocks = positions.reshape(block_count, block_rows)

    def one_block(pieces):
        query_block, pos_block = pieces
        scores = jnp.einsum('qkgd,tkd->kgqt', query_block, key, precision=lax.Precision.HIGHEST) * HEAD ** (-0.5)
        scores = jnp.where(pos_block[:, None] >= positions[None, :], scores, -1e+30)
        scores = low_back(scores)
        row_top = lax.optimization_barrier(jnp.max(scores, axis=-1, keepdims=True))
        exponent = jnp.exp(scores - row_top)
        probabilities = exponent / lax.optimization_barrier(jnp.sum(exponent, axis=-1, keepdims=True))
        result = jnp.einsum('kgqt,tkd->qkgd', low(probabilities), value, precision=lax.Precision.HIGHEST)
        return result.reshape(block_rows, HEADS * HEAD)
    results = lax.map(jax.checkpoint(one_block), (grouped, pos_blocks))
    return results.reshape(seq_rows, HEADS * HEAD)

def layer(layer_in, positions, params):
    gain_one, wq_full, wk_full, wv_full, wo_full, gain_two, wg_full, wu_full, wd_full = params
    seq_rows = layer_in.shape[0]
    angle = angles(positions)
    normed = low(norm_gain(layer_in, gain_one))
    query = low(rotate(low_back(matmul(normed, wq_full)).reshape(seq_rows, HEADS, HEAD), angle))
    key = low(rotate(low_back(matmul(normed, wk_full)).reshape(seq_rows, KV_HEADS, HEAD), angle))
    value = low(low_back(matmul(normed, wv_full))).reshape(seq_rows, KV_HEADS, HEAD)
    query = query.reshape(seq_rows, KV_HEADS, HEADS // KV_HEADS, HEAD)
    mixed = low(low_back(attend(query, key, value, positions)))
    resid = layer_in + low_back(matmul(mixed, wo_full))
    second = low(norm_gain(resid, gain_two))
    gate = low_back(matmul(second, wg_full))
    up_proj = low_back(matmul(second, wu_full))
    hidden = low(jax.nn.silu(gate) * up_proj)
    return resid + low_back(matmul(hidden, wd_full))

def reference(tokens, cotangent, block_order, norm_one, w_query, w_key, w_value, w_out, norm_two, w_gate, w_up, w_down):
    section_count = norm_one.shape[0]
    seq_rows = jnp.arange(SEQ, dtype=jnp.int32)
    positions = jnp.take(block_order, seq_rows // BLK).astype(jnp.int32) * BLK + seq_rows % BLK
    params = tuple((weight_arg.astype(jnp.float32) for weight_arg in (norm_one, w_query, w_key, w_value, w_out, norm_two, w_gate, w_up, w_down)))
    flat_tokens = tokens.astype(jnp.float32).reshape(MB * SEQS, SEQ, D)
    extras = jnp.zeros((section_count - 1, MB * SEQS, SEQ, D), jnp.float32)

    def forward(flat_in, extra_in, param_in):
        state = flat_in
        section_outs = []
        for section_number in range(section_count):
            if section_number > 0:
                state = state + extra_in[section_number - 1]
            section_params = tuple((item[section_number] for item in param_in))
            state = jax.vmap(partial(layer, positions=positions, params=section_params))(state)
            section_outs.append(state)
        return (state, jnp.stack(section_outs))
    final_out, pullback, section_outputs = jax.vjp(forward, flat_tokens, extras, params, has_aux=True)
    d_tokens, d_extras, d_params = pullback(cotangent.astype(jnp.float32).reshape(MB * SEQS, SEQ, D))
    input_grads = jnp.concatenate([d_tokens[None], d_extras], axis=0).reshape(section_count, MB, SEQS, SEQ, D)
    section_outputs = section_outputs.reshape(section_count, MB, SEQS, SEQ, D)
    return (section_outputs, input_grads, d_params[0], d_params[1], d_params[2], d_params[3], d_params[4], d_params[5], d_params[6], d_params[7], d_params[8])
```

```python
import math

import jax
import jax.numpy as jnp
from jax import lax
from jax.experimental import pallas as pl
from jax.experimental.pallas import tpu as pltpu
from jax.sharding import PartitionSpec as P

HEADS = 15
KV_HEADS = 5
HEAD = 64
GROUP = HEADS // KV_HEADS
D = 960
FF = 2560
KW = KV_HEADS * HEAD
ROWS = 128
BLK = 64
SEQ = 2048
CHUNK = 256
STEPS = 9
EPS = 1e-05
ROPE_BASE = 10000.0
BF = jnp.bfloat16
F32 = jnp.float32
QP = 1024
NEG = -1e30
VMEM_BYTES = 48 * 1024 * 1024

NN = (((1,), (0,)), ((), ()))
NT = (((1,), (1,)), ((), ()))
TN = (((0,), (0,)), ((), ()))


def dot(left, right, dims=NN):
    return lax.dot_general(left, right, dims, preferred_element_type=F32)


def call(body, outs, scratch=(), smem=0):
    def run(*args):
        in_specs = [
            pl.BlockSpec(memory_space=pltpu.SMEM if i < smem else pltpu.VMEM)
            for i in range(len(args))
        ]
        out = pl.pallas_call(
            body,
            in_specs=in_specs,
            out_specs=[pl.BlockSpec(memory_space=pltpu.VMEM) for _ in outs],
            out_shape=[jax.ShapeDtypeStruct(s, t) for s, t in outs],
            scratch_shapes=list(scratch),
            compiler_params=pltpu.CompilerParams(vmem_limit_bytes=VMEM_BYTES),
        )(*args)
        return out

    return run


def lane(shape):
    return lax.broadcasted_iota(jnp.int32, shape, 1)


def normalise(x, gain):
    return x * lax.rsqrt(jnp.mean(x * x, axis=-1, keepdims=True) + EPS) * gain


def norm_back(x, gain, dy):
    r = lax.rsqrt(jnp.mean(x * x, axis=-1, keepdims=True) + EPS)
    cdy = gain * dy
    dx = r * cdy - x * (r * r * r) * jnp.mean(x * cdy, axis=-1, keepdims=True)
    dc = jnp.sum(dy * x * r, axis=0, keepdims=True)
    return dx, dc


def spin(tile, cosine, sine):
    first = (lane(tile.shape) % HEAD) < HEAD // 2
    swapped = jnp.where(first, pltpu.roll(tile, 96, 1), pltpu.roll(tile, 32, 1))
    return tile * cosine + swapped * sine


def project_body(count):
    def body(*refs):
        base = refs[0]
        parts = refs[1 : 1 + count]
        gain, weight, cosine, sine, x_out, normed_out, q_out, kv_out = refs[1 + count :]
        x = base[...]
        for part in parts:
            x = x + part[...].astype(F32)
        x_out[...] = x
        normed = normalise(x, gain[...]).astype(BF)
        normed_out[...] = normed
        cos, sin = cosine[...], sine[...]
        qkv = dot(normed, weight[...])
        for j in range(8):
            tile = spin(qkv[:, j * 128 : (j + 1) * 128], cos, sin)
            q_out[:, j * 128 : (j + 1) * 128] = (tile * (HEAD**-0.5)).astype(BF)
        for g in range(KV_HEADS):
            tile = qkv[:, QP + g * 128 : QP + (g + 1) * 128]
            tile = jnp.where(lane(tile.shape) < HEAD, spin(tile, cos, sin), tile)
            kv_out[:, g * 128 : (g + 1) * 128] = tile.astype(BF)

    return body


def project(base, parts, gain, weight, cosine, sine):
    outs = [((ROWS, D), F32), ((ROWS, D), BF), ((ROWS, QP), BF), ((ROWS, 2 * KW), BF)]
    return call(project_body(len(parts)), outs)(base, *parts, gain, weight, cosine, sine)


def step_place(info, t):
    first, second = info[0], info[1]
    count = first // 4 + 1
    early = t < count
    block = jnp.where(early, 0, 1)
    chunk = jnp.where(early, t, t - count)
    place = jnp.where(early, first, second)
    return block, chunk, place


def causal(place, chunk):
    rows = lax.broadcasted_iota(jnp.int32, (BLK, CHUNK), 0) + place * BLK
    cols = lax.broadcasted_iota(jnp.int32, (BLK, CHUNK), 1) + chunk * CHUNK
    one = rows >= cols
    return jnp.concatenate([one] * GROUP, axis=0)


def head_tile(ref, block, head, upper):
    j = head // 2
    tile = ref[block * BLK : (block + 1) * BLK, j * 128 : (j + 1) * 128].astype(F32)
    if (head % 2 == 1) != upper:
        tile = pltpu.roll(tile, 64, 1)
    keep = (lane(tile.shape) >= HEAD) if upper else (lane(tile.shape) < HEAD)
    return jnp.where(keep, tile, 0.0)


def attend_body(count):
    def body(*refs):
        info, q_ref = refs[0], refs[1]
        pieces = refs[2 : 2 + count]
        (wo, x_ref, gain, mixed_out, lse_out, kvs, resid_out, second_out) = refs[2 + count : 10 + count]
        qh, top, total, acc = refs[10 + count :]
        number = 0
        for piece in pieces:
            for b in range(piece.shape[0] // BLK):
                at = pl.multiple_of(info[2 + number] * BLK, BLK)
                kvs[pl.ds(at, BLK), :] = piece[b * BLK : (b + 1) * BLK, :]
                number += 1
        for i in range(2):
            for g in range(KV_HEADS):
                for r in range(GROUP):
                    qh[i, g, r * BLK : (r + 1) * BLK, :] = head_tile(
                        q_ref, i, g * GROUP + r, False
                    ).astype(BF)
        top[...] = jnp.full(top.shape, NEG, F32)
        total[...] = jnp.zeros(total.shape, F32)
        acc[...] = jnp.zeros(acc.shape, F32)

        def step(t, carry):
            block, chunk, place = step_place(info, t)
            allowed = causal(place, chunk)
            at = pl.multiple_of(chunk * CHUNK, CHUNK)
            for g in range(KV_HEADS):
                keys = kvs[pl.ds(at, CHUNK), g * 128 : (g + 1) * 128]
                scores = dot(qh[block, g], keys, NT)
                scores = jnp.where(allowed, scores, NEG)
                old = top[block, g]
                new = jnp.maximum(old, jnp.max(scores, axis=1, keepdims=True))
                probs = jnp.exp(scores - jnp.concatenate([new, new], axis=1))
                shrink = jnp.exp(old - new)
                top[block, g] = new
                total[block, g] = shrink * total[block, g] + jnp.sum(probs, axis=1, keepdims=True)
                acc[block, g] = shrink * acc[block, g] + dot(probs.astype(BF), keys)
            return carry

        lax.fori_loop(0, STEPS, step, 0)
        for i in range(2):
            heads = []
            for g in range(KV_HEADS):
                sums = total[i, g]
                result = acc[i, g] / sums
                lse_out[i, g] = top[i, g] + jnp.log(sums)
                for r in range(GROUP):
                    heads.append(result[r * BLK : (r + 1) * BLK, :])
            for j in range(8):
                low = pltpu.roll(heads[2 * j], 64, 1)
                rows = slice(i * BLK, (i + 1) * BLK)
                if j < 7:
                    tile = jnp.where(lane(low.shape) < HEAD, low, heads[2 * j + 1])
                    mixed_out[rows, j * 128 : (j + 1) * 128] = tile.astype(BF)
                else:
                    mixed_out[rows, 896:960] = low[:, :64].astype(BF)
        resid = x_ref[...] + dot(mixed_out[...], wo[...])
        resid_out[...] = resid
        second_out[...] = normalise(resid, gain[...]).astype(BF)

    return body


def attend(info, q, pieces, wo, x, gain):
    outs = [
        ((ROWS, D), BF),
        ((2, KV_HEADS, GROUP * BLK, 128), F32),
        ((SEQ, 2 * KW), BF),
        ((ROWS, D), F32),
        ((ROWS, D), BF),
    ]
    shape = (2, KV_HEADS, GROUP * BLK, 128)
    scratch = [pltpu.VMEM(shape, BF)] + [pltpu.VMEM(shape, F32)] * 3
    return call(attend_body(len(pieces)), outs, scratch, smem=1)(info, q, *pieces, wo, x, gain)


def feed_body(second, wgu, wd, gu_out, hidden_out, part_out):
    gu = dot(second[...], wgu[...])
    gu_out[...] = gu
    gate, up = gu[:, : FF // 4], gu[:, FF // 4 :]
    hidden = (gate / (1.0 + jnp.exp(-gate)) * up).astype(BF)
    hidden_out[...] = hidden
    part_out[...] = dot(hidden, wd[...]).astype(BF)


def feed(second, wgu, wd):
    outs = [((ROWS, FF // 2), F32), ((ROWS, FF // 4), BF), ((ROWS, D), BF)]
    return call(feed_body, outs)(second, wgu, wd)


def feed_back_body(grad_low, gu, wgu, wd, dgu_out, part_out):
    d_hidden = dot(grad_low[...], wd[...], NT)
    gate, up = gu[:, : FF // 4], gu[:, FF // 4 :]
    sig = 1.0 / (1.0 + jnp.exp(-gate))
    d_gate = d_hidden * up * sig * (1.0 + gate * (1.0 - sig))
    d_up = d_hidden * gate * sig
    dgu_out[:, : FF // 4] = d_gate.astype(BF)
    dgu_out[:, FF // 4 :] = d_up.astype(BF)
    part_out[...] = dot(dgu_out[...], wgu[...], NT).astype(BF)


def feed_back(grad_low, gu, wgu, wd):
    outs = [((ROWS, FF // 2), BF), ((ROWS, D), BF)]
    return call(feed_back_body, outs)(grad_low, gu, wgu, wd)


def attend_back_body(
    info, p0, p1, p2, p3, grad, resid, gain, wo, mixed, q_ref, lse, kvs, cosine, sine,
    d_resid_out, d_low_out, dc_out, dq_out, o0, o1, o2, o3,
    qd, delta, dq, dkv, dm, mx,
):
    d_second = p0[...].astype(F32) + p1[...].astype(F32) + p2[...].astype(F32) + p3[...].astype(F32)
    dx, dc = norm_back(resid[...], gain[...], d_second)
    dc_out[...] = dc
    d_resid = grad[...] + dx
    d_resid_out[...] = d_resid
    low = d_resid.astype(BF)
    d_low_out[...] = low
    dm[:, :D] = dot(low, wo[...], NT).astype(BF)
    dm[:, D:] = jnp.zeros((ROWS, QP - D), BF)
    mx[:, :D] = mixed[...]
    mx[:, D:] = jnp.zeros((ROWS, QP - D), BF)
    span = GROUP * BLK
    for i in range(2):
        for g in range(KV_HEADS):
            for r in range(GROUP):
                head = g * GROUP + r
                there = slice(r * BLK, (r + 1) * BLK)
                qd[i, g, there, :] = head_tile(q_ref, i, head, False).astype(BF)
                do = head_tile(dm, i, head, True)
                qd[i, g, span + r * BLK : span + (r + 1) * BLK, :] = do.astype(BF)
                dots = jnp.sum(do * head_tile(mx, i, head, True), axis=1, keepdims=True)
                delta[i, g, there, :] = jnp.broadcast_to(dots, (BLK, 128))
    dq[...] = jnp.zeros(dq.shape, F32)
    dkv[...] = jnp.zeros(dkv.shape, F32)

    def step(t, carry):
        block, chunk, place = step_place(info, t)
        allowed = causal(place, chunk)
        at = pl.multiple_of(chunk * CHUNK, CHUNK)
        for g in range(KV_HEADS):
            keys = kvs[pl.ds(at, CHUNK), g * 128 : (g + 1) * 128]
            both = dot(qd[block, g], keys, NT)
            scores, d_probs = both[:span], both[span:]
            total = lse[block, g]
            probs = jnp.exp(
                jnp.where(allowed, scores, NEG) - jnp.concatenate([total, total], axis=1)
            )
            shift = delta[block, g]
            d_scores = probs * (d_probs - jnp.concatenate([shift, shift], axis=1))
            d_low = d_scores.astype(BF)
            dq[block, g] += dot(d_low, keys)
            stacked = jnp.concatenate([d_low, probs.astype(BF)], axis=0)
            dkv[pl.ds(at, CHUNK), g * 128 : (g + 1) * 128] += dot(stacked, qd[block, g], TN)
        return carry

    lax.fori_loop(0, STEPS, step, 0)
    for i in range(2):
        rows = slice(i * BLK, (i + 1) * BLK)
        cos, sin = cosine[rows, :], sine[rows, :]
        heads = []
        for g in range(KV_HEADS):
            for r in range(GROUP):
                heads.append(dq[i, g, r * BLK : (r + 1) * BLK, :] * (HEAD**-0.5))
        for j in range(8):
            if j < 7:
                high = pltpu.roll(heads[2 * j + 1], 64, 1)
                tile = jnp.where(lane(high.shape) < HEAD, heads[2 * j], high)
                dq_out[rows, j * 128 : (j + 1) * 128] = spin(tile, cos, -sin).astype(BF)
            else:
                dq_out[rows, 896:960] = spin(heads[14], cos, -sin)[:, :64].astype(BF)
    number = 0
    for out in (o0, o1, o2, o3):
        for b in range(out.shape[0] // BLK):
            at = pl.multiple_of(info[34 + number] * BLK, BLK)
            out[b * BLK : (b + 1) * BLK, :] = dkv[pl.ds(at, BLK), :].astype(BF)
            number += 1


def attend_back(info, parts, grad, resid, gain, wo, mixed, q, lse, kvs, cosine, sine):
    outs = [
        ((ROWS, D), F32),
        ((ROWS, D), BF),
        ((1, D), F32),
        ((ROWS, D), BF),
    ] + [((4 * ROWS, 2 * KW), BF)] * 4
    shape = (2, KV_HEADS, GROUP * BLK, 128)
    scratch = [
        pltpu.VMEM((2, KV_HEADS, 2 * GROUP * BLK, 128), BF),
        pltpu.VMEM(shape, F32),
        pltpu.VMEM(shape, F32),
        pltpu.VMEM((SEQ, 2 * KW), F32),
        pltpu.VMEM((ROWS, QP), BF),
        pltpu.VMEM((ROWS, QP), BF),
    ]
    return call(attend_back_body, outs, scratch, smem=1)(
        info, *parts, grad, resid, gain, wo, mixed, q, lse, kvs, cosine, sine
    )


def project_back_body(
    k0, k1, k2, k3, dq, d_resid, x_ref, gain, weight, cosine, sine, dkv_out, grad_out, dc_out
):
    sums = k0[...].astype(F32) + k1[...].astype(F32) + k2[...].astype(F32) + k3[...].astype(F32)
    cos, sin = cosine[...], -sine[...]
    for g in range(KV_HEADS):
        tile = sums[:, g * 128 : (g + 1) * 128]
        tile = jnp.where(lane(tile.shape) < HEAD, spin(tile, cos, sin), tile)
        dkv_out[:, g * 128 : (g + 1) * 128] = tile.astype(BF)
    d_normed = dot(dq[...], weight[:, :D], NT) + dot(dkv_out[...], weight[:, QP:], NT)
    dx, dc = norm_back(x_ref[...], gain[...], d_normed)
    dc_out[...] = dc
    grad_out[...] = d_resid[...] + dx


def project_back(pieces, dq, d_resid, x, gain, weight, cosine, sine):
    outs = [((ROWS, 2 * KW), BF), ((ROWS, D), F32), ((1, D), F32)]
    return call(project_back_body, outs)(*pieces, dq, d_resid, x, gain, weight, cosine, sine)


def z_shift(value, steps):
    return lax.ppermute(value, "wsh", [(i, (i + steps) % 4) for i in range(4)])


def x_shift(value, steps):
    pairs = [(y * 4 + x, y * 4 + (x + steps) % 4) for y in range(4) for x in range(4)]
    return lax.ppermute(value, "ctx", pairs)


def y_shift(value, steps):
    pairs = [(y * 4 + x, ((y + steps) % 4) * 4 + x) for y in range(4) for x in range(4)]
    return lax.ppermute(value, "ctx", pairs)


def swap(value):
    return lax.ppermute(value, "section", [(0, 1), (1, 0)])


def reduce_ctx(value):
    rank = lax.axis_index("ctx")
    y, x = rank // 4, rank % 4
    cut = value.reshape((4, 4) + value.shape[1:])
    total = lax.dynamic_index_in_dim(cut, y, 0, False).astype(F32)
    for k in (1, 3, 2):
        total = total + y_shift(lax.dynamic_index_in_dim(cut, (y + k) % 4, 0, False), k).astype(F32)
    low = total.astype(BF)
    out = lax.dynamic_index_in_dim(total, x, 0, False)
    for k in (1, 3, 2):
        out = out + x_shift(lax.dynamic_index_in_dim(low, (x + k) % 4, 0, False), k).astype(F32)
    return out


def in_order(pieces, rank):
    stacked = jnp.stack(pieces)
    return [lax.dynamic_index_in_dim(stacked, (rank - z) % 4, 0, False) for z in range(4)]


def shards(
    tokens, cotangent, block_order, norm_one, w_query, w_key, w_value, w_out, norm_two, w_gate, w_up, w_down
):
    section = lax.axis_index("section")
    rank = lax.axis_index("ctx")
    z_rank = lax.axis_index("wsh")
    first_core = section == 0
    quarter = FF // 4

    key_value = jnp.concatenate(
        [w_key[0].reshape(-1, KV_HEADS, HEAD), w_value[0].reshape(-1, KV_HEADS, HEAD)], axis=2
    ).reshape(-1, 2 * KW)
    shard_qkv = jnp.concatenate(
        [w_query[0], jnp.zeros((w_query.shape[1], QP - D), BF), key_value], axis=1
    )
    gains = jnp.stack([norm_one[0], norm_two[0]])
    gain_parts = [gains] + [z_shift(gains, k) for k in (1, 2, 3)]
    gains = jnp.concatenate(in_order(gain_parts, z_rank), axis=1)

    def both(value):
        other = swap(value)
        return jnp.where(first_core, value, other), jnp.where(first_core, other, value)

    gain_pair = [g.astype(F32) for g in both(gains)]
    wqkv = both(lax.all_gather(shard_qkv, "wsh", axis=0, tiled=True))
    wo = both(lax.all_gather(w_out[0], "wsh", axis=0, tiled=True))
    def columns(z):
        start = z * quarter
        return jnp.concatenate(
            [
                lax.dynamic_slice_in_dim(w_gate[0], start, quarter, 1),
                lax.dynamic_slice_in_dim(w_up[0], start, quarter, 1),
            ],
            axis=1,
        )

    wgu_parts = [columns(z_rank)] + [z_shift(columns((z_rank + k) % 4), k) for k in (1, 2, 3)]
    wgu = both(jnp.concatenate(in_order(wgu_parts, z_rank), axis=0))
    wd = both(w_down[0])

    own = lax.dynamic_slice_in_dim(block_order, 2 * rank, 2, 0)
    pairs = block_order.reshape(4, 4, 2)
    y, x = rank // 4, rank % 4
    step = jnp.arange(4, dtype=jnp.int32)
    came = pairs[(y - step) % 4][:, (x - step) % 4].reshape(32)
    goes = pairs[(y + step) % 4][:, (x + step) % 4].reshape(32)
    info = jnp.concatenate([own, came, goes]).astype(jnp.int32)
    offsets = jnp.arange(BLK, dtype=jnp.int32)
    local_pos = (own[:, None] * BLK + offsets[None, :]).reshape(ROWS)
    frequency = jnp.exp(
        jnp.arange(HEAD // 2).astype(F32) * (-2.0 * math.log(ROPE_BASE) / HEAD)
    )
    angle = local_pos.astype(F32)[:, None] * frequency[None, :]
    cos32, sin32 = jnp.cos(angle), jnp.sin(angle)
    cosine = jnp.concatenate([cos32] * 4, axis=1)
    sine = jnp.concatenate([-sin32, sin32, -sin32, sin32], axis=1)

    micro = section
    own_tokens = lax.dynamic_index_in_dim(tokens, micro, 0, False)[0]
    own_cotangent = lax.dynamic_index_in_dim(cotangent, micro, 0, False)[0]

    saved = []
    base, parts = own_tokens, []
    for layer in range(2):
        gain_one = gain_pair[layer][0:1]
        gain_two = gain_pair[layer][1:2]
        x_in, normed, q, kv = project(base, parts, gain_one, wqkv[layer], cosine, sine)
        row = jnp.concatenate([kv] + [x_shift(kv, k) for k in (1, 2, 3)], axis=0)
        pieces = [row] + [y_shift(row, k) for k in (1, 2, 3)]
        mixed, lse, kvs, resid, second = attend(info, q, pieces, wo[layer], x_in, gain_two)
        seconds = [second] + [z_shift(second, k) for k in (1, 2, 3)]
        fed = [feed(s, wgu[layer], wd[layer]) for s in seconds]
        parts = [fed[0][2]] + [z_shift(fed[k][2], -k) for k in (1, 2, 3)]
        base = resid
        saved.append(
            dict(
                x=x_in, normed=normed, q=q, mixed=mixed, lse=lse, kvs=kvs, resid=resid,
                seconds=jnp.concatenate(seconds), gu=[f[0] for f in fed],
                hidden=jnp.concatenate([f[1] for f in fed]),
            )
        )
    final = base
    for part in parts:
        final = final + part.astype(F32)
    outputs = [saved[1]["x"], final]

    grad = own_cotangent
    input_grads = [None, None]
    sums = [None, None]
    for layer in (1, 0):
        s = saved[layer]
        gain_one = gain_pair[layer][0:1]
        gain_two = gain_pair[layer][1:2]
        low = grad.astype(BF)
        lows = [low] + [z_shift(low, k) for k in (1, 2, 3)]
        back = [feed_back(lows[k], s["gu"][k], wgu[layer], wd[layer]) for k in range(4)]
        parts = [back[0][1]] + [z_shift(back[k][1], -k) for k in (1, 2, 3)]
        dgu = jnp.concatenate([b[0] for b in back])
        grad_gu = dot(s["seconds"], dgu, TN)
        grad_down = dot(s["hidden"], jnp.concatenate(lows), TN)
        d_resid, d_low, dc_two, dq, k0, k1, k2, k3 = attend_back(
            info, parts, grad, s["resid"], gain_two, wo[layer], s["mixed"], s["q"], s["lse"], s["kvs"], cosine, sine
        )
        row = k0.astype(F32)
        for k, piece in ((1, k1), (3, k3), (2, k2)):
            row = row + y_shift(piece, k).astype(F32)
        row = row.astype(BF).reshape(4, ROWS, 2 * KW)
        own_pieces = [row[0]] + [x_shift(row[k], k) for k in (1, 2, 3)]
        dkv, grad, dc_one = project_back(
            own_pieces, dq, d_resid, s["x"], gain_one, wqkv[layer], cosine, sine
        )
        input_grads[layer] = grad
        dkv_heads = dkv.reshape(ROWS, KV_HEADS, 2 * HEAD)
        dk = dkv_heads[:, :, :HEAD].reshape(ROWS, KW)
        dv = dkv_heads[:, :, HEAD:].reshape(ROWS, KW)
        cut = jnp.concatenate(
            [
                jnp.concatenate(
                    [
                        dq[:, z * 240 : (z + 1) * 240],
                        dk[:, z * 80 : (z + 1) * 80],
                        dv[:, z * 80 : (z + 1) * 80],
                        d_low[:, z * 240 : (z + 1) * 240],
                    ],
                    axis=1,
                )[None]
                for z in range(4)
            ]
        )
        mine = [lax.dynamic_index_in_dim(cut, z_rank, 0, False)] + [
            z_shift(lax.dynamic_index_in_dim(cut, (z_rank + k) % 4, 0, False), k) for k in (1, 2, 3)
        ]
        mine = jnp.concatenate(mine)
        ahead = jnp.concatenate([s["normed"], s["mixed"]], axis=1)
        ahead = jnp.concatenate([ahead] + [z_shift(ahead, k) for k in (1, 2, 3)])
        grad_qkv = dot(ahead[:, :D], mine[:, :400], TN)
        grad_out = dot(ahead[:, D:], mine[:, 400:], TN)
        halves = (
            jnp.concatenate([grad_gu[:, :quarter], grad_qkv[:, :320], dc_one.T], axis=1),
            jnp.concatenate([grad_gu[:, quarter:], grad_qkv[:, 320:], grad_out, dc_two.T], axis=1),
        )
        downs = (grad_down[:, :480], grad_down[:, 480:])

        def shared(pair):
            keep = jnp.where(first_core, pair[0], pair[1])
            give = jnp.where(first_core, pair[1], pair[0])
            return (keep + swap(give.astype(BF)).astype(F32)).astype(BF)

        part_a = reduce_ctx(shared(halves).reshape(16, 60, 961))
        part_b = reduce_ctx(shared(downs).reshape(16, 40, 480))
        sums[layer] = (part_a, part_b)

    def meet(index):
        mine = jnp.where(first_core, sums[0][index], sums[1][index])
        other = swap(jnp.where(first_core, sums[1][index], sums[0][index]))
        return mine, other

    own_a, other_a = meet(0)
    own_b, other_b = meet(1)
    half_a = (jnp.where(first_core, own_a, other_a), jnp.where(first_core, other_a, own_a))
    half_b = (jnp.where(first_core, own_b, other_b), jnp.where(first_core, other_b, own_b))
    joined = jnp.concatenate(half_a, axis=1).reshape(4, 15, 1922)
    pieces = [lax.dynamic_index_in_dim(joined, z_rank, 0, False)] + [
        z_shift(lax.dynamic_index_in_dim(joined, (z_rank + k) % 4, 0, False), k) for k in (1, 2, 3)
    ]
    pieces = in_order(pieces, z_rank)

    def spread(start, width):
        return jnp.concatenate([p[:, start : start + width] for p in pieces], axis=1)[None]

    grad_gate = spread(0, 640)
    grad_query = spread(640, 240)
    grad_key = spread(880, 80)
    gain_one_sum = sum(p[:, 960] for p in pieces)[None]
    grad_up = spread(961, 640)
    grad_value = spread(1601, 80)
    grad_out = spread(1681, 240)
    gain_two_sum = sum(p[:, 1921] for p in pieces)[None]
    down = jnp.concatenate(half_b, axis=1)
    moves = [(c * 4 + z, (4 * z + c // 4) * 4 + c % 4) for c in range(16) for z in range(4)]
    grad_down = lax.ppermute(down, ("ctx", "wsh"), moves)[None]
    def arranged(pair):
        mine = jnp.where(first_core, pair[0], pair[1])
        other = swap(jnp.where(first_core, pair[1], pair[0]))
        first = jnp.where(first_core, mine, other)
        last = jnp.where(first_core, other, mine)
        return jnp.stack([first, last])[None, :, None]

    return (
        arranged(outputs),
        arranged(input_grads),
        gain_one_sum,
        grad_query,
        grad_key,
        grad_value,
        grad_out,
        gain_two_sum,
        grad_gate,
        grad_up,
        grad_down,
    )


def solution(mesh):
    rows = P(None, "wsh", "ctx", None)
    gain = P("section", "wsh")
    weight = P("section", "wsh", None)
    in_specs = (rows, rows, P(), gain, weight, weight, weight, weight, gain, weight, weight, weight)
    result = P("section", None, "wsh", "ctx", None)
    gain_out = P("section", ("ctx", "wsh"))
    weight_out = P("section", ("ctx", "wsh"), None)
    out_specs = (
        result, result, gain_out, weight_out, weight_out, weight_out, weight_out, gain_out,
        weight_out, weight_out, weight_out,
    )
    return jax.shard_map(shards, mesh=mesh, in_specs=in_specs, out_specs=out_specs, check_vma=False)
```

```python
import math
from functools import partial

import jax
import jax.numpy as jnp
from jax import lax
from jax.experimental import pallas as pl
from jax.experimental.pallas import tpu as pltpu
from jax.sharding import PartitionSpec as P

HEADS = 15
KV_HEADS = 5
HEAD = 64
GROUP = HEADS // KV_HEADS
D = 960
FF = 2560
KW = KV_HEADS * HEAD
ROWS = 128
BLK = 64
SEQ = 2048
CHUNK = 256
STEPS = 9
EPS = 1e-05
ROPE_BASE = 10000.0
BF = jnp.bfloat16
F32 = jnp.float32
QP = 1024
HALF = 896
NEG = -1e30
VMEM_BYTES = 48 * 1024 * 1024

NN = (((1,), (0,)), ((), ()))
NT = (((1,), (1,)), ((), ()))
TN = (((0,), (0,)), ((), ()))


def dot(left, right, dims=NN):
    return lax.dot_general(left, right, dims, preferred_element_type=F32)


def call(body, outs, micros, scratch=(), smem=0):
    def run(*args, after=()):
        count = len(args)
        in_specs = [
            pl.BlockSpec(memory_space=pltpu.SMEM if i < smem else pltpu.VMEM) for i in range(count)
        ] + [pl.BlockSpec(memory_space=pl.ANY) for _ in after]

        def inner(*refs):
            body(*refs[:count], *refs[count + len(after) :])

        out = pl.pallas_call(
            inner,
            in_specs=in_specs,
            out_specs=[pl.BlockSpec(memory_space=pltpu.VMEM) for _ in outs],
            out_shape=[jax.ShapeDtypeStruct(s, t) for s, t in outs],
            scratch_shapes=list(scratch),
            cost_estimate=pl.CostEstimate(
                flops=int(micros * 1.1e9), bytes_accessed=int(micros * 3.6e6), transcendentals=0
            ),
            compiler_params=pltpu.CompilerParams(vmem_limit_bytes=VMEM_BYTES),
        )(*args, *after)
        return out

    return run


def lane(shape):
    return lax.broadcasted_iota(jnp.int32, shape, 1)


def normalise(x, gain):
    return x * lax.rsqrt(jnp.mean(x * x, axis=-1, keepdims=True) + EPS) * gain


def norm_back(x, gain, dy):
    r = lax.rsqrt(jnp.mean(x * x, axis=-1, keepdims=True) + EPS)
    cdy = gain * dy
    dx = r * cdy - x * (r * r * r) * jnp.mean(x * cdy, axis=-1, keepdims=True)
    dc = jnp.sum(dy * x * r, axis=0, keepdims=True)
    return dx, dc


def spin(tile, cosine, sine):
    first = (lane(tile.shape) % HEAD) < HEAD // 2
    swapped = jnp.where(first, pltpu.roll(tile, 96, 1), pltpu.roll(tile, 32, 1))
    return tile * cosine + swapped * sine


def project_body(count):
    def body(*refs):
        info, base = refs[:2]
        parts = refs[2 : 2 + count]
        (gain, own, other, cosine, sine, x_out, normed_out, q_out, kv_out, halves) = refs[2 + count :]
        side = info[0]
        x = base[...]
        for part in parts:
            x = x + part[...].astype(F32)
        x_out[...] = x
        normed = normalise(x, gain[...]).astype(BF)
        normed_out[...] = normed
        cos, sin = cosine[...], sine[...]
        halves[side] = dot(normed, own[:, :HALF])
        halves[1 - side] = dot(normed, other[:, :HALF])
        for j in range(8):
            tile = halves[0, :, j * 128 : (j + 1) * 128] if j < 7 else halves[1, :, 0:128]
            q_out[:, j * 128 : (j + 1) * 128] = (spin(tile, cos, sin) * (HEAD**-0.5)).astype(BF)
        for g in range(KV_HEADS):
            tile = halves[1, :, (g + 1) * 128 : (g + 2) * 128]
            tile = jnp.where(lane(tile.shape) < HEAD, spin(tile, cos, sin), tile)
            kv_out[:, g * 128 : (g + 1) * 128] = tile.astype(BF)

    return body


def project(info, base, parts, gain, weight, cosine, sine, after=()):
    outs = [((ROWS, D), F32), ((ROWS, D), BF), ((ROWS, QP), BF), ((ROWS, 2 * KW), BF)]
    scratch = [pltpu.VMEM((2, ROWS, HALF), F32)]
    return call(project_body(len(parts)), outs, 2.5, scratch, smem=1)(
        info, base, *parts, gain, *weight, cosine, sine, after=after
    )


def step_place(info, t):
    first, second = info[2], info[3]
    count = first // 4 + 1
    early = t < count
    block = jnp.where(early, 0, 1)
    chunk = jnp.where(early, t, t - count)
    place = jnp.where(early, first, second)
    return block, chunk, place


def causal(place, chunk):
    rows = lax.broadcasted_iota(jnp.int32, (BLK, CHUNK), 0) + place * BLK
    cols = lax.broadcasted_iota(jnp.int32, (BLK, CHUNK), 1) + chunk * CHUNK
    one = rows >= cols
    return jnp.concatenate([one] * GROUP, axis=0)


def head_tile(ref, block, head, upper):
    j = head // 2
    tile = ref[block * BLK : (block + 1) * BLK, j * 128 : (j + 1) * 128].astype(F32)
    if (head % 2 == 1) != upper:
        tile = pltpu.roll(tile, 64, 1)
    keep = (lane(tile.shape) >= HEAD) if upper else (lane(tile.shape) < HEAD)
    return jnp.where(keep, tile, 0.0)


def attend_body(count):
    def body(*refs):
        info, q_ref = refs[0], refs[1]
        pieces = refs[2 : 2 + count]
        (own, other, x_ref, gain, mixed_out, lse_out, kvs, resid_out, second_out) = refs[
            2 + count : 11 + count
        ]
        qh, top, total, acc, halves = refs[11 + count :]
        side = info[0]
        number = 0
        for piece in pieces:
            for b in range(piece.shape[0] // BLK):
                at = pl.multiple_of(info[4 + number] * BLK, BLK)
                kvs[pl.ds(at, BLK), :] = piece[b * BLK : (b + 1) * BLK, :]
                number += 1
        for i in range(2):
            for g in range(KV_HEADS):
                for r in range(GROUP):
                    qh[i, g, r * BLK : (r + 1) * BLK, :] = head_tile(
                        q_ref, i, g * GROUP + r, False
                    ).astype(BF)
        top[...] = jnp.full(top.shape, NEG, F32)
        total[...] = jnp.zeros(total.shape, F32)
        acc[...] = jnp.zeros(acc.shape, F32)

        def step(t, carry):
            block, chunk, place = step_place(info, t)
            allowed = causal(place, chunk)
            at = pl.multiple_of(chunk * CHUNK, CHUNK)
            for g in range(KV_HEADS):
                keys = kvs[pl.ds(at, CHUNK), g * 128 : (g + 1) * 128]
                scores = dot(qh[block, g], keys, NT)
                scores = jnp.where(allowed, scores, NEG)
                old = top[block, g]
                new = jnp.maximum(old, jnp.max(scores, axis=1, keepdims=True))
                probs = jnp.exp(scores - jnp.concatenate([new, new], axis=1))
                shrink = jnp.exp(old - new)
                top[block, g] = new
                total[block, g] = shrink * total[block, g] + jnp.sum(probs, axis=1, keepdims=True)
                acc[block, g] = shrink * acc[block, g] + dot(probs.astype(BF), keys)
            return carry

        lax.fori_loop(0, STEPS, step, 0)
        for i in range(2):
            heads = []
            for g in range(KV_HEADS):
                sums = total[i, g]
                result = acc[i, g] / sums
                lse_out[i, g] = top[i, g] + jnp.log(sums)
                for r in range(GROUP):
                    heads.append(result[r * BLK : (r + 1) * BLK, :])
            for j in range(8):
                low = pltpu.roll(heads[2 * j], 64, 1)
                rows = slice(i * BLK, (i + 1) * BLK)
                if j < 7:
                    tile = jnp.where(lane(low.shape) < HEAD, low, heads[2 * j + 1])
                    mixed_out[rows, j * 128 : (j + 1) * 128] = tile.astype(BF)
                else:
                    mixed_out[rows, 896:960] = low[:, :64].astype(BF)
        halves[side] = dot(mixed_out[...], own[:, HALF:])
        halves[1 - side] = dot(mixed_out[...], other[:, HALF:])
        resid = x_ref[...] + jnp.concatenate([halves[0], halves[1]], axis=1)
        resid_out[...] = resid
        second_out[...] = normalise(resid, gain[...]).astype(BF)

    return body


def attend(info, q, pieces, wo, x, gain, after=()):
    outs = [
        ((ROWS, D), BF),
        ((2, KV_HEADS, GROUP * BLK, 128), F32),
        ((SEQ, 2 * KW), BF),
        ((ROWS, D), F32),
        ((ROWS, D), BF),
    ]
    shape = (2, KV_HEADS, GROUP * BLK, 128)
    scratch = [pltpu.VMEM(shape, BF)] + [pltpu.VMEM(shape, F32)] * 3
    scratch.append(pltpu.VMEM((2, ROWS, D // 2), F32))
    return call(attend_body(len(pieces)), outs, 12.0, scratch, smem=1)(
        info, q, *pieces, *wo, x, gain, after=after
    )


def feed_body(layer, info, second, own, other, wd, gu_out, hidden_out, part_out):
    side = info[0]
    columns = slice(layer * FF // 4, (layer + 1) * FF // 4)
    gu_out[side] = dot(second[...], own[:, columns])
    gu_out[1 - side] = dot(second[...], other[:, columns])
    gate, up = gu_out[0], gu_out[1]
    hidden = (gate / (1.0 + jnp.exp(-gate)) * up).astype(BF)
    hidden_out[...] = hidden
    part_out[...] = dot(hidden, wd[...]).astype(BF)


def feed(layer, info, second, wgu, wd):
    outs = [((2, ROWS, FF // 4), F32), ((ROWS, FF // 4), BF), ((ROWS, D), BF)]
    body = partial(feed_body, layer)
    return call(body, outs, 1.0, smem=1)(info, second, *wgu, wd)


def feed_back_body(layer, info, grad_low, gu, own, other, wd, dgu_out, part_out):
    side = info[0]
    columns = slice(layer * FF // 4, (layer + 1) * FF // 4)
    d_hidden = dot(grad_low[...], wd[...], NT)
    gate, up = gu[0], gu[1]
    sig = 1.0 / (1.0 + jnp.exp(-gate))
    d_gate = d_hidden * up * sig * (1.0 + gate * (1.0 - sig))
    d_up = d_hidden * gate * sig
    dgu_out[0] = d_gate.astype(BF)
    dgu_out[1] = d_up.astype(BF)
    part = dot(dgu_out[side], own[:, columns], NT) + dot(dgu_out[1 - side], other[:, columns], NT)
    part_out[...] = part.astype(BF)


def feed_back(layer, info, grad_low, gu, wgu, wd):
    outs = [((2, ROWS, FF // 4), BF), ((ROWS, D), BF)]
    body = partial(feed_back_body, layer)
    return call(body, outs, 1.3, smem=1)(info, grad_low, gu, *wgu, wd)


def attend_back_body(
    info, p0, p1, p2, p3, grad, resid, gain, own, other, normed, mixed, q_ref, lse, kvs, cosine, sine,
    d_resid_out, d_low_out, dc_out, dq_out, ahead_out, o0, o1, o2, o3,
    qd, delta, dq, dkv, dm, mx, halves,
):
    d_second = p0[...].astype(F32) + p1[...].astype(F32) + p2[...].astype(F32) + p3[...].astype(F32)
    dx, dc = norm_back(resid[...], gain[...], d_second)
    dc_out[...] = dc
    d_resid = grad[...] + dx
    d_resid_out[...] = d_resid
    low = d_resid.astype(BF)
    d_low_out[...] = low
    side = info[0]
    halves[0] = d_resid[:, : D // 2].astype(BF)
    halves[1] = d_resid[:, D // 2 :].astype(BF)
    d_mixed = dot(halves[side], own[:, HALF:], NT) + dot(halves[1 - side], other[:, HALF:], NT)
    ahead_out[:, :D] = normed[...]
    ahead_out[:, QP : QP + D] = mixed[...]
    ahead_out[:, D:QP] = jnp.zeros((ROWS, QP - D), BF)
    dm[:, :D] = d_mixed.astype(BF)
    dm[:, D:] = jnp.zeros((ROWS, QP - D), BF)
    mx[:, :D] = mixed[...]
    mx[:, D:] = jnp.zeros((ROWS, QP - D), BF)
    span = GROUP * BLK
    for i in range(2):
        for g in range(KV_HEADS):
            for r in range(GROUP):
                head = g * GROUP + r
                there = slice(r * BLK, (r + 1) * BLK)
                qd[i, g, there, :] = head_tile(q_ref, i, head, False).astype(BF)
                do = head_tile(dm, i, head, True)
                qd[i, g, span + r * BLK : span + (r + 1) * BLK, :] = do.astype(BF)
                dots = jnp.sum(do * head_tile(mx, i, head, True), axis=1, keepdims=True)
                delta[i, g, there, :] = jnp.broadcast_to(dots, (BLK, 128))
    dq[...] = jnp.zeros(dq.shape, F32)
    dkv[...] = jnp.zeros(dkv.shape, F32)

    def step(t, carry):
        block, chunk, place = step_place(info, t)
        allowed = causal(place, chunk)
        at = pl.multiple_of(chunk * CHUNK, CHUNK)
        for g in range(KV_HEADS):
            keys = kvs[pl.ds(at, CHUNK), g * 128 : (g + 1) * 128]
            both = dot(qd[block, g], keys, NT)
            scores, d_probs = both[:span], both[span:]
            total = lse[block, g]
            probs = jnp.exp(
                jnp.where(allowed, scores, NEG) - jnp.concatenate([total, total], axis=1)
            )
            shift = delta[block, g]
            d_scores = probs * (d_probs - jnp.concatenate([shift, shift], axis=1))
            d_low = d_scores.astype(BF)
            dq[block, g] += dot(d_low, keys)
            stacked = jnp.concatenate([d_low, probs.astype(BF)], axis=0)
            dkv[pl.ds(at, CHUNK), g * 128 : (g + 1) * 128] += dot(stacked, qd[block, g], TN)
        return carry

    lax.fori_loop(0, STEPS, step, 0)
    for i in range(2):
        rows = slice(i * BLK, (i + 1) * BLK)
        cos, sin = cosine[rows, :], sine[rows, :]
        heads = []
        for g in range(KV_HEADS):
            for r in range(GROUP):
                heads.append(dq[i, g, r * BLK : (r + 1) * BLK, :] * (HEAD**-0.5))
        for j in range(8):
            if j < 7:
                high = pltpu.roll(heads[2 * j + 1], 64, 1)
                tile = jnp.where(lane(high.shape) < HEAD, heads[2 * j], high)
                dq_out[rows, j * 128 : (j + 1) * 128] = spin(tile, cos, -sin).astype(BF)
            else:
                dq_out[rows, 896:960] = spin(heads[14], cos, -sin)[:, :64].astype(BF)
    number = 0
    for out in (o0, o1, o2, o3):
        for b in range(out.shape[0] // BLK):
            at = pl.multiple_of(info[36 + number] * BLK, BLK)
            out[b * BLK : (b + 1) * BLK, :] = dkv[pl.ds(at, BLK), :].astype(BF)
            number += 1


def attend_back(info, parts, grad, resid, gain, wo, normed, mixed, q, lse, kvs, cosine, sine, after=()):
    outs = [
        ((ROWS, D), F32),
        ((ROWS, D), BF),
        ((1, D), F32),
        ((ROWS, D), BF),
        ((ROWS, QP + D), BF),
    ] + [((4 * ROWS, 2 * KW), BF)] * 4
    shape = (2, KV_HEADS, GROUP * BLK, 128)
    scratch = [
        pltpu.VMEM((2, KV_HEADS, 2 * GROUP * BLK, 128), BF),
        pltpu.VMEM(shape, F32),
        pltpu.VMEM(shape, F32),
        pltpu.VMEM((SEQ, 2 * KW), F32),
        pltpu.VMEM((ROWS, QP), BF),
        pltpu.VMEM((ROWS, QP), BF),
        pltpu.VMEM((2, ROWS, D // 2), BF),
    ]
    return call(attend_back_body, outs, 24.0, scratch, smem=1)(
        info, *parts, grad, resid, gain, *wo, normed, mixed, q, lse, kvs, cosine, sine, after=after
    )


def project_back_body(
    info, k0, k1, k2, k3, dq, d_resid, d_low, x_ref, gain, own, other, cosine, sine,
    cut_out, grad_out, dc_out, halves, dkv,
):
    side, z = info[0], info[1]
    sums = k0[...].astype(F32) + k1[...].astype(F32) + k2[...].astype(F32) + k3[...].astype(F32)
    cos, sin = cosine[...], -sine[...]
    halves[0] = dq[:, :HALF]
    halves[1] = jnp.zeros((ROWS, HALF), BF)
    halves[1, :, :HEAD] = dq[:, HALF:]
    for g in range(KV_HEADS):
        tile = sums[:, g * 128 : (g + 1) * 128]
        tile = jnp.where(lane(tile.shape) < HEAD, spin(tile, cos, sin), tile)
        dkv[:, g * 128 : (g + 1) * 128] = tile
        halves[1, :, (g + 1) * 128 : (g + 2) * 128] = tile.astype(BF)
    d_normed = dot(halves[side], own[:, :HALF], NT) + dot(halves[1 - side], other[:, :HALF], NT)
    dx, dc = norm_back(x_ref[...], gain[...], d_normed)
    dc_out[...] = dc
    grad_out[...] = d_resid[...] + dx
    query, low = dq[...].astype(F32), d_low[...].astype(F32)
    quarters = (
        query[:, :640],
        jnp.concatenate([query[:, 640:], dkv[:, :320]], axis=1),
        jnp.concatenate([dkv[:, 320:], low[:, :320]], axis=1),
        low[:, 320:],
    )
    for place in range(4):
        cut_out[(place + 4 - z) % 4] = quarters[place].astype(BF)


def project_back(info, pieces, dq, d_resid, d_low, x, gain, weight, cosine, sine, after=()):
    outs = [((4, ROWS, 640), BF), ((ROWS, D), F32), ((1, D), F32)]
    scratch = [pltpu.VMEM((2, ROWS, HALF), BF), pltpu.VMEM((ROWS, 2 * KW), F32)]
    return call(project_back_body, outs, 3.2, scratch, smem=1)(
        info, *pieces, dq, d_resid, d_low, x, gain, *weight, cosine, sine, after=after
    )


def slot_of(info, c, given):
    place = info[68 + c]
    return (place % 4) * 4 + place // 4 if given else place


def feed_grads_body(*refs):
    info = refs[0]
    seconds, dgus, hiddens, lows = (refs[1 + 4 * i : 5 + 4 * i] for i in range(4))
    keep_out, give_out, left, right, hidden, low, acc, down, group = refs[17:]
    side = info[0]
    for k in range(4):
        rows = slice(k * ROWS, (k + 1) * ROWS)
        left[rows, :] = seconds[k][...]
        hidden[rows, :] = hiddens[k][...]
        low[rows, :] = lows[k][...]
        for h in range(2):
            right[h, rows, :] = dgus[k][h]
    down[...] = dot(hidden[...], low[...], TN)
    group[90:, :] = jnp.zeros((6, 640), F32)
    for turn, out in ((0, keep_out), (1, give_out)):
        half = side if turn == 0 else 1 - side
        acc[...] = dot(left[...], right[half], TN)
        for h in range(2):

            @pl.when(half == h)
            def _():
                for c in range(16):
                    at = 40 * c + 20 * h
                    group[:60, :] = acc[60 * c : 60 * c + 60, :]
                    group[60:80, :] = down[at : at + 20, :640]
                    group[80:90, :320] = down[at : at + 10, 640:]
                    group[80:90, 320:] = down[at + 10 : at + 20, 640:]
                    out[slot_of(info, c, turn)] = group[...].astype(BF)


def feed_grads(info, seconds, dgus, hiddens, lows, after=()):
    rows = 4 * ROWS
    scratch = [
        pltpu.VMEM((rows, D), BF),
        pltpu.VMEM((2, rows, 640), BF),
        pltpu.VMEM((rows, 640), BF),
        pltpu.VMEM((rows, D), BF),
        pltpu.VMEM((D, 640), F32),
        pltpu.VMEM((640, D), F32),
        pltpu.VMEM((96, 640), F32),
    ]
    return call(feed_grads_body, [((16, 96, 640), BF)] * 2, 6.5, scratch, smem=1)(
        info, *seconds, *dgus, *hiddens, *lows, after=after
    )


def attend_grads_body(*refs):
    info = refs[0]
    mines, aheads = refs[1:5], refs[5:9]
    dc_one, dc_two, keep_out, give_out, lhs, mine, acc, group = refs[9:]
    side, z = info[0], info[1]
    for k in range(4):
        rows = slice(k * ROWS, (k + 1) * ROWS)
        for h in range(2):
            mine[h, rows, :] = mines[k][:, h * 320 : (h + 1) * 320].astype(F32).astype(BF)
        lhs[0, rows, :] = aheads[k][:, :D]
        lhs[1, rows, :] = aheads[k][:, QP:]
    group[60:, :] = jnp.zeros((4, 384), F32)
    for turn, out in ((0, keep_out), (1, give_out)):
        h = side if turn == 0 else 1 - side
        which = jnp.where(z + h >= 3, 1, 0)
        acc[:, :320] = dot(lhs[which], mine[h], TN)
        gain_row = jnp.where(h == 0, dc_one[...], dc_two[...])
        first = lax.broadcasted_iota(jnp.int32, (8, D), 0) == 0
        spread = jnp.where(first, jnp.broadcast_to(gain_row, (8, D)), 0.0)
        acc[:, 320:] = dot(spread, jnp.ones((8, 64), F32), TN)
        for c in range(16):
            group[:60, :] = acc[60 * c : 60 * c + 60, :]
            out[slot_of(info, c, turn)] = group[...].astype(BF)


def attend_grads(info, mines, aheads, dc_one, dc_two):
    rows = 4 * ROWS
    scratch = [
        pltpu.VMEM((2, rows, D), BF),
        pltpu.VMEM((2, rows, 320), BF),
        pltpu.VMEM((D, 384), F32),
        pltpu.VMEM((64, 384), F32),
    ]
    return call(attend_grads_body, [((16, 64, 384), BF)] * 2, 3.0, scratch, smem=1)(
        info, *mines, *aheads, dc_one, dc_two
    )


def finish_body(info, p0, p1, p2, p3, *outs):
    n1, gq, gk, gv, go, n2, gate, up = outs[:8]
    placed = outs[8]
    z = info[1]
    for k, piece in enumerate((p0, p1, p2, p3)):
        placed[(z + 4 - k) % 4] = piece[...]
    att = []
    for place in range(4):
        gate[:, 0, place * 640 : (place + 1) * 640] = placed[place, :, :640]
        up[:, 0, place * 640 : (place + 1) * 640] = placed[place, :, 1024:1664]
        att += [placed[place, :, 640:960], placed[place, :, 1664:1984]]
    gq[:, 0, :] = jnp.concatenate(att[:3], axis=1)
    go[:, 0, :] = jnp.concatenate(att[5:], axis=1)
    both = jnp.concatenate(att[3:5], axis=1)
    gk[:, 0, :] = jnp.concatenate([both[:, g * 128 : g * 128 + 64] for g in range(KV_HEADS)], axis=1)
    gv[:, 0, :] = jnp.concatenate([both[:, g * 128 + 64 : g * 128 + 128] for g in range(KV_HEADS)], axis=1)
    total = placed[0] + placed[1] + placed[2] + placed[3]
    n1[...] = total[:, 960:1024]
    n2[...] = total[:, 1984:2048]


def finish(info, pieces):
    widths = [D, KW, KW, D, FF, FF]
    shapes = [(15, 1, width) for width in widths]
    shapes = [(15, 64)] + shapes[:4] + [(15, 64)] + shapes[4:]
    return call(
        finish_body, [(s, F32) for s in shapes], 1.5, [pltpu.VMEM((4, 15, 2048), F32)], smem=1
    )(info, *pieces)


def z_shift(value, steps):
    return lax.ppermute(value, "wsh", [(i, (i + steps) % 4) for i in range(4)])


def ctx_shift(value, steps, core_along_x):
    pairs = []
    for core in range(2):
        for y in range(4):
            for x in range(4):
                to = (y, (x + steps) % 4) if core == core_along_x else ((y + steps) % 4, x)
                pairs.append((core * 16 + y * 4 + x, core * 16 + to[0] * 4 + to[1]))
    return lax.ppermute(value, ("section", "ctx"), pairs)


def gather_shift(value, steps):
    return ctx_shift(value, steps, 0)


def reduce_shift(value, steps):
    return ctx_shift(value, steps, 1)


def swap(value):
    return lax.ppermute(value, "section", [(0, 1), (1, 0)])


def add(first, *others):
    total = first.astype(F32)
    for other in others:
        total = total + other.astype(F32)
    return total


def in_order(pieces, rank):
    stacked = jnp.stack(pieces)
    return [lax.dynamic_index_in_dim(stacked, (rank - z) % 4, 0, False) for z in range(4)]


def shards(
    tokens, cotangent, block_order, norm_one, w_query, w_key, w_value, w_out, norm_two, w_gate, w_up, w_down
):
    section = lax.axis_index("section")
    rank = lax.axis_index("ctx")
    z_rank = lax.axis_index("wsh")
    first_core = section == 0
    quarter = FF // 4

    def both(value):
        other = swap(value)
        return jnp.where(first_core, value, other), jnp.where(first_core, other, value)

    key_value = jnp.concatenate(
        [w_key[0].reshape(-1, KV_HEADS, HEAD), w_value[0].reshape(-1, KV_HEADS, HEAD)], axis=2
    ).reshape(-1, 2 * KW)
    shard_rows = w_query.shape[1]
    low_half = jnp.concatenate([w_query[0][:, :HALF], w_out[0][:, : D // 2]], axis=1)
    high_half = jnp.concatenate(
        [
            w_query[0][:, HALF:],
            jnp.zeros((shard_rows, HEAD), BF),
            key_value,
            jnp.zeros((shard_rows, 128), BF),
            w_out[0][:, D // 2 :],
        ],
        axis=1,
    )
    got = swap(jnp.where(first_core, high_half, low_half))
    layer_half = (jnp.where(first_core, low_half, got), jnp.where(first_core, got, high_half))

    def whole(part):
        full = lax.all_gather(part, "wsh", axis=0, tiled=True)
        return full, swap(full)

    gathered = tuple(whole(part) for part in layer_half)

    gains = jnp.stack([norm_one[0], norm_two[0]])
    gain_parts = [gains] + [z_shift(gains, k) for k in (1, 2, 3)]
    gains = jnp.concatenate(in_order(gain_parts, z_rank), axis=1)
    gain_pair = [g.astype(F32) for g in both(gains)]

    given = swap(jnp.where(first_core, w_up[0], w_gate[0]))
    kind = (jnp.where(first_core, w_gate[0], given), jnp.where(first_core, given, w_up[0]))

    wd = both(w_down[0])

    def none_of(mark):
        return (mark != mark).astype(jnp.int32)

    def send_feed_weights(mark):
        later = none_of(mark)

        def columns(z):
            start = z * quarter + later
            return jnp.concatenate(
                [lax.dynamic_slice_in_dim(k, start, quarter, 1) for k in kind], axis=1
            )

        return [columns(z_rank)] + [z_shift(columns((z_rank + k) % 4), k) for k in (1, 2, 3)]

    def join_feed_weights(parts, mark):
        later = none_of(mark)
        ordered = jnp.zeros((D, 2 * quarter), BF)
        for k, part in enumerate(parts):
            start = ((z_rank - k) % 4) * shard_rows + later
            ordered = lax.dynamic_update_slice_in_dim(ordered, part, start, 0)
        return ordered, swap(ordered)

    own = lax.dynamic_slice_in_dim(block_order, 2 * rank, 2, 0)
    pairs = block_order.reshape(4, 4, 2)
    y, x = rank // 4, rank % 4
    step = jnp.arange(4, dtype=jnp.int32)

    def by_core(table):
        return jnp.where(first_core, table, jnp.swapaxes(table, 0, 1))

    came = by_core(pairs[(y - step) % 4][:, (x - step) % 4]).reshape(32)
    goes = by_core(pairs[(y + step) % 4][:, (x + step) % 4]).reshape(32)
    ahead_y = ((step - y) % 4)[:, None]
    ahead_x = ((step - x) % 4)[None, :]
    slot = jnp.where(first_core, ahead_y * 4 + ahead_x, ahead_x * 4 + ahead_y).reshape(16)
    info = jnp.concatenate([jnp.stack([section, z_rank]), own, came, goes, slot]).astype(jnp.int32)
    offsets = jnp.arange(BLK, dtype=jnp.int32)
    local_pos = (own[:, None] * BLK + offsets[None, :]).reshape(ROWS)
    frequency = jnp.exp(
        jnp.arange(HEAD // 2).astype(F32) * (-2.0 * math.log(ROPE_BASE) / HEAD)
    )
    angle = local_pos.astype(F32)[:, None] * frequency[None, :]
    cos32, sin32 = jnp.cos(angle), jnp.sin(angle)
    cosine = jnp.concatenate([cos32] * 4, axis=1)
    sine = jnp.concatenate([-sin32, sin32, -sin32, sin32], axis=1)

    own_tokens = lax.dynamic_index_in_dim(tokens, section, 0, False)[0]
    own_cotangent = lax.dynamic_index_in_dim(cotangent, section, 0, False)[0]

    def z_gather(value):
        return [value] + [z_shift(value, k) for k in (1, 2, 3)]

    last_lows = z_gather(own_cotangent.astype(BF))
    saved = []
    base, parts = own_tokens, []
    for layer in range(2):
        gain_one = gain_pair[layer][0:1]
        gain_two = gain_pair[layer][1:2]
        x_in, normed, q, kv = project(
            info, base, parts, gain_one, gathered[layer], cosine, sine, after=() if layer else wd
        )
        row = jnp.concatenate([kv] + [gather_shift(kv, k) for k in (1, 2, 3)], axis=0)
        pieces = [row] + [reduce_shift(row, k) for k in (1, 2, 3)]
        if layer == 0:
            sent = send_feed_weights(pieces[1][0, 0] + pieces[2][0, 0] + pieces[3][0, 0])
        mixed, lse, kvs, resid, second = attend(
            info, q, pieces, gathered[layer], x_in, gain_two, after=last_lows[1:] if layer else ()
        )
        if layer == 0:
            wgu = join_feed_weights(sent, second[0, 0])
        seconds = z_gather(second)
        fed = [feed(layer, info, s, wgu, wd[layer]) for s in seconds]
        parts = [fed[0][2]] + [z_shift(fed[k][2], -k) for k in (1, 2, 3)]
        base = resid
        saved.append(
            dict(
                x=x_in, q=q, mixed=mixed, lse=lse, kvs=kvs, resid=resid,
                normed=normed,
                seconds=seconds, gu=[f[0] for f in fed], hidden=[f[1] for f in fed],
            )
        )
    outputs = [saved[1]["x"], add(base, *parts)]

    grad = own_cotangent
    lows = last_lows
    input_grads = [None, None]
    feed_sums = [None, None]
    kept = [None, None]
    order = ()

    def stage_one(half, later=0):
        cut = [lax.dynamic_slice_in_dim(half, 4 * k + later, 4, 0) for k in range(4)]
        return add(cut[0], *[reduce_shift(cut[k], k) for k in (1, 2, 3)])

    def stage_two(stage):
        low = stage.astype(BF)
        return add(stage[0], *[gather_shift(low[k], k) for k in (1, 2, 3)])

    for layer in (1, 0):
        s = saved[layer]
        gain_one = gain_pair[layer][0:1]
        gain_two = gain_pair[layer][1:2]
        back = [feed_back(layer, info, lows[k], s["gu"][k], wgu, wd[layer]) for k in range(4)]
        parts = [back[0][1]] + [z_shift(back[k][1], -k) for k in (1, 2, 3)]
        keep, give = feed_grads(info, s["seconds"], [b[0] for b in back], s["hidden"], lows)
        d_resid, d_low, dc_two, dq, ahead, *goes_out = attend_back(
            info, parts, grad, s["resid"], gain_two, gathered[layer], s["normed"], s["mixed"], s["q"],
            s["lse"], s["kvs"], cosine, sine, after=(keep, *order),
        )
        feed_half = add(keep, swap(give)).astype(BF)
        row = add(goes_out[0], *[reduce_shift(goes_out[k], k) for k in (1, 2, 3)])
        row = row.astype(BF).reshape(4, ROWS, 2 * KW)
        own_pieces = [row[0]] + [gather_shift(row[k], k) for k in (1, 2, 3)]
        aheads = z_gather(ahead)
        if layer == 0:
            kept[1] = attention_grads(none_of(d_low[0, 0]))
        cut, grad, dc_one = project_back(
            info, own_pieces, dq, d_resid, d_low, s["x"], gain_one, gathered[layer], cosine, sine,
            after=tuple(aheads[1:]) if layer else (),
        )
        input_grads[layer] = grad
        feed_stage = stage_one(feed_half, none_of(cut[0, 0, 0]))
        if layer:
            lows = z_gather(grad.astype(BF))
            order = (feed_stage,)
            feed_sums[1] = stage_two(feed_stage)

        def attention_grads(later, cut=cut, aheads=aheads, dc_one=dc_one, dc_two=dc_two):
            mines = [lax.dynamic_index_in_dim(cut, k + later, 0, False) for k in range(4)]
            mines = [mines[0]] + [z_shift(mines[k], k) for k in (1, 2, 3)]
            keep, give = attend_grads(info, mines, aheads, dc_one, dc_two)
            return add(keep, swap(give)).astype(BF)

        if layer == 0:
            kept[0] = attention_grads(0)
    attend_stage = stage_one(jnp.concatenate(kept, axis=2))
    both_sums = stage_two(
        jnp.concatenate([feed_stage, jnp.pad(attend_stage, ((0, 0), (0, 32), (0, 0)))], axis=2)
    )
    feed_sums[0], attend_sum = both_sums[:, :640], both_sums[:64, 640:]
    sums = [
        jnp.concatenate(
            [feed_sums[layer], jnp.pad(attend_sum[:, layer * 384 : (layer + 1) * 384], ((0, 32), (0, 0)))],
            axis=1,
        )
        for layer in range(2)
    ]

    mine = jnp.where(first_core, sums[0], sums[1])
    other = swap(jnp.where(first_core, sums[1], sums[0]))
    halves = (jnp.where(first_core, mine, other), jnp.where(first_core, other, mine))
    joined = jnp.concatenate([h[:60] for h in halves], axis=1).reshape(4, 15, 2048)
    pieces = [lax.dynamic_index_in_dim(joined, z_rank, 0, False)] + [
        z_shift(lax.dynamic_index_in_dim(joined, (z_rank + k) % 4, 0, False), k) for k in (1, 2, 3)
    ]
    down = jnp.concatenate(
        [
            jnp.concatenate(
                [h[60:80, :640], jnp.concatenate([h[80:90, :320], h[80:90, 320:640]], axis=0)], axis=1
            )
            for h in halves
        ],
        axis=0,
    )
    moves = [(c * 4 + z, (4 * z + c // 4) * 4 + c % 4) for c in range(16) for z in range(4)]
    grad_down = lax.ppermute(down, ("ctx", "wsh"), moves)[None]
    sum_one, gq, gk, gv, go, sum_two, gate, up = finish(info, pieces)
    grad_query, grad_key, grad_value, grad_out, grad_gate, grad_up = (
        jnp.swapaxes(g, 0, 1) for g in (gq, gk, gv, go, gate, up)
    )

    def arranged(pair):
        mine = jnp.where(first_core, pair[0], pair[1])
        other = swap(jnp.where(first_core, pair[1], pair[0]))
        first = jnp.where(first_core, mine, other)
        last = jnp.where(first_core, other, mine)
        return jnp.stack([first, last])[None, :, None]

    return (
        arranged(outputs),
        arranged(input_grads),
        sum_one[:, 0][None],
        grad_query,
        grad_key,
        grad_value,
        grad_out,
        sum_two[:, 0][None],
        grad_gate,
        grad_up,
        grad_down,
    )


def solution(mesh):
    rows = P(None, "wsh", "ctx", None)
    gain = P("section", "wsh")
    weight = P("section", "wsh", None)
    in_specs = (rows, rows, P(), gain, weight, weight, weight, weight, gain, weight, weight, weight)
    result = P("section", None, "wsh", "ctx", None)
    gain_out = P("section", ("ctx", "wsh"))
    weight_out = P("section", ("ctx", "wsh"), None)
    out_specs = (
        result, result, gain_out, weight_out, weight_out, weight_out, weight_out, gain_out,
        weight_out, weight_out, weight_out,
    )
    return jax.shard_map(shards, mesh=mesh, in_specs=in_specs, out_specs=out_specs, check_vma=False)
```

```python
import math
from functools import partial

import jax
import jax.numpy as jnp
from jax import lax
from jax.experimental import pallas as pl
from jax.experimental.pallas import tpu as pltpu
from jax.sharding import PartitionSpec as P

HEADS = 15
KV_HEADS = 5
HEAD = 64
GROUP = HEADS // KV_HEADS
D = 960
FF = 2560
KW = KV_HEADS * HEAD
ROWS = 128
BLK = 64
SEQ = 2048
CHUNK = 256
STEPS = 9
EPS = 1e-05
ROPE_BASE = 10000.0
BF = jnp.bfloat16
F32 = jnp.float32
QP = 1024
HALF = 896
NEG = -1e30
MIB = 1024 * 1024

NN = (((1,), (0,)), ((), ()))
NT = (((1,), (1,)), ((), ()))
TN = (((0,), (0,)), ((), ()))


def dot(left, right, dims=NN):
    return lax.dot_general(left, right, dims, preferred_element_type=F32)


def call(body, outs, micros, mib, scratch=(), smem=0):
    def run(*args, after=()):
        count = len(args)
        in_specs = [
            pl.BlockSpec(memory_space=pltpu.SMEM if i < smem else pltpu.VMEM) for i in range(count)
        ] + [pl.BlockSpec(memory_space=pl.ANY) for _ in after]

        def inner(*refs):
            body(*refs[:count], *refs[count + len(after) :])

        out = pl.pallas_call(
            inner,
            in_specs=in_specs,
            out_specs=[pl.BlockSpec(memory_space=pltpu.VMEM) for _ in outs],
            out_shape=[jax.ShapeDtypeStruct(s, t) for s, t in outs],
            scratch_shapes=list(scratch),
            cost_estimate=pl.CostEstimate(
                flops=int(micros * 1.1e9), bytes_accessed=int(micros * 3.6e6), transcendentals=0
            ),
            compiler_params=pltpu.CompilerParams(vmem_limit_bytes=mib * MIB),
        )(*args, *after)
        return out

    return run


def lane(shape):
    return lax.broadcasted_iota(jnp.int32, shape, 1)


def normalise(x, gain):
    return x * lax.rsqrt(jnp.mean(x * x, axis=-1, keepdims=True) + EPS) * gain


def norm_back(x, gain, dy):
    r = lax.rsqrt(jnp.mean(x * x, axis=-1, keepdims=True) + EPS)
    cdy = gain * dy
    dx = r * cdy - x * (r * r * r) * jnp.mean(x * cdy, axis=-1, keepdims=True)
    dc = jnp.sum(dy * x * r, axis=0, keepdims=True)
    return dx, dc


def spin(tile, cosine, sine):
    first = (lane(tile.shape) % HEAD) < HEAD // 2
    swapped = jnp.where(first, pltpu.roll(tile, 96, 1), pltpu.roll(tile, 32, 1))
    return tile * cosine + swapped * sine


def project_body(count):
    def body(*refs):
        info, base = refs[:2]
        parts = refs[2 : 2 + count]
        gain, own, other, cosine, sine = refs[2 + count : 7 + count]
        if count:
            normed_in, mixed_in = refs[7 + count : 9 + count]
            x_out, normed_out, q_out, kv_out, ahead_out, halves = refs[9 + count :]
            ahead_out[:, :D] = normed_in[...]
            ahead_out[:, D:QP] = jnp.zeros((ROWS, QP - D), BF)
            ahead_out[:, QP:] = mixed_in[...]
        else:
            x_out, normed_out, q_out, kv_out, halves = refs[7:]
        side = info[0]
        x = base[...]
        for part in parts:
            x = x + part[...].astype(F32)
        x_out[...] = x
        normed = normalise(x, gain[...]).astype(BF)
        normed_out[...] = normed
        cos, sin = cosine[...], sine[...]
        halves[side] = dot(normed, own[:, :HALF])
        halves[1 - side] = dot(normed, other[:, :HALF])
        for j in range(8):
            tile = halves[0, :, j * 128 : (j + 1) * 128] if j < 7 else halves[1, :, 0:128]
            q_out[:, j * 128 : (j + 1) * 128] = (spin(tile, cos, sin) * (HEAD**-0.5)).astype(BF)
        for g in range(KV_HEADS):
            tile = halves[1, :, (g + 1) * 128 : (g + 2) * 128]
            tile = jnp.where(lane(tile.shape) < HEAD, spin(tile, cos, sin), tile)
            kv_out[:, g * 128 : (g + 1) * 128] = tile.astype(BF)

    return body


def project(info, base, parts, gain, weight, cosine, sine, ahead=()):
    outs = [((ROWS, D), F32), ((ROWS, D), BF), ((ROWS, QP), BF), ((ROWS, 2 * KW), BF)]
    if ahead:
        outs.append(((ROWS, QP + D), BF))
    scratch = [pltpu.VMEM((2, ROWS, HALF), F32)]
    return call(project_body(len(parts)), outs, 2.5, 16, scratch, smem=1)(
        info, base, *parts, gain, *weight, cosine, sine, *ahead
    )


def step_place(info, t):
    first, second = info[2], info[3]
    count = first // 4 + 1
    early = t < count
    block = jnp.where(early, 0, 1)
    chunk = jnp.where(early, t, t - count)
    place = jnp.where(early, first, second)
    return block, chunk, place


def causal(place, chunk):
    rows = lax.broadcasted_iota(jnp.int32, (BLK, CHUNK), 0) + place * BLK
    cols = lax.broadcasted_iota(jnp.int32, (BLK, CHUNK), 1) + chunk * CHUNK
    one = rows >= cols
    return jnp.concatenate([one] * GROUP, axis=0)


def head_tile(ref, block, head, upper):
    j = head // 2
    tile = ref[block * BLK : (block + 1) * BLK, j * 128 : (j + 1) * 128].astype(F32)
    if (head % 2 == 1) != upper:
        tile = pltpu.roll(tile, 64, 1)
    keep = (lane(tile.shape) >= HEAD) if upper else (lane(tile.shape) < HEAD)
    return jnp.where(keep, tile, 0.0)


def attend_body(count):
    def body(*refs):
        info, q_ref = refs[0], refs[1]
        pieces = refs[2 : 2 + count]
        (own, other, x_ref, gain, mixed_out, lse_out, kvs, resid_out, second_out) = refs[
            2 + count : 11 + count
        ]
        qh, top, total, acc, halves = refs[11 + count :]
        side = info[0]
        number = 0
        for piece in pieces:
            for b in range(piece.shape[0] // BLK):
                at = pl.multiple_of(info[4 + number] * BLK, BLK)
                kvs[pl.ds(at, BLK), :] = piece[b * BLK : (b + 1) * BLK, :]
                number += 1
        for i in range(2):
            for g in range(KV_HEADS):
                for r in range(GROUP):
                    qh[i, g, r * BLK : (r + 1) * BLK, :] = head_tile(
                        q_ref, i, g * GROUP + r, False
                    ).astype(BF)
        top[...] = jnp.full(top.shape, NEG, F32)
        total[...] = jnp.zeros(total.shape, F32)
        acc[...] = jnp.zeros(acc.shape, F32)

        def step(t, carry):
            block, chunk, place = step_place(info, t)
            allowed = causal(place, chunk)
            at = pl.multiple_of(chunk * CHUNK, CHUNK)
            for g in range(KV_HEADS):
                keys = kvs[pl.ds(at, CHUNK), g * 128 : (g + 1) * 128]
                scores = dot(qh[block, g], keys, NT)
                scores = jnp.where(allowed, scores, NEG)
                old = top[block, g]
                new = jnp.maximum(old, jnp.max(scores, axis=1, keepdims=True))
                probs = jnp.exp(scores - jnp.concatenate([new, new], axis=1))
                shrink = jnp.exp(old - new)
                top[block, g] = new
                total[block, g] = shrink * total[block, g] + jnp.sum(probs, axis=1, keepdims=True)
                acc[block, g] = shrink * acc[block, g] + dot(probs.astype(BF), keys)
            return carry

        lax.fori_loop(0, STEPS, step, 0)
        for i in range(2):
            heads = []
            for g in range(KV_HEADS):
                sums = total[i, g]
                result = acc[i, g] / sums
                lse_out[i, g] = top[i, g] + jnp.log(sums)
                for r in range(GROUP):
                    heads.append(result[r * BLK : (r + 1) * BLK, :])
            for j in range(8):
                low = pltpu.roll(heads[2 * j], 64, 1)
                rows = slice(i * BLK, (i + 1) * BLK)
                if j < 7:
                    tile = jnp.where(lane(low.shape) < HEAD, low, heads[2 * j + 1])
                    mixed_out[rows, j * 128 : (j + 1) * 128] = tile.astype(BF)
                else:
                    mixed_out[rows, 896:960] = low[:, :64].astype(BF)
        halves[side] = dot(mixed_out[...], own[:, HALF:])
        halves[1 - side] = dot(mixed_out[...], other[:, HALF:])
        resid = x_ref[...] + jnp.concatenate([halves[0], halves[1]], axis=1)
        resid_out[...] = resid
        second_out[...] = normalise(resid, gain[...]).astype(BF)

    return body


def attend(info, q, pieces, wo, x, gain, after=()):
    outs = [
        ((ROWS, D), BF),
        ((2, KV_HEADS, GROUP * BLK, 128), F32),
        ((SEQ, 2 * KW), BF),
        ((ROWS, D), F32),
        ((ROWS, D), BF),
    ]
    shape = (2, KV_HEADS, GROUP * BLK, 128)
    scratch = [pltpu.VMEM(shape, BF)] + [pltpu.VMEM(shape, F32)] * 3
    scratch.append(pltpu.VMEM((2, ROWS, D // 2), F32))
    return call(attend_body(len(pieces)), outs, 12.0, 24, scratch, smem=1)(
        info, q, *pieces, *wo, x, gain, after=after
    )


def feed_body(layer, info, second, own, other, wd, gu_out, hidden_out, part_out):
    side = info[0]
    columns = slice(layer * FF // 4, (layer + 1) * FF // 4)
    gu_out[side] = dot(second[...], own[...])
    gu_out[1 - side] = dot(second[...], other[:, columns])
    gate, up = gu_out[0], gu_out[1]
    hidden = (gate / (1.0 + jnp.exp(-gate)) * up).astype(BF)
    hidden_out[...] = hidden
    part_out[...] = dot(hidden, wd[...]).astype(BF)


def feed(layer, info, second, wgu, wd, after=()):
    outs = [((2, ROWS, FF // 4), F32), ((ROWS, FF // 4), BF), ((ROWS, D), BF)]
    body = partial(feed_body, layer)
    return call(body, outs, 1.0, 12, smem=1)(info, second, *wgu, wd, after=after)


def feed_back_body(layer, info, grad_low, gu, own, other, wd, dgu_out, part_out):
    side = info[0]
    columns = slice(layer * FF // 4, (layer + 1) * FF // 4)
    d_hidden = dot(grad_low[...], wd[...], NT)
    gate, up = gu[0], gu[1]
    sig = 1.0 / (1.0 + jnp.exp(-gate))
    d_gate = d_hidden * up * sig * (1.0 + gate * (1.0 - sig))
    d_up = d_hidden * gate * sig
    dgu_out[0] = d_gate.astype(BF)
    dgu_out[1] = d_up.astype(BF)
    part = dot(dgu_out[side], own[...], NT) + dot(dgu_out[1 - side], other[:, columns], NT)
    part_out[...] = part.astype(BF)


def feed_back(layer, info, grad_low, gu, wgu, wd):
    outs = [((2, ROWS, FF // 4), BF), ((ROWS, D), BF)]
    body = partial(feed_back_body, layer)
    return call(body, outs, 1.3, 12, smem=1)(info, grad_low, gu, *wgu, wd)


def attend_back_body(
    info, p0, p1, p2, p3, grad, resid, gain, own, other, normed, mixed, q_ref, lse, kvs, cosine, sine,
    d_resid_out, d_low_out, dc_out, dq_out, ahead_out, o0, o1, o2, o3,
    qd, delta, dq, dkv, dm, mx, halves,
):
    d_second = p0[...].astype(F32) + p1[...].astype(F32) + p2[...].astype(F32) + p3[...].astype(F32)
    dx, dc = norm_back(resid[...], gain[...], d_second)
    dc_out[...] = dc
    d_resid = grad[...] + dx
    d_resid_out[...] = d_resid
    low = d_resid.astype(BF)
    d_low_out[...] = low
    side = info[0]
    halves[0] = d_resid[:, : D // 2].astype(BF)
    halves[1] = d_resid[:, D // 2 :].astype(BF)
    d_mixed = dot(halves[side], own[:, HALF:], NT) + dot(halves[1 - side], other[:, HALF:], NT)
    ahead_out[:, :D] = normed[...]
    ahead_out[:, QP : QP + D] = mixed[...]
    ahead_out[:, D:QP] = jnp.zeros((ROWS, QP - D), BF)
    dm[:, :D] = d_mixed.astype(BF)
    dm[:, D:] = jnp.zeros((ROWS, QP - D), BF)
    mx[:, :D] = mixed[...]
    mx[:, D:] = jnp.zeros((ROWS, QP - D), BF)
    span = GROUP * BLK
    for i in range(2):
        for g in range(KV_HEADS):
            for r in range(GROUP):
                head = g * GROUP + r
                there = slice(r * BLK, (r + 1) * BLK)
                qd[i, g, there, :] = head_tile(q_ref, i, head, False).astype(BF)
                do = head_tile(dm, i, head, True)
                qd[i, g, span + r * BLK : span + (r + 1) * BLK, :] = do.astype(BF)
                dots = jnp.sum(do * head_tile(mx, i, head, True), axis=1, keepdims=True)
                delta[i, g, there, :] = jnp.broadcast_to(dots, (BLK, 128))
    dq[...] = jnp.zeros(dq.shape, F32)
    dkv[...] = jnp.zeros(dkv.shape, F32)

    def step(t, carry):
        block, chunk, place = step_place(info, t)
        allowed = causal(place, chunk)
        at = pl.multiple_of(chunk * CHUNK, CHUNK)
        for g in range(KV_HEADS):
            keys = kvs[pl.ds(at, CHUNK), g * 128 : (g + 1) * 128]
            both = dot(qd[block, g], keys, NT)
            scores, d_probs = both[:span], both[span:]
            total = lse[block, g]
            probs = jnp.exp(
                jnp.where(allowed, scores, NEG) - jnp.concatenate([total, total], axis=1)
            )
            shift = delta[block, g]
            d_scores = probs * (d_probs - jnp.concatenate([shift, shift], axis=1))
            d_low = d_scores.astype(BF)
            dq[block, g] += dot(d_low, keys)
            stacked = jnp.concatenate([d_low, probs.astype(BF)], axis=0)
            dkv[pl.ds(at, CHUNK), g * 128 : (g + 1) * 128] += dot(stacked, qd[block, g], TN)
        return carry

    lax.fori_loop(0, STEPS, step, 0)
    for i in range(2):
        rows = slice(i * BLK, (i + 1) * BLK)
        cos, sin = cosine[rows, :], sine[rows, :]
        heads = []
        for g in range(KV_HEADS):
            for r in range(GROUP):
                heads.append(dq[i, g, r * BLK : (r + 1) * BLK, :] * (HEAD**-0.5))
        for j in range(8):
            if j < 7:
                high = pltpu.roll(heads[2 * j + 1], 64, 1)
                tile = jnp.where(lane(high.shape) < HEAD, heads[2 * j], high)
                dq_out[rows, j * 128 : (j + 1) * 128] = spin(tile, cos, -sin).astype(BF)
            else:
                dq_out[rows, 896:960] = spin(heads[14], cos, -sin)[:, :64].astype(BF)
    number = 0
    for out in (o0, o1, o2, o3):
        for b in range(out.shape[0] // BLK):
            at = pl.multiple_of(info[36 + number] * BLK, BLK)
            out[b * BLK : (b + 1) * BLK, :] = dkv[pl.ds(at, BLK), :].astype(BF)
            number += 1


def attend_back(info, parts, grad, resid, gain, wo, normed, mixed, q, lse, kvs, cosine, sine, after=()):
    outs = [
        ((ROWS, D), F32),
        ((ROWS, D), BF),
        ((1, D), F32),
        ((ROWS, D), BF),
        ((ROWS, QP + D), BF),
    ] + [((4 * ROWS, 2 * KW), BF)] * 4
    shape = (2, KV_HEADS, GROUP * BLK, 128)
    scratch = [
        pltpu.VMEM((2, KV_HEADS, 2 * GROUP * BLK, 128), BF),
        pltpu.VMEM(shape, F32),
        pltpu.VMEM(shape, F32),
        pltpu.VMEM((SEQ, 2 * KW), F32),
        pltpu.VMEM((ROWS, QP), BF),
        pltpu.VMEM((ROWS, QP), BF),
        pltpu.VMEM((2, ROWS, D // 2), BF),
    ]
    return call(attend_back_body, outs, 24.0, 32, scratch, smem=1)(
        info, *parts, grad, resid, gain, *wo, normed, mixed, q, lse, kvs, cosine, sine, after=after
    )


def project_back_body(
    info, k0, k1, k2, k3, dq, d_resid, d_low, x_ref, gain, own, other, cosine, sine,
    cut_out, grad_out, dc_out, halves, dkv,
):
    side, z = info[0], info[1]
    sums = k0[...].astype(F32) + k1[...].astype(F32) + k2[...].astype(F32) + k3[...].astype(F32)
    cos, sin = cosine[...], -sine[...]
    halves[0] = dq[:, :HALF]
    halves[1] = jnp.zeros((ROWS, HALF), BF)
    halves[1, :, :HEAD] = dq[:, HALF:]
    for g in range(KV_HEADS):
        tile = sums[:, g * 128 : (g + 1) * 128]
        tile = jnp.where(lane(tile.shape) < HEAD, spin(tile, cos, sin), tile)
        dkv[:, g * 128 : (g + 1) * 128] = tile
        halves[1, :, (g + 1) * 128 : (g + 2) * 128] = tile.astype(BF)
    d_normed = dot(halves[side], own[:, :HALF], NT) + dot(halves[1 - side], other[:, :HALF], NT)
    dx, dc = norm_back(x_ref[...], gain[...], d_normed)
    dc_out[...] = dc
    grad_out[...] = d_resid[...] + dx
    query, low = dq[...].astype(F32), d_low[...].astype(F32)
    quarters = (
        query[:, :640],
        jnp.concatenate([query[:, 640:], dkv[:, :320]], axis=1),
        jnp.concatenate([dkv[:, 320:], low[:, :320]], axis=1),
        low[:, 320:],
    )
    for place in range(4):
        cut_out[(place + 4 - z) % 4] = quarters[place].astype(BF)


def project_back(info, pieces, dq, d_resid, d_low, x, gain, weight, cosine, sine, after=()):
    outs = [((4, ROWS, 640), BF), ((ROWS, D), F32), ((1, D), F32)]
    scratch = [pltpu.VMEM((2, ROWS, HALF), BF), pltpu.VMEM((ROWS, 2 * KW), F32)]
    return call(project_back_body, outs, 3.2, 16, scratch, smem=1)(
        info, *pieces, dq, d_resid, d_low, x, gain, *weight, cosine, sine, after=after
    )


def slot_of(info, c, given):
    place = info[68 + c]
    return (place % 4) * 4 + place // 4 if given else place


def feed_grads_body(*refs):
    info = refs[0]
    seconds, dgus, hiddens, lows = (refs[1 + 4 * i : 5 + 4 * i] for i in range(4))
    keep_out, give_out, left, right, hidden, low, acc, down, group = refs[17:]
    side = info[0]
    for k in range(4):
        rows = slice(k * ROWS, (k + 1) * ROWS)
        left[rows, :] = seconds[k][...]
        hidden[rows, :] = hiddens[k][...]
        low[rows, :] = lows[k][...]
        for h in range(2):
            right[h, rows, :] = dgus[k][h]
    down[...] = dot(hidden[...], low[...], TN)
    group[90:, :] = jnp.zeros((6, 640), F32)
    for turn, out in ((0, keep_out), (1, give_out)):
        half = side if turn == 0 else 1 - side
        acc[...] = dot(left[...], right[half], TN)
        for h in range(2):

            @pl.when(half == h)
            def _():
                for c in range(16):
                    at = 40 * c + 20 * h
                    group[:60, :] = acc[60 * c : 60 * c + 60, :]
                    group[60:80, :] = down[at : at + 20, :640]
                    group[80:90, :320] = down[at : at + 10, 640:]
                    group[80:90, 320:] = down[at + 10 : at + 20, 640:]
                    out[slot_of(info, c, turn)] = group[...].astype(BF)


def feed_grads(info, seconds, dgus, hiddens, lows, after=()):
    rows = 4 * ROWS
    scratch = [
        pltpu.VMEM((rows, D), BF),
        pltpu.VMEM((2, rows, 640), BF),
        pltpu.VMEM((rows, 640), BF),
        pltpu.VMEM((rows, D), BF),
        pltpu.VMEM((D, 640), F32),
        pltpu.VMEM((640, D), F32),
        pltpu.VMEM((96, 640), F32),
    ]
    return call(feed_grads_body, [((16, 96, 640), BF)] * 2, 6.5, 24, scratch, smem=1)(
        info, *seconds, *dgus, *hiddens, *lows, after=after
    )


def attend_grads_body(*refs):
    info = refs[0]
    mines, aheads = refs[1:5], refs[5:9]
    dc_one, dc_two, keep_out, give_out, lhs, mine, acc, group = refs[9:]
    side, z = info[0], info[1]
    for k in range(4):
        rows = slice(k * ROWS, (k + 1) * ROWS)
        for h in range(2):
            mine[h, rows, :] = mines[k][:, h * 320 : (h + 1) * 320].astype(F32).astype(BF)
        lhs[0, rows, :] = aheads[k][:, :D]
        lhs[1, rows, :] = aheads[k][:, QP:]
    group[60:, :] = jnp.zeros((4, 384), F32)
    for turn, out in ((0, keep_out), (1, give_out)):
        h = side if turn == 0 else 1 - side
        which = jnp.where(z + h >= 3, 1, 0)
        acc[:, :320] = dot(lhs[which], mine[h], TN)
        gain_row = jnp.where(h == 0, dc_one[...], dc_two[...])
        first = lax.broadcasted_iota(jnp.int32, (8, D), 0) == 0
        spread = jnp.where(first, jnp.broadcast_to(gain_row, (8, D)), 0.0)
        acc[:, 320:] = dot(spread, jnp.ones((8, 64), F32), TN)
        for c in range(16):
            group[:60, :] = acc[60 * c : 60 * c + 60, :]
            out[slot_of(info, c, turn)] = group[...].astype(BF)


def attend_grads(info, mines, aheads, dc_one, dc_two):
    rows = 4 * ROWS
    scratch = [
        pltpu.VMEM((2, rows, D), BF),
        pltpu.VMEM((2, rows, 320), BF),
        pltpu.VMEM((D, 384), F32),
        pltpu.VMEM((64, 384), F32),
    ]
    return call(attend_grads_body, [((16, 64, 384), BF)] * 2, 3.0, 16, scratch, smem=1)(
        info, *mines, *aheads, dc_one, dc_two
    )


def finish_body(info, p0, p1, p2, p3, *outs):
    n1, gq, gk, gv, go, n2, gate, up = outs[:8]
    placed = outs[8]
    z = info[1]
    for k, piece in enumerate((p0, p1, p2, p3)):
        placed[(z + 4 - k) % 4] = piece[...]
    att = []
    for place in range(4):
        gate[:, 0, place * 640 : (place + 1) * 640] = placed[place, :, :640]
        up[:, 0, place * 640 : (place + 1) * 640] = placed[place, :, 1024:1664]
        att += [placed[place, :, 640:960], placed[place, :, 1664:1984]]
    gq[:, 0, :] = jnp.concatenate(att[:3], axis=1)
    go[:, 0, :] = jnp.concatenate(att[5:], axis=1)
    both = jnp.concatenate(att[3:5], axis=1)
    gk[:, 0, :] = jnp.concatenate([both[:, g * 128 : g * 128 + 64] for g in range(KV_HEADS)], axis=1)
    gv[:, 0, :] = jnp.concatenate([both[:, g * 128 + 64 : g * 128 + 128] for g in range(KV_HEADS)], axis=1)
    total = placed[0] + placed[1] + placed[2] + placed[3]
    n1[...] = total[:, 960:1024]
    n2[...] = total[:, 1984:2048]


def finish(info, pieces):
    widths = [D, KW, KW, D, FF, FF]
    shapes = [(15, 1, width) for width in widths]
    shapes = [(15, 64)] + shapes[:4] + [(15, 64)] + shapes[4:]
    return call(
        finish_body, [(s, F32) for s in shapes], 1.5, 8, [pltpu.VMEM((4, 15, 2048), F32)], smem=1
    )(info, *pieces)


def z_shift(value, steps):
    return lax.ppermute(value, "wsh", [(i, (i + steps) % 4) for i in range(4)])


def ctx_shift(value, steps, core_along_x):
    pairs = []
    for core in range(2):
        for y in range(4):
            for x in range(4):
                to = (y, (x + steps) % 4) if core == core_along_x else ((y + steps) % 4, x)
                pairs.append((core * 16 + y * 4 + x, core * 16 + to[0] * 4 + to[1]))
    return lax.ppermute(value, ("section", "ctx"), pairs)


def gather_shift(value, steps):
    return ctx_shift(value, steps, 0)


def reduce_shift(value, steps):
    return ctx_shift(value, steps, 1)


def swap(value):
    return lax.ppermute(value, "section", [(0, 1), (1, 0)])


def add(first, *others):
    total = first.astype(F32)
    for other in others:
        total = total + other.astype(F32)
    return total


def in_order(pieces, rank):
    stacked = jnp.stack(pieces)
    return [lax.dynamic_index_in_dim(stacked, (rank - z) % 4, 0, False) for z in range(4)]


def shards(
    tokens, cotangent, block_order, norm_one, w_query, w_key, w_value, w_out, norm_two, w_gate, w_up, w_down
):
    section = lax.axis_index("section")
    rank = lax.axis_index("ctx")
    z_rank = lax.axis_index("wsh")
    first_core = section == 0
    quarter = FF // 4

    def both(value):
        other = swap(value)
        return jnp.where(first_core, value, other), jnp.where(first_core, other, value)

    key_value = jnp.concatenate(
        [w_key[0].reshape(-1, KV_HEADS, HEAD), w_value[0].reshape(-1, KV_HEADS, HEAD)], axis=2
    ).reshape(-1, 2 * KW)
    shard_rows = w_query.shape[1]
    low_half = jnp.concatenate([w_query[0][:, :HALF], w_out[0][:, : D // 2]], axis=1)
    high_half = jnp.concatenate(
        [
            w_query[0][:, HALF:],
            jnp.zeros((shard_rows, HEAD), BF),
            key_value,
            jnp.zeros((shard_rows, 128), BF),
            w_out[0][:, D // 2 :],
        ],
        axis=1,
    )
    got = swap(jnp.where(first_core, high_half, low_half))
    layer_half = (jnp.where(first_core, low_half, got), jnp.where(first_core, got, high_half))

    def whole(part):
        full = lax.all_gather(part, "wsh", axis=0, tiled=True)
        return full, swap(full)

    gathered = tuple(whole(part) for part in layer_half)

    gains = jnp.stack([norm_one[0], norm_two[0]])
    gain_parts = [gains] + [z_shift(gains, k) for k in (1, 2, 3)]
    gains = jnp.concatenate(in_order(gain_parts, z_rank), axis=1)
    gain_pair = [g.astype(F32) for g in both(gains)]

    given = swap(jnp.where(first_core, w_up[0], w_gate[0]))
    kind = (jnp.where(first_core, w_gate[0], given), jnp.where(first_core, given, w_up[0]))

    wd = both(w_down[0])

    def none_of(mark):
        return (mark != mark).astype(jnp.int32)

    def send_feed_weights(mark):
        later = none_of(mark)

        def columns(z):
            start = z * quarter + later
            return jnp.concatenate(
                [lax.dynamic_slice_in_dim(k, start, quarter, 1) for k in kind], axis=1
            )

        return [columns(z_rank)] + [z_shift(columns((z_rank + k) % 4), k) for k in (1, 2, 3)]

    def join_feed_weights(parts, mark):
        later = none_of(mark)
        ordered = jnp.concatenate(in_order(parts, z_rank + later), axis=0)
        other = swap(ordered)
        return [(ordered[:, layer * quarter : (layer + 1) * quarter], other) for layer in range(2)]

    own = lax.dynamic_slice_in_dim(block_order, 2 * rank, 2, 0)
    pairs = block_order.reshape(4, 4, 2)
    y, x = rank // 4, rank % 4
    step = jnp.arange(4, dtype=jnp.int32)

    def by_core(table):
        return jnp.where(first_core, table, jnp.swapaxes(table, 0, 1))

    came = by_core(pairs[(y - step) % 4][:, (x - step) % 4]).reshape(32)
    goes = by_core(pairs[(y + step) % 4][:, (x + step) % 4]).reshape(32)
    ahead_y = ((step - y) % 4)[:, None]
    ahead_x = ((step - x) % 4)[None, :]
    slot = jnp.where(first_core, ahead_y * 4 + ahead_x, ahead_x * 4 + ahead_y).reshape(16)
    info = jnp.concatenate([jnp.stack([section, z_rank]), own, came, goes, slot]).astype(jnp.int32)
    offsets = jnp.arange(BLK, dtype=jnp.int32)
    local_pos = (own[:, None] * BLK + offsets[None, :]).reshape(ROWS)
    frequency = jnp.exp(
        jnp.arange(HEAD // 2).astype(F32) * (-2.0 * math.log(ROPE_BASE) / HEAD)
    )
    angle = local_pos.astype(F32)[:, None] * frequency[None, :]
    cos32, sin32 = jnp.cos(angle), jnp.sin(angle)
    cosine = jnp.concatenate([cos32] * 4, axis=1)
    sine = jnp.concatenate([-sin32, sin32, -sin32, sin32], axis=1)

    own_tokens = lax.dynamic_index_in_dim(tokens, section, 0, False)[0]
    own_cotangent = lax.dynamic_index_in_dim(cotangent, section, 0, False)[0]

    def z_gather(value):
        return [value] + [z_shift(value, k) for k in (1, 2, 3)]

    last_lows = z_gather(own_cotangent.astype(BF))
    saved = []
    base, parts = own_tokens, []
    for layer in range(2):
        gain_one = gain_pair[layer][0:1]
        gain_two = gain_pair[layer][1:2]
        ahead = (saved[0]["normed"], saved[0]["mixed"]) if layer else ()
        x_in, normed, q, kv, *ahead = project(
            info, base, parts, gain_one, gathered[layer], cosine, sine, ahead
        )
        if layer:
            first_aheads = z_gather(ahead[0])
        row = jnp.concatenate([kv] + [gather_shift(kv, k) for k in (1, 2, 3)], axis=0)
        pieces = [row] + [reduce_shift(row, k) for k in (1, 2, 3)]
        if layer == 0:
            sent = send_feed_weights(pieces[1][0, 0] + pieces[2][0, 0] + pieces[3][0, 0])
        mixed, lse, kvs, resid, second = attend(
            info, q, pieces, gathered[layer], x_in, gain_two, after=last_lows[1:] if layer else wd
        )
        if layer == 0:
            wgu = join_feed_weights(sent, second[0, 0])
        seconds = z_gather(second)
        after = first_aheads[1:] if layer else ()
        fed = [feed(layer, info, s, wgu[layer], wd[layer], after) for s in seconds]
        parts = [fed[0][2]] + [z_shift(fed[k][2], -k) for k in (1, 2, 3)]
        base = resid
        saved.append(
            dict(
                x=x_in, q=q, mixed=mixed, lse=lse, kvs=kvs, resid=resid,
                normed=normed,
                seconds=seconds, gu=[f[0] for f in fed], hidden=[f[1] for f in fed],
            )
        )
    outputs = [saved[1]["x"], add(base, *parts)]

    grad = own_cotangent
    lows = last_lows
    input_grads = [None, None]
    feed_sums = [None, None]
    kept = [None, None]
    order = ()

    def stage_one(half, later=0):
        cut = [lax.dynamic_slice_in_dim(half, 4 * k + later, 4, 0) for k in range(4)]
        return add(cut[0], *[reduce_shift(cut[k], k) for k in (1, 2, 3)])

    def stage_two(stage):
        low = stage.astype(BF)
        return add(stage[0], *[gather_shift(low[k], k) for k in (1, 2, 3)])

    for layer in (1, 0):
        s = saved[layer]
        gain_one = gain_pair[layer][0:1]
        gain_two = gain_pair[layer][1:2]
        back = [feed_back(layer, info, lows[k], s["gu"][k], wgu[layer], wd[layer]) for k in range(4)]
        parts = [back[0][1]] + [z_shift(back[k][1], -k) for k in (1, 2, 3)]
        keep, give = feed_grads(info, s["seconds"], [b[0] for b in back], s["hidden"], lows)
        d_resid, d_low, dc_two, dq, ahead, *goes_out = attend_back(
            info, parts, grad, s["resid"], gain_two, gathered[layer], s["normed"], s["mixed"], s["q"],
            s["lse"], s["kvs"], cosine, sine, after=(keep, *order),
        )
        feed_half = add(keep, swap(give)).astype(BF)
        row = add(goes_out[0], *[reduce_shift(goes_out[k], k) for k in (1, 2, 3)])
        row = row.astype(BF).reshape(4, ROWS, 2 * KW)
        own_pieces = [row[0]] + [gather_shift(row[k], k) for k in (1, 2, 3)]
        aheads = z_gather(ahead) if layer else first_aheads
        if layer == 0:
            kept[1] = attention_grads(none_of(d_low[0, 0]))
        cut, grad, dc_one = project_back(
            info, own_pieces, dq, d_resid, d_low, s["x"], gain_one, gathered[layer], cosine, sine,
            after=tuple(aheads[1:]) if layer else (),
        )
        input_grads[layer] = grad
        feed_stage = stage_one(feed_half, none_of(cut[0, 0, 0]))
        if layer:
            lows = z_gather(grad.astype(BF))
            order = (feed_stage,)
            feed_sums[1] = stage_two(feed_stage)

        def attention_grads(later, cut=cut, aheads=aheads, dc_one=dc_one, dc_two=dc_two):
            mines = [lax.dynamic_index_in_dim(cut, k + later, 0, False) for k in range(4)]
            mines = [mines[0]] + [z_shift(mines[k], k) for k in (1, 2, 3)]
            keep, give = attend_grads(info, mines, aheads, dc_one, dc_two)
            return add(keep, swap(give)).astype(BF)

        if layer == 0:
            kept[0] = attention_grads(0)
    attend_stage = stage_one(jnp.concatenate(kept, axis=2))
    both_sums = stage_two(
        jnp.concatenate([feed_stage, jnp.pad(attend_stage, ((0, 0), (0, 32), (0, 0)))], axis=2)
    )
    feed_sums[0], attend_sum = both_sums[:, :640], both_sums[:64, 640:]
    sums = [
        jnp.concatenate(
            [feed_sums[layer], jnp.pad(attend_sum[:, layer * 384 : (layer + 1) * 384], ((0, 32), (0, 0)))],
            axis=1,
        )
        for layer in range(2)
    ]

    mine = jnp.where(first_core, sums[0], sums[1])
    other = swap(jnp.where(first_core, sums[1], sums[0]))
    halves = (jnp.where(first_core, mine, other), jnp.where(first_core, other, mine))
    joined = jnp.concatenate([h[:60] for h in halves], axis=1).reshape(4, 15, 2048)
    pieces = [lax.dynamic_index_in_dim(joined, z_rank, 0, False)] + [
        z_shift(lax.dynamic_index_in_dim(joined, (z_rank + k) % 4, 0, False), k) for k in (1, 2, 3)
    ]
    down = jnp.concatenate(
        [
            jnp.concatenate(
                [h[60:80, :640], jnp.concatenate([h[80:90, :320], h[80:90, 320:640]], axis=0)], axis=1
            )
            for h in halves
        ],
        axis=0,
    )
    moves = [(c * 4 + z, (4 * z + c // 4) * 4 + c % 4) for c in range(16) for z in range(4)]
    grad_down = lax.ppermute(down, ("ctx", "wsh"), moves)[None]
    sum_one, gq, gk, gv, go, sum_two, gate, up = finish(info, pieces)
    grad_query, grad_key, grad_value, grad_out, grad_gate, grad_up = (
        jnp.swapaxes(g, 0, 1) for g in (gq, gk, gv, go, gate, up)
    )

    def arranged(pair):
        mine = jnp.where(first_core, pair[0], pair[1])
        other = swap(jnp.where(first_core, pair[1], pair[0]))
        first = jnp.where(first_core, mine, other)
        last = jnp.where(first_core, other, mine)
        return jnp.stack([first, last])[None, :, None]

    return (
        arranged(outputs),
        arranged(input_grads),
        sum_one[:, 0][None],
        grad_query,
        grad_key,
        grad_value,
        grad_out,
        sum_two[:, 0][None],
        grad_gate,
        grad_up,
        grad_down,
    )


def solution(mesh):
    rows = P(None, "wsh", "ctx", None)
    gain = P("section", "wsh")
    weight = P("section", "wsh", None)
    in_specs = (rows, rows, P(), gain, weight, weight, weight, weight, gain, weight, weight, weight)
    result = P("section", None, "wsh", "ctx", None)
    gain_out = P("section", ("ctx", "wsh"))
    weight_out = P("section", ("ctx", "wsh"), None)
    out_specs = (
        result, result, gain_out, weight_out, weight_out, weight_out, weight_out, gain_out,
        weight_out, weight_out, weight_out,
    )
    return jax.shard_map(shards, mesh=mesh, in_specs=in_specs, out_specs=out_specs, check_vma=False)
```

```python
import math
from functools import partial

import jax
import jax.numpy as jnp
from jax import lax
from jax.experimental import pallas as pl
from jax.experimental.pallas import tpu as pltpu
from jax.sharding import PartitionSpec as P

HEADS = 15
KV_HEADS = 5
HEAD = 64
GROUP = HEADS // KV_HEADS
D = 960
FF = 2560
KW = KV_HEADS * HEAD
ROWS = 128
BLK = 64
SEQ = 2048
CHUNK = 256
STEPS = 9
EPS = 1e-05
ROPE_BASE = 10000.0
BF = jnp.bfloat16
F32 = jnp.float32
QP = 1024
HALF = 896
NEG = -1e30
MIB = 1024 * 1024

NN = (((1,), (0,)), ((), ()))
NT = (((1,), (1,)), ((), ()))
TN = (((0,), (0,)), ((), ()))


def dot(left, right, dims=NN):
    return lax.dot_general(left, right, dims, preferred_element_type=F32)


def call(body, outs, micros, mib, scratch=(), smem=0):
    def run(*args, after=()):
        count = len(args)
        in_specs = [
            pl.BlockSpec(memory_space=pltpu.SMEM if i < smem else pltpu.VMEM) for i in range(count)
        ] + [pl.BlockSpec(memory_space=pl.ANY) for _ in after]

        def inner(*refs):
            body(*refs[:count], *refs[count + len(after) :])

        out = pl.pallas_call(
            inner,
            in_specs=in_specs,
            out_specs=[pl.BlockSpec(memory_space=pltpu.VMEM) for _ in outs],
            out_shape=[jax.ShapeDtypeStruct(s, t) for s, t in outs],
            scratch_shapes=list(scratch),
            cost_estimate=pl.CostEstimate(
                flops=int(micros * 1.1e9), bytes_accessed=int(micros * 3.6e6), transcendentals=0
            ),
            compiler_params=pltpu.CompilerParams(vmem_limit_bytes=mib * MIB),
        )(*args, *after)
        return out

    return run


def token(*arrays):
    return jnp.stack([a[(0,) * a.ndim].astype(F32) for a in arrays])


def hold(arrays, mark):
    count = len(arrays)

    def body(*refs):
        del refs

    return pl.pallas_call(
        body,
        in_specs=[pl.BlockSpec(memory_space=pl.ANY)] * (count + 1),
        out_specs=[pl.BlockSpec(memory_space=pl.ANY)] * count,
        out_shape=[jax.ShapeDtypeStruct(a.shape, a.dtype) for a in arrays],
        input_output_aliases={i: i for i in range(count)},
    )(*arrays, mark)


def lane(shape):
    return lax.broadcasted_iota(jnp.int32, shape, 1)


def normalise(x, gain):
    return x * lax.rsqrt(jnp.mean(x * x, axis=-1, keepdims=True) + EPS) * gain


def norm_back(x, gain, dy):
    r = lax.rsqrt(jnp.mean(x * x, axis=-1, keepdims=True) + EPS)
    cdy = gain * dy
    dx = r * cdy - x * (r * r * r) * jnp.mean(x * cdy, axis=-1, keepdims=True)
    dc = jnp.sum(dy * x * r, axis=0, keepdims=True)
    return dx, dc


def spin(tile, cosine, sine):
    first = (lane(tile.shape) % HEAD) < HEAD // 2
    swapped = jnp.where(first, pltpu.roll(tile, 96, 1), pltpu.roll(tile, 32, 1))
    return tile * cosine + swapped * sine


def project_body(count):
    def body(*refs):
        info, base = refs[:2]
        parts = refs[2 : 2 + count]
        gain, own, other, cosine, sine = refs[2 + count : 7 + count]
        if count:
            normed_in, mixed_in = refs[7 + count : 9 + count]
            x_out, normed_out, q_out, kv_out, ahead_out, halves = refs[9 + count :]
            ahead_out[:, :D] = normed_in[...]
            ahead_out[:, D:QP] = jnp.zeros((ROWS, QP - D), BF)
            ahead_out[:, QP:] = mixed_in[...]
        else:
            x_out, normed_out, q_out, kv_out, halves = refs[7:]
        side = info[0]
        x = base[...]
        for part in parts:
            x = x + part[...].astype(F32)
        x_out[...] = x
        normed = normalise(x, gain[...]).astype(BF)
        normed_out[...] = normed
        cos, sin = cosine[...], sine[...]
        halves[side] = dot(normed, own[:, :HALF])
        halves[1 - side] = dot(normed, other[:, :HALF])
        for j in range(8):
            tile = halves[0, :, j * 128 : (j + 1) * 128] if j < 7 else halves[1, :, 0:128]
            q_out[:, j * 128 : (j + 1) * 128] = (spin(tile, cos, sin) * (HEAD**-0.5)).astype(BF)
        for g in range(KV_HEADS):
            tile = halves[1, :, (g + 1) * 128 : (g + 2) * 128]
            tile = jnp.where(lane(tile.shape) < HEAD, spin(tile, cos, sin), tile)
            kv_out[:, g * 128 : (g + 1) * 128] = tile.astype(BF)

    return body


def project(info, base, parts, gain, weight, cosine, sine, ahead=()):
    outs = [((ROWS, D), F32), ((ROWS, D), BF), ((ROWS, QP), BF), ((ROWS, 2 * KW), BF)]
    if ahead:
        outs.append(((ROWS, QP + D), BF))
    scratch = [pltpu.VMEM((2, ROWS, HALF), F32)]
    return call(project_body(len(parts)), outs, 2.5, 16, scratch, smem=1)(
        info, base, *parts, gain, *weight, cosine, sine, *ahead
    )


def step_place(info, t):
    first, second = info[2], info[3]
    count = first // 4 + 1
    early = t < count
    block = jnp.where(early, 0, 1)
    chunk = jnp.where(early, t, t - count)
    place = jnp.where(early, first, second)
    return block, chunk, place


def causal(place, chunk):
    rows = lax.broadcasted_iota(jnp.int32, (BLK, CHUNK), 0) + place * BLK
    cols = lax.broadcasted_iota(jnp.int32, (BLK, CHUNK), 1) + chunk * CHUNK
    one = rows >= cols
    return jnp.concatenate([one] * GROUP, axis=0)


def head_tile(ref, block, head, upper):
    j = head // 2
    tile = ref[block * BLK : (block + 1) * BLK, j * 128 : (j + 1) * 128].astype(F32)
    if (head % 2 == 1) != upper:
        tile = pltpu.roll(tile, 64, 1)
    keep = (lane(tile.shape) >= HEAD) if upper else (lane(tile.shape) < HEAD)
    return jnp.where(keep, tile, 0.0)


def attend_body(count):
    def body(*refs):
        info, q_ref = refs[0], refs[1]
        pieces = refs[2 : 2 + count]
        (own, other, x_ref, gain, mixed_out, lse_out, kvs, resid_out, second_out) = refs[
            2 + count : 11 + count
        ]
        qh, top, total, acc, halves = refs[11 + count :]
        side = info[0]
        number = 0
        for piece in pieces:
            for b in range(piece.shape[0] // BLK):
                at = pl.multiple_of(info[4 + number] * BLK, BLK)
                kvs[pl.ds(at, BLK), :] = piece[b * BLK : (b + 1) * BLK, :]
                number += 1
        for i in range(2):
            for g in range(KV_HEADS):
                for r in range(GROUP):
                    qh[i, g, r * BLK : (r + 1) * BLK, :] = head_tile(
                        q_ref, i, g * GROUP + r, False
                    ).astype(BF)
        top[...] = jnp.full(top.shape, NEG, F32)
        total[...] = jnp.zeros(total.shape, F32)
        acc[...] = jnp.zeros(acc.shape, F32)

        def step(t, carry):
            block, chunk, place = step_place(info, t)
            allowed = causal(place, chunk)
            at = pl.multiple_of(chunk * CHUNK, CHUNK)
            for g in range(KV_HEADS):
                keys = kvs[pl.ds(at, CHUNK), g * 128 : (g + 1) * 128]
                scores = dot(qh[block, g], keys, NT)
                scores = jnp.where(allowed, scores, NEG)
                old = top[block, g]
                new = jnp.maximum(old, jnp.max(scores, axis=1, keepdims=True))
                probs = jnp.exp(scores - jnp.concatenate([new, new], axis=1))
                shrink = jnp.exp(old - new)
                top[block, g] = new
                total[block, g] = shrink * total[block, g] + jnp.sum(probs, axis=1, keepdims=True)
                acc[block, g] = shrink * acc[block, g] + dot(probs.astype(BF), keys)
            return carry

        lax.fori_loop(0, STEPS, step, 0)
        for i in range(2):
            heads = []
            for g in range(KV_HEADS):
                sums = total[i, g]
                result = acc[i, g] / sums
                lse_out[i, g] = top[i, g] + jnp.log(sums)
                for r in range(GROUP):
                    heads.append(result[r * BLK : (r + 1) * BLK, :])
            for j in range(8):
                low = pltpu.roll(heads[2 * j], 64, 1)
                rows = slice(i * BLK, (i + 1) * BLK)
                if j < 7:
                    tile = jnp.where(lane(low.shape) < HEAD, low, heads[2 * j + 1])
                    mixed_out[rows, j * 128 : (j + 1) * 128] = tile.astype(BF)
                else:
                    mixed_out[rows, 896:960] = low[:, :64].astype(BF)
        halves[side] = dot(mixed_out[...], own[:, HALF:])
        halves[1 - side] = dot(mixed_out[...], other[:, HALF:])
        resid = x_ref[...] + jnp.concatenate([halves[0], halves[1]], axis=1)
        resid_out[...] = resid
        second_out[...] = normalise(resid, gain[...]).astype(BF)

    return body


def attend(info, q, pieces, wo, x, gain, after=()):
    outs = [
        ((ROWS, D), BF),
        ((2, KV_HEADS, GROUP * BLK, 128), F32),
        ((SEQ, 2 * KW), BF),
        ((ROWS, D), F32),
        ((ROWS, D), BF),
    ]
    shape = (2, KV_HEADS, GROUP * BLK, 128)
    scratch = [pltpu.VMEM(shape, BF)] + [pltpu.VMEM(shape, F32)] * 3
    scratch.append(pltpu.VMEM((2, ROWS, D // 2), F32))
    return call(attend_body(len(pieces)), outs, 12.0, 18, scratch, smem=1)(
        info, q, *pieces, *wo, x, gain, after=after
    )


def feed_body(layer, info, second, own, other, wd, gu_out, hidden_out, part_out):
    side = info[0]
    columns = slice(layer * FF // 4, (layer + 1) * FF // 4)
    gu_out[side] = dot(second[...], own[...])
    gu_out[1 - side] = dot(second[...], other[:, columns])
    gate, up = gu_out[0], gu_out[1]
    hidden = (gate / (1.0 + jnp.exp(-gate)) * up).astype(BF)
    hidden_out[...] = hidden
    part_out[...] = dot(hidden, wd[...]).astype(BF)


def feed(layer, info, second, wgu, wd, after=()):
    outs = [((2, ROWS, FF // 4), F32), ((ROWS, FF // 4), BF), ((ROWS, D), BF)]
    body = partial(feed_body, layer)
    return call(body, outs, 1.0, 12, smem=1)(info, second, *wgu, wd, after=after)


def feed_back_body(layer, info, grad_low, gu, own, other, wd, dgu_out, part_out):
    side = info[0]
    columns = slice(layer * FF // 4, (layer + 1) * FF // 4)
    d_hidden = dot(grad_low[...], wd[...], NT)
    gate, up = gu[0], gu[1]
    sig = 1.0 / (1.0 + jnp.exp(-gate))
    d_gate = d_hidden * up * sig * (1.0 + gate * (1.0 - sig))
    d_up = d_hidden * gate * sig
    dgu_out[0] = d_gate.astype(BF)
    dgu_out[1] = d_up.astype(BF)
    part = dot(dgu_out[side], own[...], NT) + dot(dgu_out[1 - side], other[:, columns], NT)
    part_out[...] = part.astype(BF)


def feed_back(layer, info, grad_low, gu, wgu, wd):
    outs = [((2, ROWS, FF // 4), BF), ((ROWS, D), BF)]
    body = partial(feed_back_body, layer)
    return call(body, outs, 1.3, 12, smem=1)(info, grad_low, gu, *wgu, wd)


def attend_back_body(
    info, p0, p1, p2, p3, grad, resid, gain, own, other, normed, mixed, q_ref, lse, kvs, cosine, sine,
    d_resid_out, d_low_out, dc_out, dq_out, ahead_out, o0, o1, o2, o3,
    qd, delta, dq, dkv, dm, mx, halves,
):
    d_second = p0[...].astype(F32) + p1[...].astype(F32) + p2[...].astype(F32) + p3[...].astype(F32)
    dx, dc = norm_back(resid[...], gain[...], d_second)
    dc_out[...] = dc
    d_resid = grad[...] + dx
    d_resid_out[...] = d_resid
    low = d_resid.astype(BF)
    d_low_out[...] = low
    side = info[0]
    halves[0] = d_resid[:, : D // 2].astype(BF)
    halves[1] = d_resid[:, D // 2 :].astype(BF)
    d_mixed = dot(halves[side], own[:, HALF:], NT) + dot(halves[1 - side], other[:, HALF:], NT)
    ahead_out[:, :D] = normed[...]
    ahead_out[:, QP : QP + D] = mixed[...]
    ahead_out[:, D:QP] = jnp.zeros((ROWS, QP - D), BF)
    dm[:, :D] = d_mixed.astype(BF)
    dm[:, D:] = jnp.zeros((ROWS, QP - D), BF)
    mx[:, :D] = mixed[...]
    mx[:, D:] = jnp.zeros((ROWS, QP - D), BF)
    span = GROUP * BLK
    for i in range(2):
        for g in range(KV_HEADS):
            for r in range(GROUP):
                head = g * GROUP + r
                there = slice(r * BLK, (r + 1) * BLK)
                qd[i, g, there, :] = head_tile(q_ref, i, head, False).astype(BF)
                do = head_tile(dm, i, head, True)
                qd[i, g, span + r * BLK : span + (r + 1) * BLK, :] = do.astype(BF)
                dots = jnp.sum(do * head_tile(mx, i, head, True), axis=1, keepdims=True)
                delta[i, g, there, :] = jnp.broadcast_to(dots, (BLK, 128))
    dq[...] = jnp.zeros(dq.shape, F32)
    dkv[...] = jnp.zeros(dkv.shape, F32)

    def step(t, carry):
        block, chunk, place = step_place(info, t)
        allowed = causal(place, chunk)
        at = pl.multiple_of(chunk * CHUNK, CHUNK)
        for g in range(KV_HEADS):
            keys = kvs[pl.ds(at, CHUNK), g * 128 : (g + 1) * 128]
            both = dot(qd[block, g], keys, NT)
            scores, d_probs = both[:span], both[span:]
            total = lse[block, g]
            probs = jnp.exp(
                jnp.where(allowed, scores, NEG) - jnp.concatenate([total, total], axis=1)
            )
            shift = delta[block, g]
            d_scores = probs * (d_probs - jnp.concatenate([shift, shift], axis=1))
            d_low = d_scores.astype(BF)
            dq[block, g] += dot(d_low, keys)
            stacked = jnp.concatenate([d_low, probs.astype(BF)], axis=0)
            dkv[pl.ds(at, CHUNK), g * 128 : (g + 1) * 128] += dot(stacked, qd[block, g], TN)
        return carry

    lax.fori_loop(0, STEPS, step, 0)
    for i in range(2):
        rows = slice(i * BLK, (i + 1) * BLK)
        cos, sin = cosine[rows, :], sine[rows, :]
        heads = []
        for g in range(KV_HEADS):
            for r in range(GROUP):
                heads.append(dq[i, g, r * BLK : (r + 1) * BLK, :] * (HEAD**-0.5))
        for j in range(8):
            if j < 7:
                high = pltpu.roll(heads[2 * j + 1], 64, 1)
                tile = jnp.where(lane(high.shape) < HEAD, heads[2 * j], high)
                dq_out[rows, j * 128 : (j + 1) * 128] = spin(tile, cos, -sin).astype(BF)
            else:
                dq_out[rows, 896:960] = spin(heads[14], cos, -sin)[:, :64].astype(BF)
    number = 0
    for out in (o0, o1, o2, o3):
        for b in range(out.shape[0] // BLK):
            at = pl.multiple_of(info[36 + number] * BLK, BLK)
            out[b * BLK : (b + 1) * BLK, :] = dkv[pl.ds(at, BLK), :].astype(BF)
            number += 1


def attend_back(info, parts, grad, resid, gain, wo, normed, mixed, q, lse, kvs, cosine, sine, after=()):
    outs = [
        ((ROWS, D), F32),
        ((ROWS, D), BF),
        ((1, D), F32),
        ((ROWS, D), BF),
        ((ROWS, QP + D), BF),
    ] + [((4 * ROWS, 2 * KW), BF)] * 4
    shape = (2, KV_HEADS, GROUP * BLK, 128)
    scratch = [
        pltpu.VMEM((2, KV_HEADS, 2 * GROUP * BLK, 128), BF),
        pltpu.VMEM(shape, F32),
        pltpu.VMEM(shape, F32),
        pltpu.VMEM((SEQ, 2 * KW), F32),
        pltpu.VMEM((ROWS, QP), BF),
        pltpu.VMEM((ROWS, QP), BF),
        pltpu.VMEM((2, ROWS, D // 2), BF),
    ]
    return call(attend_back_body, outs, 24.0, 22, scratch, smem=1)(
        info, *parts, grad, resid, gain, *wo, normed, mixed, q, lse, kvs, cosine, sine, after=after
    )


def project_back_body(
    info, k0, k1, k2, k3, dq, d_resid, d_low, x_ref, gain, own, other, cosine, sine,
    cut_out, grad_out, dc_out, halves, dkv,
):
    side, z = info[0], info[1]
    sums = k0[...].astype(F32) + k1[...].astype(F32) + k2[...].astype(F32) + k3[...].astype(F32)
    cos, sin = cosine[...], -sine[...]
    halves[0] = dq[:, :HALF]
    halves[1] = jnp.zeros((ROWS, HALF), BF)
    halves[1, :, :HEAD] = dq[:, HALF:]
    for g in range(KV_HEADS):
        tile = sums[:, g * 128 : (g + 1) * 128]
        tile = jnp.where(lane(tile.shape) < HEAD, spin(tile, cos, sin), tile)
        dkv[:, g * 128 : (g + 1) * 128] = tile
        halves[1, :, (g + 1) * 128 : (g + 2) * 128] = tile.astype(BF)
    d_normed = dot(halves[side], own[:, :HALF], NT) + dot(halves[1 - side], other[:, :HALF], NT)
    dx, dc = norm_back(x_ref[...], gain[...], d_normed)
    dc_out[...] = dc
    grad_out[...] = d_resid[...] + dx
    query, low = dq[...].astype(F32), d_low[...].astype(F32)
    quarters = (
        query[:, :640],
        jnp.concatenate([query[:, 640:], dkv[:, :320]], axis=1),
        jnp.concatenate([dkv[:, 320:], low[:, :320]], axis=1),
        low[:, 320:],
    )
    for place in range(4):
        cut_out[(place + 4 - z) % 4] = quarters[place].astype(BF)


def project_back(info, pieces, dq, d_resid, d_low, x, gain, weight, cosine, sine, after=()):
    outs = [((4, ROWS, 640), BF), ((ROWS, D), F32), ((1, D), F32)]
    scratch = [pltpu.VMEM((2, ROWS, HALF), BF), pltpu.VMEM((ROWS, 2 * KW), F32)]
    return call(project_back_body, outs, 3.2, 16, scratch, smem=1)(
        info, *pieces, dq, d_resid, d_low, x, gain, *weight, cosine, sine, after=after
    )


def slot_of(info, c, given):
    place = info[68 + c]
    return (place % 4) * 4 + place // 4 if given else place


def feed_grads_body(*refs):
    info = refs[0]
    seconds, dgus, hiddens, lows = (refs[1 + 4 * i : 5 + 4 * i] for i in range(4))
    keep_out, give_out, left, right, hidden, low, acc, down, group = refs[17:]
    side = info[0]
    for k in range(4):
        rows = slice(k * ROWS, (k + 1) * ROWS)
        left[rows, :] = seconds[k][...]
        hidden[rows, :] = hiddens[k][...]
        low[rows, :] = lows[k][...]
        for h in range(2):
            right[h, rows, :] = dgus[k][h]
    down[...] = dot(hidden[...], low[...], TN)
    group[90:, :] = jnp.zeros((6, 640), F32)
    for turn, out in ((0, keep_out), (1, give_out)):
        half = side if turn == 0 else 1 - side
        acc[...] = dot(left[...], right[half], TN)
        for h in range(2):

            @pl.when(half == h)
            def _():
                for c in range(16):
                    at = 40 * c + 20 * h
                    group[:60, :] = acc[60 * c : 60 * c + 60, :]
                    group[60:80, :] = down[at : at + 20, :640]
                    group[80:90, :320] = down[at : at + 10, 640:]
                    group[80:90, 320:] = down[at + 10 : at + 20, 640:]
                    out[slot_of(info, c, turn)] = group[...].astype(BF)


def feed_grads(info, seconds, dgus, hiddens, lows, after=()):
    rows = 4 * ROWS
    scratch = [
        pltpu.VMEM((rows, D), BF),
        pltpu.VMEM((2, rows, 640), BF),
        pltpu.VMEM((rows, 640), BF),
        pltpu.VMEM((rows, D), BF),
        pltpu.VMEM((D, 640), F32),
        pltpu.VMEM((640, D), F32),
        pltpu.VMEM((96, 640), F32),
    ]
    return call(feed_grads_body, [((16, 96, 640), BF)] * 2, 6.5, 20, scratch, smem=1)(
        info, *seconds, *dgus, *hiddens, *lows, after=after
    )


def attend_grads_body(*refs):
    info = refs[0]
    mines, aheads = refs[1:5], refs[5:9]
    dc_one, dc_two, keep_out, give_out, lhs, mine, acc, group = refs[9:]
    side, z = info[0], info[1]
    for k in range(4):
        rows = slice(k * ROWS, (k + 1) * ROWS)
        for h in range(2):
            mine[h, rows, :] = mines[k][:, h * 320 : (h + 1) * 320].astype(F32).astype(BF)
        lhs[0, rows, :] = aheads[k][:, :D]
        lhs[1, rows, :] = aheads[k][:, QP:]
    group[60:, :] = jnp.zeros((4, 384), F32)
    for turn, out in ((0, keep_out), (1, give_out)):
        h = side if turn == 0 else 1 - side
        which = jnp.where(z + h >= 3, 1, 0)
        acc[:, :320] = dot(lhs[which], mine[h], TN)
        gain_row = jnp.where(h == 0, dc_one[...], dc_two[...])
        first = lax.broadcasted_iota(jnp.int32, (8, D), 0) == 0
        spread = jnp.where(first, jnp.broadcast_to(gain_row, (8, D)), 0.0)
        acc[:, 320:] = dot(spread, jnp.ones((8, 64), F32), TN)
        for c in range(16):
            group[:60, :] = acc[60 * c : 60 * c + 60, :]
            out[slot_of(info, c, turn)] = group[...].astype(BF)


def attend_grads(info, mines, aheads, dc_one, dc_two, after=()):
    rows = 4 * ROWS
    scratch = [
        pltpu.VMEM((2, rows, D), BF),
        pltpu.VMEM((2, rows, 320), BF),
        pltpu.VMEM((D, 384), F32),
        pltpu.VMEM((64, 384), F32),
    ]
    return call(attend_grads_body, [((16, 64, 384), BF)] * 2, 3.0, 16, scratch, smem=1)(
        info, *mines, *aheads, dc_one, dc_two, after=after
    )


def finish_body(info, p0, p1, p2, p3, *outs):
    n1, gq, gk, gv, go, n2, gate, up = outs[:8]
    placed = outs[8]
    z = info[1]
    for k, piece in enumerate((p0, p1, p2, p3)):
        placed[(z + 4 - k) % 4] = piece[...]
    att = []
    for place in range(4):
        gate[:, 0, place * 640 : (place + 1) * 640] = placed[place, :, :640]
        up[:, 0, place * 640 : (place + 1) * 640] = placed[place, :, 1024:1664]
        att += [placed[place, :, 640:960], placed[place, :, 1664:1984]]
    gq[:, 0, :] = jnp.concatenate(att[:3], axis=1)
    go[:, 0, :] = jnp.concatenate(att[5:], axis=1)
    both = jnp.concatenate(att[3:5], axis=1)
    gk[:, 0, :] = jnp.concatenate([both[:, g * 128 : g * 128 + 64] for g in range(KV_HEADS)], axis=1)
    gv[:, 0, :] = jnp.concatenate([both[:, g * 128 + 64 : g * 128 + 128] for g in range(KV_HEADS)], axis=1)
    total = placed[0] + placed[1] + placed[2] + placed[3]
    n1[...] = total[:, 960:1024]
    n2[...] = total[:, 1984:2048]


def finish(info, pieces):
    widths = [D, KW, KW, D, FF, FF]
    shapes = [(15, 1, width) for width in widths]
    shapes = [(15, 64)] + shapes[:4] + [(15, 64)] + shapes[4:]
    return call(
        finish_body, [(s, F32) for s in shapes], 1.5, 8, [pltpu.VMEM((4, 15, 2048), F32)], smem=1
    )(info, *pieces)


def z_shift(value, steps):
    return lax.ppermute(value, "wsh", [(i, (i + steps) % 4) for i in range(4)])


def ctx_shift(value, steps, core_along_x):
    pairs = []
    for core in range(2):
        for y in range(4):
            for x in range(4):
                to = (y, (x + steps) % 4) if core == core_along_x else ((y + steps) % 4, x)
                pairs.append((core * 16 + y * 4 + x, core * 16 + to[0] * 4 + to[1]))
    return lax.ppermute(value, ("section", "ctx"), pairs)


def gather_shift(value, steps):
    return ctx_shift(value, steps, 0)


def reduce_shift(value, steps):
    return ctx_shift(value, steps, 1)


def swap(value):
    return lax.ppermute(value, "section", [(0, 1), (1, 0)])


def add(first, *others):
    total = first.astype(F32)
    for other in others:
        total = total + other.astype(F32)
    return total


def in_order(pieces, rank):
    stacked = jnp.stack(pieces)
    return [lax.dynamic_index_in_dim(stacked, (rank - z) % 4, 0, False) for z in range(4)]


def shards(
    tokens, cotangent, block_order, norm_one, w_query, w_key, w_value, w_out, norm_two, w_gate, w_up, w_down
):
    section = lax.axis_index("section")
    rank = lax.axis_index("ctx")
    z_rank = lax.axis_index("wsh")
    first_core = section == 0
    quarter = FF // 4

    def both(value):
        other = swap(value)
        return jnp.where(first_core, value, other), jnp.where(first_core, other, value)

    key_value = jnp.concatenate(
        [w_key[0].reshape(-1, KV_HEADS, HEAD), w_value[0].reshape(-1, KV_HEADS, HEAD)], axis=2
    ).reshape(-1, 2 * KW)
    shard_rows = w_query.shape[1]
    low_half = jnp.concatenate([w_query[0][:, :HALF], w_out[0][:, : D // 2]], axis=1)
    high_half = jnp.concatenate(
        [
            w_query[0][:, HALF:],
            jnp.zeros((shard_rows, HEAD), BF),
            key_value,
            jnp.zeros((shard_rows, 128), BF),
            w_out[0][:, D // 2 :],
        ],
        axis=1,
    )
    got = swap(jnp.where(first_core, high_half, low_half))
    layer_half = (jnp.where(first_core, low_half, got), jnp.where(first_core, got, high_half))

    gains = jnp.stack([norm_one[0], norm_two[0]])
    gain_parts = [gains] + [z_shift(gains, k) for k in (1, 2, 3)]
    gains = jnp.concatenate(in_order(gain_parts, z_rank), axis=1)
    gain_pair = [g.astype(F32) for g in both(gains)]

    given = swap(jnp.where(first_core, w_up[0], w_gate[0]))
    kind = (jnp.where(first_core, w_gate[0], given), jnp.where(first_core, given, w_up[0]))

    wd = both(w_down[0])

    def none_of(mark):
        return (mark != mark).astype(jnp.int32)

    def columns(z):
        start = z * quarter
        return jnp.concatenate(
            [lax.dynamic_slice_in_dim(k, start, quarter, 1) for k in kind], axis=1
        )

    feed_columns = [columns((z_rank + k) % 4) for k in range(4)]

    def send_feed_weights(mark):
        sent = hold(feed_columns[1:], mark)
        return feed_columns[:1] + [z_shift(sent[k - 1], k) for k in (1, 2, 3)]

    def join_feed_weights(parts, mark):
        later = none_of(mark)
        ordered = jnp.concatenate(in_order(parts, z_rank + later), axis=0)
        other = swap(ordered)
        return [(ordered[:, layer * quarter : (layer + 1) * quarter], other) for layer in range(2)]

    own = lax.dynamic_slice_in_dim(block_order, 2 * rank, 2, 0)
    pairs = block_order.reshape(4, 4, 2)
    y, x = rank // 4, rank % 4
    step = jnp.arange(4, dtype=jnp.int32)

    def by_core(table):
        return jnp.where(first_core, table, jnp.swapaxes(table, 0, 1))

    came = by_core(pairs[(y - step) % 4][:, (x - step) % 4]).reshape(32)
    goes = by_core(pairs[(y + step) % 4][:, (x + step) % 4]).reshape(32)
    ahead_y = ((step - y) % 4)[:, None]
    ahead_x = ((step - x) % 4)[None, :]
    slot = jnp.where(first_core, ahead_y * 4 + ahead_x, ahead_x * 4 + ahead_y).reshape(16)
    info = jnp.concatenate([jnp.stack([section, z_rank]), own, came, goes, slot]).astype(jnp.int32)
    offsets = jnp.arange(BLK, dtype=jnp.int32)
    local_pos = (own[:, None] * BLK + offsets[None, :]).reshape(ROWS)
    frequency = jnp.exp(
        jnp.arange(HEAD // 2).astype(F32) * (-2.0 * math.log(ROPE_BASE) / HEAD)
    )
    angle = local_pos.astype(F32)[:, None] * frequency[None, :]
    cos32, sin32 = jnp.cos(angle), jnp.sin(angle)
    cosine = jnp.concatenate([cos32] * 4, axis=1)
    sine = jnp.concatenate([-sin32, sin32, -sin32, sin32], axis=1)

    own_tokens = lax.dynamic_index_in_dim(tokens, section, 0, False)[0]
    own_cotangent = lax.dynamic_index_in_dim(cotangent, section, 0, False)[0]

    def z_gather(value):
        return [value] + [z_shift(value, k) for k in (1, 2, 3)]

    last_lows = z_gather(own_cotangent.astype(BF))

    def whole(part, *before):
        full = lax.all_gather(part, "wsh", axis=0, tiled=True)
        if before:
            (full,) = hold([full], token(*before))
        return full, swap(full)

    gathered = (
        whole(layer_half[0], info, cosine, sine, own_tokens, *wd, *last_lows[1:], *feed_columns, *gain_pair),
        whole(layer_half[1]),
    )
    saved = []
    base, parts = own_tokens, []
    for layer in range(2):
        gain_one = gain_pair[layer][0:1]
        gain_two = gain_pair[layer][1:2]
        ahead = (saved[0]["normed"], saved[0]["mixed"]) if layer else ()
        x_in, normed, q, kv, *ahead = project(
            info, base, parts, gain_one, gathered[layer], cosine, sine, ahead
        )
        if layer:
            first_aheads = z_gather(ahead[0])
        row = jnp.concatenate([kv] + [gather_shift(kv, k) for k in (1, 2, 3)], axis=0)
        pieces = [row] + [reduce_shift(row, k) for k in (1, 2, 3)]
        if layer == 0:
            sent = send_feed_weights(token(*pieces[1:]))
        mixed, lse, kvs, resid, second = attend(
            info, q, pieces, gathered[layer], x_in, gain_two, after=() if layer else (token(*wd),)
        )
        seconds = z_gather(second)
        if layer == 0:
            wgu = join_feed_weights(sent, seconds[1][0, 0])
        after = (token(*first_aheads[1:]),) if layer else ()
        fed = [feed(layer, info, s, wgu[layer], wd[layer], after) for s in seconds]
        parts = [fed[0][2]] + [z_shift(fed[k][2], -k) for k in (1, 2, 3)]
        base = resid
        saved.append(
            dict(
                x=x_in, q=q, mixed=mixed, lse=lse, kvs=kvs, resid=resid,
                normed=normed,
                seconds=seconds, gu=[f[0] for f in fed], hidden=[f[1] for f in fed],
            )
        )
    outputs = [saved[1]["x"], add(base, *parts)]

    grad = own_cotangent
    lows = last_lows
    input_grads = [None, None]
    feed_halves = [None, None]
    kept = [None, None]

    def stage_one(half):
        cut = [half[4 * k : 4 * k + 4] for k in range(4)]
        return add(cut[0], *[reduce_shift(cut[k], k) for k in (1, 2, 3)])

    def stage_two(stage):
        low = stage.astype(BF)
        return add(stage[0], *[gather_shift(low[k], k) for k in (1, 2, 3)])

    for layer in (1, 0):
        s = saved[layer]
        gain_one = gain_pair[layer][0:1]
        gain_two = gain_pair[layer][1:2]
        back = [feed_back(layer, info, lows[k], s["gu"][k], wgu[layer], wd[layer]) for k in range(4)]
        parts = [back[0][1]] + [z_shift(back[k][1], -k) for k in (1, 2, 3)]
        keep, give = feed_grads(info, s["seconds"], [b[0] for b in back], s["hidden"], lows)
        d_resid, d_low, dc_two, dq, ahead, *goes_out = attend_back(
            info, parts, grad, s["resid"], gain_two, gathered[layer], s["normed"], s["mixed"], s["q"],
            s["lse"], s["kvs"], cosine, sine, after=(token(keep),),
        )
        feed_halves[layer] = add(keep, swap(give)).astype(BF)
        row = add(goes_out[0], *[reduce_shift(goes_out[k], k) for k in (1, 2, 3)])
        row = row.astype(BF).reshape(4, ROWS, 2 * KW)
        own_pieces = [row[0]] + [gather_shift(row[k], k) for k in (1, 2, 3)]
        aheads = z_gather(ahead) if layer else first_aheads
        if layer == 0:
            kept[1] = attention_grads(none_of(d_low[0, 0]))
        cut, grad, dc_one = project_back(
            info, own_pieces, dq, d_resid, d_low, s["x"], gain_one, gathered[layer], cosine, sine,
            after=(token(*aheads[1:]),) if layer else (),
        )
        input_grads[layer] = grad
        if layer:
            lows = z_gather(grad.astype(BF))

        def attention_grads(later, after=(), cut=cut, aheads=aheads, dc_one=dc_one, dc_two=dc_two):
            mines = [lax.dynamic_index_in_dim(cut, k + later, 0, False) for k in range(4)]
            mines = [mines[0]] + [z_shift(mines[k], k) for k in (1, 2, 3)]
            keep, give = attend_grads(info, mines, aheads, dc_one, dc_two, after)
            return add(keep, swap(give)).astype(BF)

        if layer == 0:
            feed_stage = stage_one(jnp.concatenate(hold(feed_halves, token(cut)), axis=1))
            kept[0] = attention_grads(0, (token(feed_stage),))
    attend_stage = stage_one(jnp.concatenate(kept, axis=2))
    both_sums = stage_two(
        jnp.concatenate(
            [feed_stage[:, :96], feed_stage[:, 96:], jnp.pad(attend_stage, ((0, 0), (0, 32), (0, 0)))],
            axis=2,
        )
    )
    feed_sums = (both_sums[:, :640], both_sums[:, 640:1280])
    attend_sum = both_sums[:64, 1280:]
    sums = [
        jnp.concatenate(
            [feed_sums[layer], jnp.pad(attend_sum[:, layer * 384 : (layer + 1) * 384], ((0, 32), (0, 0)))],
            axis=1,
        )
        for layer in range(2)
    ]

    mine = jnp.where(first_core, sums[0], sums[1])
    other = swap(jnp.where(first_core, sums[1], sums[0]))
    halves = (jnp.where(first_core, mine, other), jnp.where(first_core, other, mine))
    joined = jnp.concatenate([h[:60] for h in halves], axis=1).reshape(4, 15, 2048)
    pieces = [lax.dynamic_index_in_dim(joined, z_rank, 0, False)] + [
        z_shift(lax.dynamic_index_in_dim(joined, (z_rank + k) % 4, 0, False), k) for k in (1, 2, 3)
    ]
    down = jnp.concatenate(
        [
            jnp.concatenate(
                [h[60:80, :640], jnp.concatenate([h[80:90, :320], h[80:90, 320:640]], axis=0)], axis=1
            )
            for h in halves
        ],
        axis=0,
    )
    moves = [(c * 4 + z, (4 * z + c // 4) * 4 + c % 4) for c in range(16) for z in range(4)]
    grad_down = lax.ppermute(down, ("ctx", "wsh"), moves)[None]
    sum_one, gq, gk, gv, go, sum_two, gate, up = finish(info, pieces)
    grad_query, grad_key, grad_value, grad_out, grad_gate, grad_up = (
        jnp.swapaxes(g, 0, 1) for g in (gq, gk, gv, go, gate, up)
    )

    def arranged(pair):
        mine = jnp.where(first_core, pair[0], pair[1])
        other = swap(jnp.where(first_core, pair[1], pair[0]))
        first = jnp.where(first_core, mine, other)
        last = jnp.where(first_core, other, mine)
        return jnp.stack([first, last])[None, :, None]

    return (
        arranged(outputs),
        arranged(input_grads),
        sum_one[:, 0][None],
        grad_query,
        grad_key,
        grad_value,
        grad_out,
        sum_two[:, 0][None],
        grad_gate,
        grad_up,
        grad_down,
    )


def solution(mesh):
    rows = P(None, "wsh", "ctx", None)
    gain = P("section", "wsh")
    weight = P("section", "wsh", None)
    in_specs = (rows, rows, P(), gain, weight, weight, weight, weight, gain, weight, weight, weight)
    result = P("section", None, "wsh", "ctx", None)
    gain_out = P("section", ("ctx", "wsh"))
    weight_out = P("section", ("ctx", "wsh"), None)
    out_specs = (
        result, result, gain_out, weight_out, weight_out, weight_out, weight_out, gain_out,
        weight_out, weight_out, weight_out,
    )
    return jax.shard_map(shards, mesh=mesh, in_specs=in_specs, out_specs=out_specs, check_vma=False)
```

```python
import math
from functools import partial

import jax
import jax.numpy as jnp
from jax import lax
from jax.experimental import pallas as pl
from jax.experimental.pallas import tpu as pltpu
from jax.sharding import PartitionSpec as P

HEADS = 15
KV_HEADS = 5
HEAD = 64
GROUP = HEADS // KV_HEADS
D = 960
FF = 2560
KW = KV_HEADS * HEAD
ROWS = 128
BLK = 64
SEQ = 2048
CHUNK = 256
STEPS = 9
EPS = 1e-05
ROPE_BASE = 10000.0
BF = jnp.bfloat16
F32 = jnp.float32
QP = 1024
HALF = 896
NEG = -1e30
MIB = 1024 * 1024

NN = (((1,), (0,)), ((), ()))
NT = (((1,), (1,)), ((), ()))
TN = (((0,), (0,)), ((), ()))


def dot(left, right, dims=NN):
    return lax.dot_general(left, right, dims, preferred_element_type=F32)


def call(body, outs, micros, mib, scratch=(), smem=0):
    def run(*args, after=()):
        count = len(args)
        in_specs = [
            pl.BlockSpec(memory_space=pltpu.SMEM if i < smem else pltpu.VMEM) for i in range(count)
        ] + [pl.BlockSpec(memory_space=pl.ANY) for _ in after]

        def inner(*refs):
            body(*refs[:count], *refs[count + len(after) :])

        out = pl.pallas_call(
            inner,
            in_specs=in_specs,
            out_specs=[pl.BlockSpec(memory_space=pltpu.VMEM) for _ in outs],
            out_shape=[jax.ShapeDtypeStruct(s, t) for s, t in outs],
            scratch_shapes=list(scratch),
            cost_estimate=pl.CostEstimate(
                flops=int(micros * 1.1e9), bytes_accessed=int(micros * 3.6e6), transcendentals=0
            ),
            compiler_params=pltpu.CompilerParams(vmem_limit_bytes=mib * MIB),
        )(*args, *after)
        return out

    return run


def token(*arrays):
    return jnp.stack([a[(0,) * a.ndim].astype(F32) for a in arrays])


def hold(arrays, mark):
    count = len(arrays)

    def body(*refs):
        del refs

    return pl.pallas_call(
        body,
        in_specs=[pl.BlockSpec(memory_space=pl.ANY)] * (count + 1),
        out_specs=[pl.BlockSpec(memory_space=pl.ANY)] * count,
        out_shape=[jax.ShapeDtypeStruct(a.shape, a.dtype) for a in arrays],
        input_output_aliases={i: i for i in range(count)},
    )(*arrays, mark)


def lane(shape):
    return lax.broadcasted_iota(jnp.int32, shape, 1)


def normalise(x, gain):
    return x * lax.rsqrt(jnp.mean(x * x, axis=-1, keepdims=True) + EPS) * gain


def norm_back(x, gain, dy):
    r = lax.rsqrt(jnp.mean(x * x, axis=-1, keepdims=True) + EPS)
    cdy = gain * dy
    dx = r * cdy - x * (r * r * r) * jnp.mean(x * cdy, axis=-1, keepdims=True)
    dc = jnp.sum(dy * x * r, axis=0, keepdims=True)
    return dx, dc


def spin(tile, cosine, sine):
    first = (lane(tile.shape) % HEAD) < HEAD // 2
    swapped = jnp.where(first, pltpu.roll(tile, 96, 1), pltpu.roll(tile, 32, 1))
    return tile * cosine + swapped * sine


def project_body(count):
    def body(*refs):
        info, base = refs[:2]
        parts = refs[2 : 2 + count]
        gain, own, other, cosine, sine = refs[2 + count : 7 + count]
        if count:
            ahead_in = refs[7 + count : 10 + count]
            x_out, normed_out, q_out, kv_out, ahead_out, halves = refs[10 + count :]
            ahead_out[...] = jnp.zeros((ROWS, 2 * QP + D), BF)
            for i in range(3):
                ahead_out[:, i * QP : i * QP + D] = ahead_in[i][...]
        else:
            x_out, normed_out, q_out, kv_out, halves = refs[7:]
        side = info[0]
        x = base[...]
        for part in parts:
            x = x + part[...].astype(F32)
        x_out[...] = x
        normed = normalise(x, gain[...]).astype(BF)
        normed_out[...] = normed
        cos, sin = cosine[...], sine[...]
        halves[side] = dot(normed, own[:, :HALF])
        halves[1 - side] = dot(normed, other[:, :HALF])
        for j in range(8):
            tile = halves[0, :, j * 128 : (j + 1) * 128] if j < 7 else halves[1, :, 0:128]
            q_out[:, j * 128 : (j + 1) * 128] = (spin(tile, cos, sin) * (HEAD**-0.5)).astype(BF)
        for g in range(KV_HEADS):
            tile = halves[1, :, (g + 1) * 128 : (g + 2) * 128]
            tile = jnp.where(lane(tile.shape) < HEAD, spin(tile, cos, sin), tile)
            kv_out[:, g * 128 : (g + 1) * 128] = tile.astype(BF)

    return body


def project(info, base, parts, gain, weight, cosine, sine, ahead=()):
    outs = [((ROWS, D), F32), ((ROWS, D), BF), ((ROWS, QP), BF), ((ROWS, 2 * KW), BF)]
    if ahead:
        outs.append(((ROWS, 2 * QP + D), BF))
    scratch = [pltpu.VMEM((2, ROWS, HALF), F32)]
    return call(project_body(len(parts)), outs, 2.5, 16, scratch, smem=1)(
        info, base, *parts, gain, *weight, cosine, sine, *ahead
    )


def step_place(info, t):
    first, second = info[2], info[3]
    count = first // 4 + 1
    early = t < count
    block = jnp.where(early, 0, 1)
    chunk = jnp.where(early, t, t - count)
    place = jnp.where(early, first, second)
    return block, chunk, place


def causal(place, chunk):
    rows = lax.broadcasted_iota(jnp.int32, (BLK, CHUNK), 0) + place * BLK
    cols = lax.broadcasted_iota(jnp.int32, (BLK, CHUNK), 1) + chunk * CHUNK
    one = rows >= cols
    return jnp.concatenate([one] * GROUP, axis=0)


def head_tile(ref, block, head, upper):
    j = head // 2
    tile = ref[block * BLK : (block + 1) * BLK, j * 128 : (j + 1) * 128].astype(F32)
    if (head % 2 == 1) != upper:
        tile = pltpu.roll(tile, 64, 1)
    keep = (lane(tile.shape) >= HEAD) if upper else (lane(tile.shape) < HEAD)
    return jnp.where(keep, tile, 0.0)


def attend_body(count):
    def body(*refs):
        info, q_ref = refs[0], refs[1]
        pieces = refs[2 : 2 + count]
        (own, other, x_ref, gain, mixed_out, lse_out, kvs, resid_out, second_out) = refs[
            2 + count : 11 + count
        ]
        qh, top, total, acc, halves = refs[11 + count :]
        side = info[0]
        number = 0
        for piece in pieces:
            for b in range(piece.shape[0] // BLK):
                at = pl.multiple_of(info[4 + number] * BLK, BLK)
                kvs[pl.ds(at, BLK), :] = piece[b * BLK : (b + 1) * BLK, :]
                number += 1
        for i in range(2):
            for g in range(KV_HEADS):
                for r in range(GROUP):
                    qh[i, g, r * BLK : (r + 1) * BLK, :] = head_tile(
                        q_ref, i, g * GROUP + r, False
                    ).astype(BF)
        top[...] = jnp.full(top.shape, NEG, F32)
        total[...] = jnp.zeros(total.shape, F32)
        acc[...] = jnp.zeros(acc.shape, F32)

        def step(t, carry):
            block, chunk, place = step_place(info, t)
            allowed = causal(place, chunk)
            at = pl.multiple_of(chunk * CHUNK, CHUNK)
            for g in range(KV_HEADS):
                keys = kvs[pl.ds(at, CHUNK), g * 128 : (g + 1) * 128]
                scores = dot(qh[block, g], keys, NT)
                scores = jnp.where(allowed, scores, NEG)
                old = top[block, g]
                new = jnp.maximum(old, jnp.max(scores, axis=1, keepdims=True))
                probs = jnp.exp(scores - jnp.concatenate([new, new], axis=1))
                shrink = jnp.exp(old - new)
                top[block, g] = new
                total[block, g] = shrink * total[block, g] + jnp.sum(probs, axis=1, keepdims=True)
                acc[block, g] = shrink * acc[block, g] + dot(probs.astype(BF), keys)
            return carry

        lax.fori_loop(0, STEPS, step, 0)
        for i in range(2):
            heads = []
            for g in range(KV_HEADS):
                sums = total[i, g]
                result = acc[i, g] / sums
                lse_out[i, g] = top[i, g] + jnp.log(sums)
                for r in range(GROUP):
                    heads.append(result[r * BLK : (r + 1) * BLK, :])
            for j in range(8):
                low = pltpu.roll(heads[2 * j], 64, 1)
                rows = slice(i * BLK, (i + 1) * BLK)
                if j < 7:
                    tile = jnp.where(lane(low.shape) < HEAD, low, heads[2 * j + 1])
                    mixed_out[rows, j * 128 : (j + 1) * 128] = tile.astype(BF)
                else:
                    mixed_out[rows, 896:960] = low[:, :64].astype(BF)
        halves[side] = dot(mixed_out[...], own[:, HALF:])
        halves[1 - side] = dot(mixed_out[...], other[:, HALF:])
        resid = x_ref[...] + jnp.concatenate([halves[0], halves[1]], axis=1)
        resid_out[...] = resid
        second_out[...] = normalise(resid, gain[...]).astype(BF)

    return body


def attend(info, q, pieces, wo, x, gain, after=()):
    outs = [
        ((ROWS, D), BF),
        ((2, KV_HEADS, GROUP * BLK, 128), F32),
        ((SEQ, 2 * KW), BF),
        ((ROWS, D), F32),
        ((ROWS, D), BF),
    ]
    shape = (2, KV_HEADS, GROUP * BLK, 128)
    scratch = [pltpu.VMEM(shape, BF)] + [pltpu.VMEM(shape, F32)] * 3
    scratch.append(pltpu.VMEM((2, ROWS, D // 2), F32))
    return call(attend_body(len(pieces)), outs, 12.0, 18, scratch, smem=1)(
        info, q, *pieces, *wo, x, gain, after=after
    )


def feed_body(layer, info, second, own, other, wd, gu_out, hidden_out, part_out):
    side = info[0]
    columns = slice(layer * FF // 4, (layer + 1) * FF // 4)
    gu_out[side] = dot(second[...], own[...])
    gu_out[1 - side] = dot(second[...], other[:, columns])
    gate, up = gu_out[0], gu_out[1]
    hidden = (gate / (1.0 + jnp.exp(-gate)) * up).astype(BF)
    hidden_out[...] = hidden
    part_out[...] = dot(hidden, wd[...]).astype(BF)


def feed(layer, info, second, wgu, wd):
    outs = [((2, ROWS, FF // 4), F32), ((ROWS, FF // 4), BF), ((ROWS, D), BF)]
    body = partial(feed_body, layer)
    return call(body, outs, 1.0, 12, smem=1)(info, second, *wgu, wd)


def feed_back_body(layer, info, grad_low, gu, own, other, wd, dgu_out, part_out):
    side = info[0]
    columns = slice(layer * FF // 4, (layer + 1) * FF // 4)
    d_hidden = dot(grad_low[...], wd[...], NT)
    gate, up = gu[0], gu[1]
    sig = 1.0 / (1.0 + jnp.exp(-gate))
    d_gate = d_hidden * up * sig * (1.0 + gate * (1.0 - sig))
    d_up = d_hidden * gate * sig
    dgu_out[0] = d_gate.astype(BF)
    dgu_out[1] = d_up.astype(BF)
    part = dot(dgu_out[side], own[...], NT) + dot(dgu_out[1 - side], other[:, columns], NT)
    part_out[...] = part.astype(BF)


def feed_back(layer, info, grad_low, gu, wgu, wd):
    outs = [((2, ROWS, FF // 4), BF), ((ROWS, D), BF)]
    body = partial(feed_back_body, layer)
    return call(body, outs, 1.3, 12, smem=1)(info, grad_low, gu, *wgu, wd)


def attend_back_body(
    info, p0, p1, p2, p3, grad, resid, gain, own, other, normed, mixed, q_ref, lse, kvs, cosine, sine,
    d_resid_out, d_low_out, dc_out, dq_out, ahead_out, o0, o1, o2, o3,
    qd, delta, dq, dkv, dm, mx, halves,
):
    d_second = p0[...].astype(F32) + p1[...].astype(F32) + p2[...].astype(F32) + p3[...].astype(F32)
    dx, dc = norm_back(resid[...], gain[...], d_second)
    dc_out[...] = dc
    d_resid = grad[...] + dx
    d_resid_out[...] = d_resid
    low = d_resid.astype(BF)
    d_low_out[...] = low
    side = info[0]
    halves[0] = d_resid[:, : D // 2].astype(BF)
    halves[1] = d_resid[:, D // 2 :].astype(BF)
    d_mixed = dot(halves[side], own[:, HALF:], NT) + dot(halves[1 - side], other[:, HALF:], NT)
    ahead_out[:, :D] = normed[...]
    ahead_out[:, QP : QP + D] = mixed[...]
    ahead_out[:, D:QP] = jnp.zeros((ROWS, QP - D), BF)
    dm[:, :D] = d_mixed.astype(BF)
    dm[:, D:] = jnp.zeros((ROWS, QP - D), BF)
    mx[:, :D] = mixed[...]
    mx[:, D:] = jnp.zeros((ROWS, QP - D), BF)
    span = GROUP * BLK
    for i in range(2):
        for g in range(KV_HEADS):
            for r in range(GROUP):
                head = g * GROUP + r
                there = slice(r * BLK, (r + 1) * BLK)
                qd[i, g, there, :] = head_tile(q_ref, i, head, False).astype(BF)
                do = head_tile(dm, i, head, True)
                qd[i, g, span + r * BLK : span + (r + 1) * BLK, :] = do.astype(BF)
                dots = jnp.sum(do * head_tile(mx, i, head, True), axis=1, keepdims=True)
                delta[i, g, there, :] = jnp.broadcast_to(dots, (BLK, 128))
    dq[...] = jnp.zeros(dq.shape, F32)
    dkv[...] = jnp.zeros(dkv.shape, F32)

    def step(t, carry):
        block, chunk, place = step_place(info, t)
        allowed = causal(place, chunk)
        at = pl.multiple_of(chunk * CHUNK, CHUNK)
        for g in range(KV_HEADS):
            keys = kvs[pl.ds(at, CHUNK), g * 128 : (g + 1) * 128]
            both = dot(qd[block, g], keys, NT)
            scores, d_probs = both[:span], both[span:]
            total = lse[block, g]
            probs = jnp.exp(
                jnp.where(allowed, scores, NEG) - jnp.concatenate([total, total], axis=1)
            )
            shift = delta[block, g]
            d_scores = probs * (d_probs - jnp.concatenate([shift, shift], axis=1))
            d_low = d_scores.astype(BF)
            dq[block, g] += dot(d_low, keys)
            stacked = jnp.concatenate([d_low, probs.astype(BF)], axis=0)
            dkv[pl.ds(at, CHUNK), g * 128 : (g + 1) * 128] += dot(stacked, qd[block, g], TN)
        return carry

    lax.fori_loop(0, STEPS, step, 0)
    for i in range(2):
        rows = slice(i * BLK, (i + 1) * BLK)
        cos, sin = cosine[rows, :], sine[rows, :]
        heads = []
        for g in range(KV_HEADS):
            for r in range(GROUP):
                heads.append(dq[i, g, r * BLK : (r + 1) * BLK, :] * (HEAD**-0.5))
        for j in range(8):
            if j < 7:
                high = pltpu.roll(heads[2 * j + 1], 64, 1)
                tile = jnp.where(lane(high.shape) < HEAD, heads[2 * j], high)
                dq_out[rows, j * 128 : (j + 1) * 128] = spin(tile, cos, -sin).astype(BF)
            else:
                dq_out[rows, 896:960] = spin(heads[14], cos, -sin)[:, :64].astype(BF)
    number = 0
    for out in (o0, o1, o2, o3):
        for b in range(out.shape[0] // BLK):
            at = pl.multiple_of(info[36 + number] * BLK, BLK)
            out[b * BLK : (b + 1) * BLK, :] = dkv[pl.ds(at, BLK), :].astype(BF)
            number += 1


def attend_back(info, parts, grad, resid, gain, wo, normed, mixed, q, lse, kvs, cosine, sine, after=()):
    outs = [
        ((ROWS, D), F32),
        ((ROWS, D), BF),
        ((1, D), F32),
        ((ROWS, D), BF),
        ((ROWS, QP + D), BF),
    ] + [((4 * ROWS, 2 * KW), BF)] * 4
    shape = (2, KV_HEADS, GROUP * BLK, 128)
    scratch = [
        pltpu.VMEM((2, KV_HEADS, 2 * GROUP * BLK, 128), BF),
        pltpu.VMEM(shape, F32),
        pltpu.VMEM(shape, F32),
        pltpu.VMEM((SEQ, 2 * KW), F32),
        pltpu.VMEM((ROWS, QP), BF),
        pltpu.VMEM((ROWS, QP), BF),
        pltpu.VMEM((2, ROWS, D // 2), BF),
    ]
    return call(attend_back_body, outs, 24.0, 22, scratch, smem=1)(
        info, *parts, grad, resid, gain, *wo, normed, mixed, q, lse, kvs, cosine, sine, after=after
    )


def project_back_body(
    info, k0, k1, k2, k3, dq, d_resid, d_low, x_ref, gain, own, other, cosine, sine,
    cut_out, grad_out, dc_out, halves, dkv,
):
    side, z = info[0], info[1]
    sums = k0[...].astype(F32) + k1[...].astype(F32) + k2[...].astype(F32) + k3[...].astype(F32)
    cos, sin = cosine[...], -sine[...]
    halves[0] = dq[:, :HALF]
    halves[1] = jnp.zeros((ROWS, HALF), BF)
    halves[1, :, :HEAD] = dq[:, HALF:]
    for g in range(KV_HEADS):
        tile = sums[:, g * 128 : (g + 1) * 128]
        tile = jnp.where(lane(tile.shape) < HEAD, spin(tile, cos, sin), tile)
        dkv[:, g * 128 : (g + 1) * 128] = tile
        halves[1, :, (g + 1) * 128 : (g + 2) * 128] = tile.astype(BF)
    d_normed = dot(halves[side], own[:, :HALF], NT) + dot(halves[1 - side], other[:, :HALF], NT)
    dx, dc = norm_back(x_ref[...], gain[...], d_normed)
    dc_out[...] = dc
    grad_out[...] = d_resid[...] + dx
    query, low = dq[...].astype(F32), d_low[...].astype(F32)
    quarters = (
        query[:, :640],
        jnp.concatenate([query[:, 640:], dkv[:, :320]], axis=1),
        jnp.concatenate([dkv[:, 320:], low[:, :320]], axis=1),
        low[:, 320:],
    )
    for place in range(4):
        cut_out[(place + 4 - z) % 4] = quarters[place].astype(BF)


def project_back(info, pieces, dq, d_resid, d_low, x, gain, weight, cosine, sine, after=()):
    outs = [((4, ROWS, 640), BF), ((ROWS, D), F32), ((1, D), F32)]
    scratch = [pltpu.VMEM((2, ROWS, HALF), BF), pltpu.VMEM((ROWS, 2 * KW), F32)]
    return call(project_back_body, outs, 3.2, 16, scratch, smem=1)(
        info, *pieces, dq, d_resid, d_low, x, gain, *weight, cosine, sine, after=after
    )


def slot_of(info, c, given):
    place = info[68 + c]
    return (place % 4) * 4 + place // 4 if given else place


def feed_grads_body(*refs):
    info = refs[0]
    seconds, dgus, hiddens, lows = (refs[1 + 4 * i : 5 + 4 * i] for i in range(4))
    keep_out, give_out, left, right, hidden, low, acc, down, group = refs[17:]
    side = info[0]
    for k in range(4):
        rows = slice(k * ROWS, (k + 1) * ROWS)
        left[rows, :] = seconds[k][...]
        hidden[rows, :] = hiddens[k][...]
        low[rows, :] = lows[k][...]
        for h in range(2):
            right[h, rows, :] = dgus[k][h]
    down[...] = dot(hidden[...], low[...], TN)
    group[90:, :] = jnp.zeros((6, 640), F32)
    for turn, out in ((0, keep_out), (1, give_out)):
        half = side if turn == 0 else 1 - side
        acc[...] = dot(left[...], right[half], TN)
        for h in range(2):

            @pl.when(half == h)
            def _():
                for c in range(16):
                    at = 40 * c + 20 * h
                    group[:60, :] = acc[60 * c : 60 * c + 60, :]
                    group[60:80, :] = down[at : at + 20, :640]
                    group[80:90, :320] = down[at : at + 10, 640:]
                    group[80:90, 320:] = down[at + 10 : at + 20, 640:]
                    out[slot_of(info, c, turn)] = group[...].astype(BF)


def feed_grads(info, seconds, dgus, hiddens, lows, after=()):
    rows = 4 * ROWS
    scratch = [
        pltpu.VMEM((rows, D), BF),
        pltpu.VMEM((2, rows, 640), BF),
        pltpu.VMEM((rows, 640), BF),
        pltpu.VMEM((rows, D), BF),
        pltpu.VMEM((D, 640), F32),
        pltpu.VMEM((640, D), F32),
        pltpu.VMEM((96, 640), F32),
    ]
    return call(feed_grads_body, [((16, 96, 640), BF)] * 2, 6.5, 20, scratch, smem=1)(
        info, *seconds, *dgus, *hiddens, *lows, after=after
    )


def attend_grads_body(*refs):
    info = refs[0]
    mines, ahead = refs[1:5], refs[5]
    dc_one, dc_two, keep_out, give_out, lhs, mine, acc, group = refs[6:]
    side, z = info[0], info[1]
    for k in range(4):
        rows = slice(k * ROWS, (k + 1) * ROWS)
        for h in range(2):
            mine[h, rows, :] = mines[k][:, h * 320 : (h + 1) * 320].astype(F32).astype(BF)
        lhs[0, rows, :] = ahead[(z + 4 - k) % 4, :, :D]
        lhs[1, rows, :] = ahead[(z + 4 - k) % 4, :, QP : QP + D]
    group[60:, :] = jnp.zeros((4, 384), F32)
    for turn, out in ((0, keep_out), (1, give_out)):
        h = side if turn == 0 else 1 - side
        which = jnp.where(z + h >= 3, 1, 0)
        acc[:, :320] = dot(lhs[which], mine[h], TN)
        gain_row = jnp.where(h == 0, dc_one[...], dc_two[...])
        first = lax.broadcasted_iota(jnp.int32, (8, D), 0) == 0
        spread = jnp.where(first, jnp.broadcast_to(gain_row, (8, D)), 0.0)
        acc[:, 320:] = dot(spread, jnp.ones((8, 64), F32), TN)
        for c in range(16):
            group[:60, :] = acc[60 * c : 60 * c + 60, :]
            out[slot_of(info, c, turn)] = group[...].astype(BF)


def attend_grads(info, mines, ahead, dc_one, dc_two, after=()):
    rows = 4 * ROWS
    scratch = [
        pltpu.VMEM((2, rows, D), BF),
        pltpu.VMEM((2, rows, 320), BF),
        pltpu.VMEM((D, 384), F32),
        pltpu.VMEM((64, 384), F32),
    ]
    return call(attend_grads_body, [((16, 64, 384), BF)] * 2, 3.0, 16, scratch, smem=1)(
        info, *mines, ahead, dc_one, dc_two, after=after
    )


def finish_body(info, p0, p1, p2, p3, *outs):
    n1, gq, gk, gv, go, n2, gate, up = outs[:8]
    placed = outs[8]
    z = info[1]
    for k, piece in enumerate((p0, p1, p2, p3)):
        placed[(z + 4 - k) % 4] = piece[...]
    att = []
    for place in range(4):
        gate[:, 0, place * 640 : (place + 1) * 640] = placed[place, :, :640]
        up[:, 0, place * 640 : (place + 1) * 640] = placed[place, :, 1024:1664]
        att += [placed[place, :, 640:960], placed[place, :, 1664:1984]]
    gq[:, 0, :] = jnp.concatenate(att[:3], axis=1)
    go[:, 0, :] = jnp.concatenate(att[5:], axis=1)
    both = jnp.concatenate(att[3:5], axis=1)
    gk[:, 0, :] = jnp.concatenate([both[:, g * 128 : g * 128 + 64] for g in range(KV_HEADS)], axis=1)
    gv[:, 0, :] = jnp.concatenate([both[:, g * 128 + 64 : g * 128 + 128] for g in range(KV_HEADS)], axis=1)
    total = placed[0] + placed[1] + placed[2] + placed[3]
    n1[...] = total[:, 960:1024]
    n2[...] = total[:, 1984:2048]


def finish(info, pieces):
    widths = [D, KW, KW, D, FF, FF]
    shapes = [(15, 1, width) for width in widths]
    shapes = [(15, 64)] + shapes[:4] + [(15, 64)] + shapes[4:]
    return call(
        finish_body, [(s, F32) for s in shapes], 1.5, 8, [pltpu.VMEM((4, 15, 2048), F32)], smem=1
    )(info, *pieces)


def z_shift(value, steps):
    return lax.ppermute(value, "wsh", [(i, (i + steps) % 4) for i in range(4)])


def ctx_shift(value, steps, core_along_x):
    pairs = []
    for core in range(2):
        for y in range(4):
            for x in range(4):
                to = (y, (x + steps) % 4) if core == core_along_x else ((y + steps) % 4, x)
                pairs.append((core * 16 + y * 4 + x, core * 16 + to[0] * 4 + to[1]))
    return lax.ppermute(value, ("section", "ctx"), pairs)


def gather_shift(value, steps):
    return ctx_shift(value, steps, 0)


def reduce_shift(value, steps):
    return ctx_shift(value, steps, 1)


def swap(value):
    return lax.ppermute(value, "section", [(0, 1), (1, 0)])


def add(first, *others):
    total = first.astype(F32)
    for other in others:
        total = total + other.astype(F32)
    return total


def in_order(pieces, rank):
    stacked = jnp.stack(pieces)
    return [lax.dynamic_index_in_dim(stacked, (rank - z) % 4, 0, False) for z in range(4)]


def shards(
    tokens, cotangent, block_order, norm_one, w_query, w_key, w_value, w_out, norm_two, w_gate, w_up, w_down
):
    section = lax.axis_index("section")
    rank = lax.axis_index("ctx")
    z_rank = lax.axis_index("wsh")
    first_core = section == 0
    quarter = FF // 4

    def both(value):
        other = swap(value)
        return jnp.where(first_core, value, other), jnp.where(first_core, other, value)

    key_value = jnp.concatenate(
        [w_key[0].reshape(-1, KV_HEADS, HEAD), w_value[0].reshape(-1, KV_HEADS, HEAD)], axis=2
    ).reshape(-1, 2 * KW)
    shard_rows = w_query.shape[1]
    low_half = jnp.concatenate([w_query[0][:, :HALF], w_out[0][:, : D // 2]], axis=1)
    high_half = jnp.concatenate(
        [
            w_query[0][:, HALF:],
            jnp.zeros((shard_rows, HEAD), BF),
            key_value,
            jnp.zeros((shard_rows, 128), BF),
            w_out[0][:, D // 2 :],
        ],
        axis=1,
    )
    got = swap(jnp.where(first_core, high_half, low_half))
    layer_half = (jnp.where(first_core, low_half, got), jnp.where(first_core, got, high_half))

    gains = jnp.stack([norm_one[0], norm_two[0]])
    gain_parts = [gains] + [z_shift(gains, k) for k in (1, 2, 3)]
    gains = jnp.concatenate(in_order(gain_parts, z_rank), axis=1)
    gain_pair = [g.astype(F32) for g in both(gains)]

    given = swap(jnp.where(first_core, w_up[0], w_gate[0]))
    kind = (jnp.where(first_core, w_gate[0], given), jnp.where(first_core, given, w_up[0]))

    def none_of(mark):
        return (mark != mark).astype(jnp.int32)

    def columns(z):
        start = z * quarter
        return jnp.concatenate(
            [lax.dynamic_slice_in_dim(k, start, quarter, 1) for k in kind], axis=1
        )

    feed_columns = [columns((z_rank + k) % 4) for k in range(4)]

    def send_feed_weights(early, late):
        after, before = hold([feed_columns[1], feed_columns[3]], early)
        (across,) = hold([feed_columns[2]], late)
        return [feed_columns[0], z_shift(after, 1), z_shift(across, 2), z_shift(before, 3)]

    def join_feed_weights(parts, mark):
        later = none_of(mark)
        ordered = jnp.concatenate(in_order(parts, z_rank + later), axis=0)
        other = swap(ordered)
        return [(ordered[:, layer * quarter : (layer + 1) * quarter], other) for layer in range(2)]

    own = lax.dynamic_slice_in_dim(block_order, 2 * rank, 2, 0)
    pairs = block_order.reshape(4, 4, 2)
    y, x = rank // 4, rank % 4
    step = jnp.arange(4, dtype=jnp.int32)

    def by_core(table):
        return jnp.where(first_core, table, jnp.swapaxes(table, 0, 1))

    came = by_core(pairs[(y - step) % 4][:, (x - step) % 4]).reshape(32)
    goes = by_core(pairs[(y + step) % 4][:, (x + step) % 4]).reshape(32)
    ahead_y = ((step - y) % 4)[:, None]
    ahead_x = ((step - x) % 4)[None, :]
    slot = jnp.where(first_core, ahead_y * 4 + ahead_x, ahead_x * 4 + ahead_y).reshape(16)
    place = jnp.stack([section, z_rank]).astype(jnp.int32)
    info = jnp.concatenate([place, own, came, goes, slot]).astype(jnp.int32)
    offsets = jnp.arange(BLK, dtype=jnp.int32)
    local_pos = (own[:, None] * BLK + offsets[None, :]).reshape(ROWS)
    frequency = jnp.exp(
        jnp.arange(HEAD // 2).astype(F32) * (-2.0 * math.log(ROPE_BASE) / HEAD)
    )
    angle = local_pos.astype(F32)[:, None] * frequency[None, :]
    cos32, sin32 = jnp.cos(angle), jnp.sin(angle)
    cosine = jnp.concatenate([cos32] * 4, axis=1)
    sine = jnp.concatenate([-sin32, sin32, -sin32, sin32], axis=1)

    own_tokens = lax.dynamic_index_in_dim(tokens, section, 0, False)[0]
    own_cotangent = lax.dynamic_index_in_dim(cotangent, section, 0, False)[0]

    def z_gather(value):
        return [value] + [z_shift(value, k) for k in (1, 2, 3)]

    last_low = own_cotangent.astype(BF)

    def whole(part):
        full = lax.all_gather(part, "wsh", axis=0, tiled=True)
        return full, swap(full)

    gathered = tuple(whole(part) for part in layer_half)
    saved = []
    base, parts = own_tokens, []
    for layer in range(2):
        gain_one = gain_pair[layer][0:1]
        gain_two = gain_pair[layer][1:2]
        ahead = (saved[0]["normed"], saved[0]["mixed"], last_low) if layer else ()
        x_in, normed, q, kv, *ahead = project(
            place, base, parts, gain_one, gathered[layer], cosine, sine, ahead
        )
        if layer:
            first_ahead = lax.all_gather(ahead[0], "wsh")
        row = jnp.concatenate([kv] + [gather_shift(kv, k) for k in (1, 2, 3)], axis=0)
        pieces = [row] + [reduce_shift(row, k) for k in (1, 2, 3)]
        if layer == 0:
            sent = send_feed_weights(token(row), token(pieces[1]))
            wd = both(hold([w_down[0]], token(kv))[0])
        mixed, lse, kvs, resid, second = attend(
            info, q, pieces, gathered[layer], x_in, gain_two, after=() if layer else (token(wd[0]),)
        )
        seconds = z_gather(second)
        if layer == 0:
            wgu = join_feed_weights(sent, second[0, 0])
        fed = [feed(layer, place, s, wgu[layer], wd[layer]) for s in seconds]
        parts = [fed[0][2]] + [z_shift(fed[k][2], -k) for k in (1, 2, 3)]
        base = resid
        saved.append(
            dict(
                x=x_in, q=q, mixed=mixed, lse=lse, kvs=kvs, resid=resid,
                normed=normed,
                seconds=seconds, gu=[f[0] for f in fed], hidden=[f[1] for f in fed],
            )
        )
    outputs = [saved[1]["x"], add(base, *parts)]

    grad = own_cotangent
    lows = [last_low] + [
        lax.dynamic_index_in_dim(first_ahead, (z_rank - k) % 4, 0, False)[:, 2 * QP :] for k in (1, 2, 3)
    ]
    input_grads = [None, None]
    feed_halves = [None, None]
    kept = [None, None]

    def stage_one(half):
        cut = [half[4 * k : 4 * k + 4] for k in range(4)]
        return add(cut[0], *[reduce_shift(cut[k], k) for k in (1, 2, 3)])

    def stage_two(stage):
        low = stage.astype(BF)
        return add(stage[0], *[gather_shift(low[k], k) for k in (1, 2, 3)])

    for layer in (1, 0):
        s = saved[layer]
        gain_one = gain_pair[layer][0:1]
        gain_two = gain_pair[layer][1:2]
        back = [feed_back(layer, place, lows[k], s["gu"][k], wgu[layer], wd[layer]) for k in range(4)]
        parts = [back[0][1]] + [z_shift(back[k][1], -k) for k in (1, 2, 3)]
        keep, give = feed_grads(info, s["seconds"], [b[0] for b in back], s["hidden"], lows)
        d_resid, d_low, dc_two, dq, ahead, *goes_out = attend_back(
            info, parts, grad, s["resid"], gain_two, gathered[layer], s["normed"], s["mixed"], s["q"],
            s["lse"], s["kvs"], cosine, sine, after=(token(keep),),
        )
        feed_halves[layer] = add(keep, swap(give)).astype(BF)
        row = add(goes_out[0], *[reduce_shift(goes_out[k], k) for k in (1, 2, 3)])
        row = row.astype(BF).reshape(4, ROWS, 2 * KW)
        own_pieces = [row[0]] + [gather_shift(row[k], k) for k in (1, 2, 3)]
        ahead = lax.all_gather(ahead, "wsh") if layer else first_ahead
        if layer == 0:
            kept[1] = attention_grads(none_of(d_low[0, 0]))
        cut, grad, dc_one = project_back(
            info, own_pieces, dq, d_resid, d_low, s["x"], gain_one, gathered[layer], cosine, sine,
            after=(token(ahead),) if layer else (),
        )
        input_grads[layer] = grad
        if layer:
            lows = z_gather(grad.astype(BF))

        def attention_grads(later, after=(), cut=cut, ahead=ahead, dc_one=dc_one, dc_two=dc_two):
            mines = [lax.dynamic_index_in_dim(cut, k + later, 0, False) for k in range(4)]
            mines = [mines[0]] + [z_shift(mines[k], k) for k in (1, 2, 3)]
            keep, give = attend_grads(info, mines, ahead, dc_one, dc_two, after)
            return add(keep, swap(give)).astype(BF)

        if layer == 0:
            feed_stage = stage_one(jnp.concatenate(hold(feed_halves, token(row)), axis=1))
            kept[0] = attention_grads(0, (token(feed_stage),))
    attend_stage = stage_one(jnp.concatenate(kept, axis=2))
    both_sums = stage_two(
        jnp.concatenate(
            [feed_stage[:, :96], feed_stage[:, 96:], jnp.pad(attend_stage, ((0, 0), (0, 32), (0, 0)))],
            axis=2,
        )
    )
    feed_sums = (both_sums[:, :640], both_sums[:, 640:1280])
    attend_sum = both_sums[:64, 1280:]
    sums = [
        jnp.concatenate(
            [feed_sums[layer], jnp.pad(attend_sum[:, layer * 384 : (layer + 1) * 384], ((0, 32), (0, 0)))],
            axis=1,
        )
        for layer in range(2)
    ]

    mine = jnp.where(first_core, sums[0], sums[1])
    other = swap(jnp.where(first_core, sums[1], sums[0]))
    halves = (jnp.where(first_core, mine, other), jnp.where(first_core, other, mine))
    joined = jnp.concatenate([h[:60] for h in halves], axis=1).reshape(4, 15, 2048)
    pieces = [lax.dynamic_index_in_dim(joined, z_rank, 0, False)] + [
        z_shift(lax.dynamic_index_in_dim(joined, (z_rank + k) % 4, 0, False), k) for k in (1, 2, 3)
    ]
    down = jnp.concatenate(
        [
            jnp.concatenate(
                [h[60:80, :640], jnp.concatenate([h[80:90, :320], h[80:90, 320:640]], axis=0)], axis=1
            )
            for h in halves
        ],
        axis=0,
    )
    moves = [(c * 4 + z, (4 * z + c // 4) * 4 + c % 4) for c in range(16) for z in range(4)]
    grad_down = lax.ppermute(down, ("ctx", "wsh"), moves)[None]
    sum_one, gq, gk, gv, go, sum_two, gate, up = finish(info, pieces)
    grad_query, grad_key, grad_value, grad_out, grad_gate, grad_up = (
        jnp.swapaxes(g, 0, 1) for g in (gq, gk, gv, go, gate, up)
    )

    def arranged(pair):
        mine = jnp.where(first_core, pair[0], pair[1])
        other = swap(jnp.where(first_core, pair[1], pair[0]))
        first = jnp.where(first_core, mine, other)
        last = jnp.where(first_core, other, mine)
        return jnp.stack([first, last])[None, :, None]

    return (
        arranged(outputs),
        arranged(input_grads),
        sum_one[:, 0][None],
        grad_query,
        grad_key,
        grad_value,
        grad_out,
        sum_two[:, 0][None],
        grad_gate,
        grad_up,
        grad_down,
    )


def solution(mesh):
    rows = P(None, "wsh", "ctx", None)
    gain = P("section", "wsh")
    weight = P("section", "wsh", None)
    in_specs = (rows, rows, P(), gain, weight, weight, weight, weight, gain, weight, weight, weight)
    result = P("section", None, "wsh", "ctx", None)
    gain_out = P("section", ("ctx", "wsh"))
    weight_out = P("section", ("ctx", "wsh"), None)
    out_specs = (
        result, result, gain_out, weight_out, weight_out, weight_out, weight_out, gain_out,
        weight_out, weight_out, weight_out,
    )
    return jax.shard_map(shards, mesh=mesh, in_specs=in_specs, out_specs=out_specs, check_vma=False)
```

```python
import math
from functools import partial

import jax
import jax.numpy as jnp
from jax import lax
from jax.experimental import pallas as pl
from jax.experimental.pallas import tpu as pltpu
from jax.sharding import PartitionSpec as P

HEADS = 15
KV_HEADS = 5
HEAD = 64
GROUP = HEADS // KV_HEADS
D = 960
FF = 2560
KW = KV_HEADS * HEAD
ROWS = 128
BLK = 64
SEQ = 2048
CHUNK = 256
STEPS = 9
EPS = 1e-05
ROPE_BASE = 10000.0
BF = jnp.bfloat16
F32 = jnp.float32
QP = 1024
HALF = 896
NEG = -1e30
MIB = 1024 * 1024

NN = (((1,), (0,)), ((), ()))
NT = (((1,), (1,)), ((), ()))
TN = (((0,), (0,)), ((), ()))


def dot(left, right, dims=NN):
    return lax.dot_general(left, right, dims, preferred_element_type=F32)


def call(body, outs, micros, mib, scratch=(), smem=0):
    def run(*args, after=()):
        count = len(args)
        in_specs = [
            pl.BlockSpec(memory_space=pltpu.SMEM if i < smem else pltpu.VMEM) for i in range(count)
        ] + [pl.BlockSpec(memory_space=pl.ANY) for _ in after]

        def inner(*refs):
            body(*refs[:count], *refs[count + len(after) :])

        out = pl.pallas_call(
            inner,
            in_specs=in_specs,
            out_specs=[pl.BlockSpec(memory_space=pltpu.VMEM) for _ in outs],
            out_shape=[jax.ShapeDtypeStruct(s, t) for s, t in outs],
            scratch_shapes=list(scratch),
            cost_estimate=pl.CostEstimate(
                flops=int(micros * 1.1e9), bytes_accessed=int(micros * 3.6e6), transcendentals=0
            ),
            compiler_params=pltpu.CompilerParams(vmem_limit_bytes=mib * MIB),
        )(*args, *after)
        return out

    return run


def token(*arrays):
    return jnp.stack([a[(0,) * a.ndim].astype(F32) for a in arrays])


def hold(arrays, mark):
    count = len(arrays)

    def body(*refs):
        del refs

    return pl.pallas_call(
        body,
        in_specs=[pl.BlockSpec(memory_space=pl.ANY)] * (count + 1),
        out_specs=[pl.BlockSpec(memory_space=pl.ANY)] * count,
        out_shape=[jax.ShapeDtypeStruct(a.shape, a.dtype) for a in arrays],
        input_output_aliases={i: i for i in range(count)},
    )(*arrays, mark)


def lane(shape):
    return lax.broadcasted_iota(jnp.int32, shape, 1)


def normalise(x, gain):
    return x * lax.rsqrt(jnp.mean(x * x, axis=-1, keepdims=True) + EPS) * gain


def norm_back(x, gain, dy):
    r = lax.rsqrt(jnp.mean(x * x, axis=-1, keepdims=True) + EPS)
    cdy = gain * dy
    dx = r * cdy - x * (r * r * r) * jnp.mean(x * cdy, axis=-1, keepdims=True)
    dc = jnp.sum(dy * x * r, axis=0, keepdims=True)
    return dx, dc


def spin(tile, cosine, sine):
    first = (lane(tile.shape) % HEAD) < HEAD // 2
    swapped = jnp.where(first, pltpu.roll(tile, 96, 1), pltpu.roll(tile, 32, 1))
    return tile * cosine + swapped * sine


def project_body(count):
    def body(*refs):
        info, base = refs[:2]
        parts = refs[2 : 2 + count]
        gain, own, other, cosine, sine = refs[2 + count : 7 + count]
        if count:
            ahead_in = refs[7 + count : 10 + count]
            x_out, normed_out, q_out, kv_out, ahead_out, halves = refs[10 + count :]
            ahead_out[...] = jnp.zeros((ROWS, 2 * QP + D), BF)
            for i in range(3):
                ahead_out[:, i * QP : i * QP + D] = ahead_in[i][...]
        else:
            x_out, normed_out, q_out, kv_out, halves = refs[7:]
        side = info[0]
        x = base[...]
        for part in parts:
            x = x + part[...].astype(F32)
        x_out[...] = x
        normed = normalise(x, gain[...]).astype(BF)
        normed_out[...] = normed
        cos, sin = cosine[...], sine[...]
        halves[side] = dot(normed, own[:, :HALF])
        halves[1 - side] = dot(normed, other[:, :HALF])
        for j in range(8):
            tile = halves[0, :, j * 128 : (j + 1) * 128] if j < 7 else halves[1, :, 0:128]
            q_out[:, j * 128 : (j + 1) * 128] = (spin(tile, cos, sin) * (HEAD**-0.5)).astype(BF)
        for g in range(KV_HEADS):
            tile = halves[1, :, (g + 1) * 128 : (g + 2) * 128]
            tile = jnp.where(lane(tile.shape) < HEAD, spin(tile, cos, sin), tile)
            kv_out[:, g * 128 : (g + 1) * 128] = tile.astype(BF)

    return body


def project(info, base, parts, gain, weight, cosine, sine, ahead=()):
    outs = [((ROWS, D), F32), ((ROWS, D), BF), ((ROWS, QP), BF), ((ROWS, 2 * KW), BF)]
    if ahead:
        outs.append(((ROWS, 2 * QP + D), BF))
    scratch = [pltpu.VMEM((2, ROWS, HALF), F32)]
    return call(project_body(len(parts)), outs, 2.5, 16, scratch, smem=1)(
        info, base, *parts, gain, *weight, cosine, sine, *ahead
    )


def step_place(info, t):
    first, second = info[2], info[3]
    count = first // 4 + 1
    early = t < count
    block = jnp.where(early, 0, 1)
    chunk = jnp.where(early, t, t - count)
    place = jnp.where(early, first, second)
    return block, chunk, place


def causal(place, chunk):
    rows = lax.broadcasted_iota(jnp.int32, (BLK, CHUNK), 0) + place * BLK
    cols = lax.broadcasted_iota(jnp.int32, (BLK, CHUNK), 1) + chunk * CHUNK
    one = rows >= cols
    return jnp.concatenate([one] * GROUP, axis=0)


def head_tile(ref, block, head, upper):
    j = head // 2
    tile = ref[block * BLK : (block + 1) * BLK, j * 128 : (j + 1) * 128].astype(F32)
    if (head % 2 == 1) != upper:
        tile = pltpu.roll(tile, 64, 1)
    keep = (lane(tile.shape) >= HEAD) if upper else (lane(tile.shape) < HEAD)
    return jnp.where(keep, tile, 0.0)


def attend_body(count):
    def body(*refs):
        info, q_ref = refs[0], refs[1]
        pieces = refs[2 : 2 + count]
        (own, other, x_ref, gain, mixed_out, lse_out, kvs, resid_out, second_out) = refs[
            2 + count : 11 + count
        ]
        qh, top, total, acc, halves = refs[11 + count :]
        side = info[0]
        number = 0
        for piece in pieces:
            for b in range(piece.shape[0] // BLK):
                at = pl.multiple_of(info[4 + number] * BLK, BLK)
                kvs[pl.ds(at, BLK), :] = piece[b * BLK : (b + 1) * BLK, :]
                number += 1
        for i in range(2):
            for g in range(KV_HEADS):
                for r in range(GROUP):
                    qh[i, g, r * BLK : (r + 1) * BLK, :] = head_tile(
                        q_ref, i, g * GROUP + r, False
                    ).astype(BF)
        top[...] = jnp.full(top.shape, NEG, F32)
        total[...] = jnp.zeros(total.shape, F32)
        acc[...] = jnp.zeros(acc.shape, F32)

        def step(t, carry):
            block, chunk, place = step_place(info, t)
            allowed = causal(place, chunk)
            at = pl.multiple_of(chunk * CHUNK, CHUNK)
            for g in range(KV_HEADS):
                keys = kvs[pl.ds(at, CHUNK), g * 128 : (g + 1) * 128]
                scores = dot(qh[block, g], keys, NT)
                scores = jnp.where(allowed, scores, NEG)
                old = top[block, g]
                new = jnp.maximum(old, jnp.max(scores, axis=1, keepdims=True))
                probs = jnp.exp(scores - jnp.concatenate([new, new], axis=1))
                shrink = jnp.exp(old - new)
                top[block, g] = new
                total[block, g] = shrink * total[block, g] + jnp.sum(probs, axis=1, keepdims=True)
                acc[block, g] = shrink * acc[block, g] + dot(probs.astype(BF), keys)
            return carry

        lax.fori_loop(0, STEPS, step, 0)
        for i in range(2):
            heads = []
            for g in range(KV_HEADS):
                sums = total[i, g]
                result = acc[i, g] / sums
                lse_out[i, g] = top[i, g] + jnp.log(sums)
                for r in range(GROUP):
                    heads.append(result[r * BLK : (r + 1) * BLK, :])
            for j in range(8):
                low = pltpu.roll(heads[2 * j], 64, 1)
                rows = slice(i * BLK, (i + 1) * BLK)
                if j < 7:
                    tile = jnp.where(lane(low.shape) < HEAD, low, heads[2 * j + 1])
                    mixed_out[rows, j * 128 : (j + 1) * 128] = tile.astype(BF)
                else:
                    mixed_out[rows, 896:960] = low[:, :64].astype(BF)
        halves[side] = dot(mixed_out[...], own[:, HALF:])
        halves[1 - side] = dot(mixed_out[...], other[:, HALF:])
        resid = x_ref[...] + jnp.concatenate([halves[0], halves[1]], axis=1)
        resid_out[...] = resid
        second_out[...] = normalise(resid, gain[...]).astype(BF)

    return body


def attend(info, q, pieces, wo, x, gain, after=()):
    outs = [
        ((ROWS, D), BF),
        ((2, KV_HEADS, GROUP * BLK, 128), F32),
        ((SEQ, 2 * KW), BF),
        ((ROWS, D), F32),
        ((ROWS, D), BF),
    ]
    shape = (2, KV_HEADS, GROUP * BLK, 128)
    scratch = [pltpu.VMEM(shape, BF)] + [pltpu.VMEM(shape, F32)] * 3
    scratch.append(pltpu.VMEM((2, ROWS, D // 2), F32))
    return call(attend_body(len(pieces)), outs, 12.0, 18, scratch, smem=1)(
        info, q, *pieces, *wo, x, gain, after=after
    )


def feed_body(layer, info, second, own, other, wd, gu_out, hidden_out, part_out):
    side = info[0]
    columns = slice(layer * FF // 4, (layer + 1) * FF // 4)
    gu_out[side] = dot(second[...], own[...])
    gu_out[1 - side] = dot(second[...], other[:, columns])
    gate, up = gu_out[0], gu_out[1]
    hidden = (gate / (1.0 + jnp.exp(-gate)) * up).astype(BF)
    hidden_out[...] = hidden
    part_out[...] = dot(hidden, wd[...]).astype(BF)


def feed(layer, info, second, wgu, wd):
    outs = [((2, ROWS, FF // 4), F32), ((ROWS, FF // 4), BF), ((ROWS, D), BF)]
    body = partial(feed_body, layer)
    return call(body, outs, 1.0, 12, smem=1)(info, second, *wgu, wd)


def feed_back_body(layer, info, grad_low, gu, own, other, wd, dgu_out, part_out):
    side = info[0]
    columns = slice(layer * FF // 4, (layer + 1) * FF // 4)
    d_hidden = dot(grad_low[...], wd[...], NT)
    gate, up = gu[0], gu[1]
    sig = 1.0 / (1.0 + jnp.exp(-gate))
    d_gate = d_hidden * up * sig * (1.0 + gate * (1.0 - sig))
    d_up = d_hidden * gate * sig
    dgu_out[0] = d_gate.astype(BF)
    dgu_out[1] = d_up.astype(BF)
    part = dot(dgu_out[side], own[...], NT) + dot(dgu_out[1 - side], other[:, columns], NT)
    part_out[...] = part.astype(BF)


def feed_back(layer, info, grad_low, gu, wgu, wd):
    outs = [((2, ROWS, FF // 4), BF), ((ROWS, D), BF)]
    body = partial(feed_back_body, layer)
    return call(body, outs, 1.3, 12, smem=1)(info, grad_low, gu, *wgu, wd)


def feed_both_body(
    layer, info, second, grad_low, own, other, wd, dgu_out, hidden_out, part_out, back_out, gu
):
    feed_body(layer, info, second, own, other, wd, gu, hidden_out, part_out)
    feed_back_body(layer, info, grad_low, gu, own, other, wd, dgu_out, back_out)


def feed_both(layer, info, second, grad_low, wgu, wd):
    half = (2, ROWS, FF // 4)
    outs = [(half, BF), ((ROWS, FF // 4), BF), ((ROWS, D), BF), ((ROWS, D), BF)]
    body = partial(feed_both_body, layer)
    return call(body, outs, 2.5, 12, [pltpu.VMEM(half, F32)], smem=1)(
        info, second, grad_low, *wgu, wd
    )


def attend_back_body(
    info, p0, p1, p2, p3, grad, resid, gain, own, other, normed, mixed, q_ref, lse, kvs, cosine, sine,
    d_resid_out, d_low_out, dc_out, dq_out, ahead_out, o0, o1, o2, o3,
    qd, qd_turned, delta, dq, dkv, placed, dm, mx, halves,
):
    d_second = p0[...].astype(F32) + p1[...].astype(F32) + p2[...].astype(F32) + p3[...].astype(F32)
    dx, dc = norm_back(resid[...], gain[...], d_second)
    dc_out[...] = dc
    d_resid = grad[...] + dx
    d_resid_out[...] = d_resid
    low = d_resid.astype(BF)
    d_low_out[...] = low
    side = info[0]
    halves[0] = d_resid[:, : D // 2].astype(BF)
    halves[1] = d_resid[:, D // 2 :].astype(BF)
    d_mixed = dot(halves[side], own[:, HALF:], NT) + dot(halves[1 - side], other[:, HALF:], NT)
    ahead_out[:, :D] = normed[...]
    ahead_out[:, QP : QP + D] = mixed[...]
    ahead_out[:, D:QP] = jnp.zeros((ROWS, QP - D), BF)
    dm[:, :D] = d_mixed.astype(BF)
    dm[:, D:] = jnp.zeros((ROWS, QP - D), BF)
    mx[:, :D] = mixed[...]
    mx[:, D:] = jnp.zeros((ROWS, QP - D), BF)
    span = GROUP * BLK
    for i in range(2):
        for g in range(KV_HEADS):
            for r in range(GROUP):
                head = g * GROUP + r
                there = slice(r * BLK, (r + 1) * BLK)
                qd[i, g, there, :] = head_tile(q_ref, i, head, False).astype(BF)
                do = head_tile(dm, i, head, True)
                qd[i, g, span + r * BLK : span + (r + 1) * BLK, :] = do.astype(BF)
                dots = jnp.sum(do * head_tile(mx, i, head, True), axis=1, keepdims=True)
                delta[i, g, there, :] = jnp.broadcast_to(dots, (BLK, 128))
            qd_turned[i, g] = qd[i, g].astype(F32).T.astype(BF)
    dq[...] = jnp.zeros(dq.shape, F32)
    dkv[...] = jnp.zeros(dkv.shape, F32)

    def step(t, carry):
        block, chunk, place = step_place(info, t)
        allowed = causal(place, chunk)
        at = pl.multiple_of(chunk * CHUNK, CHUNK)
        for g in range(KV_HEADS):
            keys = kvs[pl.ds(at, CHUNK), g * 128 : (g + 1) * 128]
            both = dot(qd[block, g], keys, NT)
            scores, d_probs = both[:span], both[span:]
            total = lse[block, g]
            probs = jnp.exp(
                jnp.where(allowed, scores, NEG) - jnp.concatenate([total, total], axis=1)
            )
            shift = delta[block, g]
            d_scores = probs * (d_probs - jnp.concatenate([shift, shift], axis=1))
            d_low = d_scores.astype(BF)
            dq[block, g] += dot(d_low, keys)
            stacked = jnp.concatenate([d_low, probs.astype(BF)], axis=0)
            dkv[chunk, g] += dot(qd_turned[block, g], stacked)
        return carry

    lax.fori_loop(0, STEPS, step, 0)
    for i in range(2):
        rows = slice(i * BLK, (i + 1) * BLK)
        cos, sin = cosine[rows, :], sine[rows, :]
        heads = []
        for g in range(KV_HEADS):
            for r in range(GROUP):
                heads.append(dq[i, g, r * BLK : (r + 1) * BLK, :] * (HEAD**-0.5))
        for j in range(8):
            if j < 7:
                high = pltpu.roll(heads[2 * j + 1], 64, 1)
                tile = jnp.where(lane(high.shape) < HEAD, heads[2 * j], high)
                dq_out[rows, j * 128 : (j + 1) * 128] = spin(tile, cos, -sin).astype(BF)
            else:
                dq_out[rows, 896:960] = spin(heads[14], cos, -sin)[:, :64].astype(BF)
    for c in range(SEQ // CHUNK):
        for g in range(KV_HEADS):
            rows, columns = slice(c * CHUNK, (c + 1) * CHUNK), slice(g * 128, (g + 1) * 128)
            placed[rows, columns] = dkv[c, g].T.astype(BF)
    number = 0
    for out in (o0, o1, o2, o3):
        for b in range(out.shape[0] // BLK):
            at = pl.multiple_of(info[36 + number] * BLK, BLK)
            out[b * BLK : (b + 1) * BLK, :] = placed[pl.ds(at, BLK), :]
            number += 1


def attend_back(info, parts, grad, resid, gain, wo, normed, mixed, q, lse, kvs, cosine, sine, after=()):
    outs = [
        ((ROWS, D), F32),
        ((ROWS, D), BF),
        ((1, D), F32),
        ((ROWS, D), BF),
        ((ROWS, QP + D), BF),
    ] + [((4 * ROWS, 2 * KW), BF)] * 4
    shape = (2, KV_HEADS, GROUP * BLK, 128)
    scratch = [
        pltpu.VMEM((2, KV_HEADS, 2 * GROUP * BLK, 128), BF),
        pltpu.VMEM((2, KV_HEADS, 128, 2 * GROUP * BLK), BF),
        pltpu.VMEM(shape, F32),
        pltpu.VMEM(shape, F32),
        pltpu.VMEM((SEQ // CHUNK, KV_HEADS, 128, CHUNK), F32),
        pltpu.VMEM((SEQ, 2 * KW), BF),
        pltpu.VMEM((ROWS, QP), BF),
        pltpu.VMEM((ROWS, QP), BF),
        pltpu.VMEM((2, ROWS, D // 2), BF),
    ]
    return call(attend_back_body, outs, 20.0, 28, scratch, smem=1)(
        info, *parts, grad, resid, gain, *wo, normed, mixed, q, lse, kvs, cosine, sine, after=after
    )


def project_back_body(
    info, k0, k1, k2, k3, dq, d_resid, d_low, x_ref, gain, own, other, cosine, sine,
    cut_out, grad_out, dc_out, halves, dkv,
):
    side, z = info[0], info[1]
    sums = k0[...].astype(F32) + k1[...].astype(F32) + k2[...].astype(F32) + k3[...].astype(F32)
    cos, sin = cosine[...], -sine[...]
    halves[0] = dq[:, :HALF]
    halves[1] = jnp.zeros((ROWS, HALF), BF)
    halves[1, :, :HEAD] = dq[:, HALF:]
    for g in range(KV_HEADS):
        tile = sums[:, g * 128 : (g + 1) * 128]
        tile = jnp.where(lane(tile.shape) < HEAD, spin(tile, cos, sin), tile)
        dkv[:, g * 128 : (g + 1) * 128] = tile
        halves[1, :, (g + 1) * 128 : (g + 2) * 128] = tile.astype(BF)
    d_normed = dot(halves[side], own[:, :HALF], NT) + dot(halves[1 - side], other[:, :HALF], NT)
    dx, dc = norm_back(x_ref[...], gain[...], d_normed)
    dc_out[...] = dc
    grad_out[...] = d_resid[...] + dx
    query, low = dq[...].astype(F32), d_low[...].astype(F32)
    quarters = (
        query[:, :640],
        jnp.concatenate([query[:, 640:], dkv[:, :320]], axis=1),
        jnp.concatenate([dkv[:, 320:], low[:, :320]], axis=1),
        low[:, 320:],
    )
    for place in range(4):
        cut_out[(place + 4 - z) % 4] = quarters[place].astype(BF)


def project_back(info, pieces, dq, d_resid, d_low, x, gain, weight, cosine, sine, after=()):
    outs = [((4, ROWS, 640), BF), ((ROWS, D), F32), ((1, D), F32)]
    scratch = [pltpu.VMEM((2, ROWS, HALF), BF), pltpu.VMEM((ROWS, 2 * KW), F32)]
    return call(project_back_body, outs, 3.2, 16, scratch, smem=1)(
        info, *pieces, dq, d_resid, d_low, x, gain, *weight, cosine, sine, after=after
    )


def slot_of(info, c, given):
    place = info[68 + c]
    return (place % 4) * 4 + place // 4 if given else place


def feed_grads_body(*refs):
    info = refs[0]
    seconds, dgus, hiddens, lows = (refs[1 + 4 * i : 5 + 4 * i] for i in range(4))
    keep_out, give_out, left, right, hidden, low, acc, down, group = refs[17:]
    side = info[0]
    for k in range(4):
        rows = slice(k * ROWS, (k + 1) * ROWS)
        left[rows, :] = seconds[k][...]
        hidden[rows, :] = hiddens[k][...]
        low[rows, :] = lows[k][...]
        for h in range(2):
            right[h, rows, :] = dgus[k][h]
    down[...] = dot(hidden[...], low[...], TN)
    group[90:, :] = jnp.zeros((6, 640), F32)
    for turn, out in ((0, keep_out), (1, give_out)):
        half = side if turn == 0 else 1 - side
        acc[...] = dot(left[...], right[half], TN)
        for h in range(2):

            @pl.when(half == h)
            def _():
                for c in range(16):
                    at = 40 * c + 20 * h
                    group[:60, :] = acc[60 * c : 60 * c + 60, :]
                    group[60:80, :] = down[at : at + 20, :640]
                    group[80:90, :320] = down[at : at + 10, 640:]
                    group[80:90, 320:] = down[at + 10 : at + 20, 640:]
                    out[slot_of(info, c, turn)] = group[...].astype(BF)


def feed_grads(info, seconds, dgus, hiddens, lows, after=()):
    rows = 4 * ROWS
    scratch = [
        pltpu.VMEM((rows, D), BF),
        pltpu.VMEM((2, rows, 640), BF),
        pltpu.VMEM((rows, 640), BF),
        pltpu.VMEM((rows, D), BF),
        pltpu.VMEM((D, 640), F32),
        pltpu.VMEM((640, D), F32),
        pltpu.VMEM((96, 640), F32),
    ]
    return call(feed_grads_body, [((16, 96, 640), BF)] * 2, 6.5, 20, scratch, smem=1)(
        info, *seconds, *dgus, *hiddens, *lows, after=after
    )


def attend_grads_body(*refs):
    info = refs[0]
    mines, ahead = refs[1:5], refs[5]
    dc_one, dc_two, keep_out, give_out, lhs, mine, acc, group = refs[6:]
    side, z = info[0], info[1]
    for k in range(4):
        rows = slice(k * ROWS, (k + 1) * ROWS)
        for h in range(2):
            mine[h, rows, :] = mines[k][:, h * 320 : (h + 1) * 320].astype(F32).astype(BF)
        lhs[0, rows, :] = ahead[(z + 4 - k) % 4, :, :D]
        lhs[1, rows, :] = ahead[(z + 4 - k) % 4, :, QP : QP + D]
    group[60:, :] = jnp.zeros((4, 384), F32)
    for turn, out in ((0, keep_out), (1, give_out)):
        h = side if turn == 0 else 1 - side
        which = jnp.where(z + h >= 3, 1, 0)
        acc[:, :320] = dot(lhs[which], mine[h], TN)
        gain_row = jnp.where(h == 0, dc_one[...], dc_two[...])
        first = lax.broadcasted_iota(jnp.int32, (8, D), 0) == 0
        spread = jnp.where(first, jnp.broadcast_to(gain_row, (8, D)), 0.0)
        acc[:, 320:] = dot(spread, jnp.ones((8, 64), F32), TN)
        for c in range(16):
            group[:60, :] = acc[60 * c : 60 * c + 60, :]
            out[slot_of(info, c, turn)] = group[...].astype(BF)


def attend_grads(info, mines, ahead, dc_one, dc_two, after=()):
    rows = 4 * ROWS
    scratch = [
        pltpu.VMEM((2, rows, D), BF),
        pltpu.VMEM((2, rows, 320), BF),
        pltpu.VMEM((D, 384), F32),
        pltpu.VMEM((64, 384), F32),
    ]
    return call(attend_grads_body, [((16, 64, 384), BF)] * 2, 3.0, 16, scratch, smem=1)(
        info, *mines, ahead, dc_one, dc_two, after=after
    )


def finish_body(info, p0, p1, p2, p3, *outs):
    n1, gq, gk, gv, go, n2, gate, up = outs[:8]
    placed = outs[8]
    z = info[1]
    for k, piece in enumerate((p0, p1, p2, p3)):
        placed[(z + 4 - k) % 4] = piece[...]
    att = []
    for place in range(4):
        gate[:, 0, place * 640 : (place + 1) * 640] = placed[place, :, :640]
        up[:, 0, place * 640 : (place + 1) * 640] = placed[place, :, 1024:1664]
        att += [placed[place, :, 640:960], placed[place, :, 1664:1984]]
    gq[:, 0, :] = jnp.concatenate(att[:3], axis=1)
    go[:, 0, :] = jnp.concatenate(att[5:], axis=1)
    both = jnp.concatenate(att[3:5], axis=1)
    gk[:, 0, :] = jnp.concatenate([both[:, g * 128 : g * 128 + 64] for g in range(KV_HEADS)], axis=1)
    gv[:, 0, :] = jnp.concatenate([both[:, g * 128 + 64 : g * 128 + 128] for g in range(KV_HEADS)], axis=1)
    total = placed[0] + placed[1] + placed[2] + placed[3]
    n1[...] = total[:, 960:1024]
    n2[...] = total[:, 1984:2048]


def finish(info, pieces):
    widths = [D, KW, KW, D, FF, FF]
    shapes = [(15, 1, width) for width in widths]
    shapes = [(15, 64)] + shapes[:4] + [(15, 64)] + shapes[4:]
    return call(
        finish_body, [(s, F32) for s in shapes], 1.5, 8, [pltpu.VMEM((4, 15, 2048), F32)], smem=1
    )(info, *pieces)


def z_shift(value, steps):
    return lax.ppermute(value, "wsh", [(i, (i + steps) % 4) for i in range(4)])


def ctx_shift(value, steps, core_along_x):
    pairs = []
    for core in range(2):
        for y in range(4):
            for x in range(4):
                to = (y, (x + steps) % 4) if core == core_along_x else ((y + steps) % 4, x)
                pairs.append((core * 16 + y * 4 + x, core * 16 + to[0] * 4 + to[1]))
    return lax.ppermute(value, ("section", "ctx"), pairs)


def gather_shift(value, steps):
    return ctx_shift(value, steps, 0)


def reduce_shift(value, steps):
    return ctx_shift(value, steps, 1)


def swap(value):
    return lax.ppermute(value, "section", [(0, 1), (1, 0)])


def add(first, *others):
    total = first.astype(F32)
    for other in others:
        total = total + other.astype(F32)
    return total


def in_order(pieces, rank):
    stacked = jnp.stack(pieces)
    return [lax.dynamic_index_in_dim(stacked, (rank - z) % 4, 0, False) for z in range(4)]


def shards(
    tokens, cotangent, block_order, norm_one, w_query, w_key, w_value, w_out, norm_two, w_gate, w_up, w_down
):
    section = lax.axis_index("section")
    rank = lax.axis_index("ctx")
    z_rank = lax.axis_index("wsh")
    first_core = section == 0
    quarter = FF // 4

    def both(value):
        other = swap(value)
        return jnp.where(first_core, value, other), jnp.where(first_core, other, value)

    key_value = jnp.concatenate(
        [w_key[0].reshape(-1, KV_HEADS, HEAD), w_value[0].reshape(-1, KV_HEADS, HEAD)], axis=2
    ).reshape(-1, 2 * KW)
    shard_rows = w_query.shape[1]
    low_half = jnp.concatenate([w_query[0][:, :HALF], w_out[0][:, : D // 2]], axis=1)
    high_half = jnp.concatenate(
        [
            w_query[0][:, HALF:],
            jnp.zeros((shard_rows, HEAD), BF),
            key_value,
            jnp.zeros((shard_rows, 128), BF),
            w_out[0][:, D // 2 :],
        ],
        axis=1,
    )
    got = swap(jnp.where(first_core, high_half, low_half))
    layer_half = (jnp.where(first_core, low_half, got), jnp.where(first_core, got, high_half))

    gains = jnp.stack([norm_one[0], norm_two[0]])
    gain_parts = [gains] + [z_shift(gains, k) for k in (1, 2, 3)]
    gains = jnp.concatenate(in_order(gain_parts, z_rank), axis=1)
    gain_pair = [g.astype(F32) for g in both(gains)]

    given = swap(jnp.where(first_core, w_up[0], w_gate[0]))
    kind = (jnp.where(first_core, w_gate[0], given), jnp.where(first_core, given, w_up[0]))

    def none_of(mark):
        return (mark != mark).astype(jnp.int32)

    def columns(z):
        start = z * quarter
        return jnp.concatenate(
            [lax.dynamic_slice_in_dim(k, start, quarter, 1) for k in kind], axis=1
        )

    feed_columns = [columns((z_rank + k) % 4) for k in range(4)]

    def send_feed_weights(early, late):
        after, before = hold([feed_columns[1], feed_columns[3]], early)
        (across,) = hold([feed_columns[2]], late)
        return [feed_columns[0], z_shift(after, 1), z_shift(across, 2), z_shift(before, 3)]

    def join_feed_weights(parts, mark):
        later = none_of(mark)
        ordered = jnp.concatenate(in_order(parts, z_rank + later), axis=0)
        other = swap(ordered)
        return [(ordered[:, layer * quarter : (layer + 1) * quarter], other) for layer in range(2)]

    own = lax.dynamic_slice_in_dim(block_order, 2 * rank, 2, 0)
    pairs = block_order.reshape(4, 4, 2)
    y, x = rank // 4, rank % 4
    step = jnp.arange(4, dtype=jnp.int32)

    def by_core(table):
        return jnp.where(first_core, table, jnp.swapaxes(table, 0, 1))

    came = by_core(pairs[(y - step) % 4][:, (x - step) % 4]).reshape(32)
    goes = by_core(pairs[(y + step) % 4][:, (x + step) % 4]).reshape(32)
    ahead_y = ((step - y) % 4)[:, None]
    ahead_x = ((step - x) % 4)[None, :]
    slot = jnp.where(first_core, ahead_y * 4 + ahead_x, ahead_x * 4 + ahead_y).reshape(16)
    place = jnp.stack([section, z_rank]).astype(jnp.int32)
    info = jnp.concatenate([place, own, came, goes, slot]).astype(jnp.int32)
    offsets = jnp.arange(BLK, dtype=jnp.int32)
    local_pos = (own[:, None] * BLK + offsets[None, :]).reshape(ROWS)
    frequency = jnp.exp(
        jnp.arange(HEAD // 2).astype(F32) * (-2.0 * math.log(ROPE_BASE) / HEAD)
    )
    angle = local_pos.astype(F32)[:, None] * frequency[None, :]
    cos32, sin32 = jnp.cos(angle), jnp.sin(angle)
    cosine = jnp.concatenate([cos32] * 4, axis=1)
    sine = jnp.concatenate([-sin32, sin32, -sin32, sin32], axis=1)

    own_tokens = lax.dynamic_index_in_dim(tokens, section, 0, False)[0]
    own_cotangent = lax.dynamic_index_in_dim(cotangent, section, 0, False)[0]

    def z_gather(value):
        return [value] + [z_shift(value, k) for k in (1, 2, 3)]

    last_low = own_cotangent.astype(BF)

    def whole(part):
        full = lax.all_gather(part, "wsh", axis=0, tiled=True)
        return full, swap(full)

    gathered = tuple(whole(part) for part in layer_half)
    saved = []
    base, parts = own_tokens, []
    for layer in range(2):
        gain_one = gain_pair[layer][0:1]
        gain_two = gain_pair[layer][1:2]
        ahead = (saved[0]["normed"], saved[0]["mixed"], last_low) if layer else ()
        x_in, normed, q, kv, *ahead = project(
            place, base, parts, gain_one, gathered[layer], cosine, sine, ahead
        )
        if layer:
            first_ahead = lax.all_gather(ahead[0], "wsh")
        row = jnp.concatenate([kv] + [gather_shift(kv, k) for k in (1, 2, 3)], axis=0)
        pieces = [row] + [reduce_shift(row, k) for k in (1, 2, 3)]
        if layer == 0:
            sent = send_feed_weights(token(row), token(pieces[1]))
            wd = both(hold([w_down[0]], token(kv))[0])
        mixed, lse, kvs, resid, second = attend(
            info, q, pieces, gathered[layer], x_in, gain_two, after=() if layer else (token(wd[0]),)
        )
        seconds = z_gather(second)
        if layer == 0:
            wgu = join_feed_weights(sent, second[0, 0])
        if layer:
            lows = [last_low] + [
                lax.dynamic_index_in_dim(first_ahead, (z_rank - k) % 4, 0, False)[:, 2 * QP :]
                for k in (1, 2, 3)
            ]
            fed = [
                feed_both(layer, place, seconds[k], lows[k], wgu[layer], wd[layer])
                for k in range(4)
            ]
        else:
            fed = [feed(layer, place, s, wgu[layer], wd[layer]) for s in seconds]
        parts = [fed[0][2]] + [z_shift(fed[k][2], -k) for k in (1, 2, 3)]
        base = resid
        saved.append(
            dict(
                x=x_in, q=q, mixed=mixed, lse=lse, kvs=kvs, resid=resid,
                normed=normed,
                seconds=seconds, gu=[f[0] for f in fed], hidden=[f[1] for f in fed],
            )
        )
    outputs = [saved[1]["x"], add(base, *parts)]

    grad = own_cotangent
    input_grads = [None, None]
    feed_halves = [None, None]
    kept = [None, None]

    def stage_one(half):
        cut = [half[4 * k : 4 * k + 4] for k in range(4)]
        return add(cut[0], *[reduce_shift(cut[k], k) for k in (1, 2, 3)])

    def stage_two(stage):
        low = stage.astype(BF)
        return add(stage[0], *[gather_shift(low[k], k) for k in (1, 2, 3)])

    for layer in (1, 0):
        s = saved[layer]
        gain_one = gain_pair[layer][0:1]
        gain_two = gain_pair[layer][1:2]
        if layer:
            back = [(f[0], f[3]) for f in fed]
        else:
            back = [
                feed_back(layer, place, lows[k], s["gu"][k], wgu[layer], wd[layer]) for k in range(4)
            ]
        parts = [back[0][1]] + [z_shift(back[k][1], -k) for k in (1, 2, 3)]
        keep, give = feed_grads(info, s["seconds"], [b[0] for b in back], s["hidden"], lows)
        d_resid, d_low, dc_two, dq, ahead, *goes_out = attend_back(
            info, parts, grad, s["resid"], gain_two, gathered[layer], s["normed"], s["mixed"], s["q"],
            s["lse"], s["kvs"], cosine, sine, after=(token(keep),),
        )
        feed_halves[layer] = add(keep, swap(give)).astype(BF)
        row = add(goes_out[0], *[reduce_shift(goes_out[k], k) for k in (1, 2, 3)])
        row = row.astype(BF).reshape(4, ROWS, 2 * KW)
        own_pieces = [row[0]] + [gather_shift(row[k], k) for k in (1, 2, 3)]
        ahead = lax.all_gather(ahead, "wsh") if layer else first_ahead
        if layer == 0:
            kept[1] = attention_grads(none_of(d_low[0, 0]))
        cut, grad, dc_one = project_back(
            info, own_pieces, dq, d_resid, d_low, s["x"], gain_one, gathered[layer], cosine, sine,
            after=(token(ahead),) if layer else (),
        )
        input_grads[layer] = grad
        if layer:
            lows = z_gather(grad.astype(BF))

        def attention_grads(later, after=(), cut=cut, ahead=ahead, dc_one=dc_one, dc_two=dc_two):
            mines = [lax.dynamic_index_in_dim(cut, k + later, 0, False) for k in range(4)]
            mines = [mines[0]] + [z_shift(mines[k], k) for k in (1, 2, 3)]
            keep, give = attend_grads(info, mines, ahead, dc_one, dc_two, after)
            return add(keep, swap(give)).astype(BF)

        if layer == 0:
            feed_stage = stage_one(jnp.concatenate(hold(feed_halves, token(row)), axis=1))
            kept[0] = attention_grads(0, (token(feed_stage),))
    attend_stage = stage_one(jnp.concatenate(kept, axis=2))
    both_sums = stage_two(
        jnp.concatenate(
            [feed_stage[:, :96], feed_stage[:, 96:], jnp.pad(attend_stage, ((0, 0), (0, 32), (0, 0)))],
            axis=2,
        )
    )
    feed_sums = (both_sums[:, :640], both_sums[:, 640:1280])
    attend_sum = both_sums[:64, 1280:]
    sums = [
        jnp.concatenate(
            [feed_sums[layer], jnp.pad(attend_sum[:, layer * 384 : (layer + 1) * 384], ((0, 32), (0, 0)))],
            axis=1,
        )
        for layer in range(2)
    ]

    mine = jnp.where(first_core, sums[0], sums[1])
    other = swap(jnp.where(first_core, sums[1], sums[0]))
    halves = (jnp.where(first_core, mine, other), jnp.where(first_core, other, mine))
    joined = jnp.concatenate([h[:60] for h in halves], axis=1).reshape(4, 15, 2048)
    pieces = [lax.dynamic_index_in_dim(joined, z_rank, 0, False)] + [
        z_shift(lax.dynamic_index_in_dim(joined, (z_rank + k) % 4, 0, False), k) for k in (1, 2, 3)
    ]
    down = jnp.concatenate(
        [
            jnp.concatenate(
                [h[60:80, :640], jnp.concatenate([h[80:90, :320], h[80:90, 320:640]], axis=0)], axis=1
            )
            for h in halves
        ],
        axis=0,
    )
    moves = [(c * 4 + z, (4 * z + c // 4) * 4 + c % 4) for c in range(16) for z in range(4)]
    grad_down = lax.ppermute(down, ("ctx", "wsh"), moves)[None]
    sum_one, gq, gk, gv, go, sum_two, gate, up = finish(info, pieces)
    grad_query, grad_key, grad_value, grad_out, grad_gate, grad_up = (
        jnp.swapaxes(g, 0, 1) for g in (gq, gk, gv, go, gate, up)
    )

    def arranged(pair):
        mine = jnp.where(first_core, pair[0], pair[1])
        other = swap(jnp.where(first_core, pair[1], pair[0]))
        first = jnp.where(first_core, mine, other)
        last = jnp.where(first_core, other, mine)
        return jnp.stack([first, last])[None, :, None]

    return (
        arranged(outputs),
        arranged(input_grads),
        sum_one[:, 0][None],
        grad_query,
        grad_key,
        grad_value,
        grad_out,
        sum_two[:, 0][None],
        grad_gate,
        grad_up,
        grad_down,
    )


def solution(mesh):
    rows = P(None, "wsh", "ctx", None)
    gain = P("section", "wsh")
    weight = P("section", "wsh", None)
    in_specs = (rows, rows, P(), gain, weight, weight, weight, weight, gain, weight, weight, weight)
    result = P("section", None, "wsh", "ctx", None)
    gain_out = P("section", ("ctx", "wsh"))
    weight_out = P("section", ("ctx", "wsh"), None)
    out_specs = (
        result, result, gain_out, weight_out, weight_out, weight_out, weight_out, gain_out,
        weight_out, weight_out, weight_out,
    )
    return jax.shard_map(shards, mesh=mesh, in_specs=in_specs, out_specs=out_specs, check_vma=False)
```

```python
import math
from functools import partial

import jax
import jax.numpy as jnp
from jax import lax
from jax.experimental import pallas as pl
from jax.experimental.pallas import tpu as pltpu
from jax.sharding import PartitionSpec as P

HEADS = 15
KV_HEADS = 5
HEAD = 64
GROUP = HEADS // KV_HEADS
D = 960
FF = 2560
KW = KV_HEADS * HEAD
ROWS = 128
BLK = 64
SEQ = 2048
CHUNK = 256
STEPS = 9
EPS = 1e-05
ROPE_BASE = 10000.0
BF = jnp.bfloat16
F32 = jnp.float32
QP = 1024
HALF = 896
NEG = -1e30
MIB = 1024 * 1024

NN = (((1,), (0,)), ((), ()))
NT = (((1,), (1,)), ((), ()))
TN = (((0,), (0,)), ((), ()))


def dot(left, right, dims=NN):
    return lax.dot_general(left, right, dims, preferred_element_type=F32)


def call(body, outs, micros, mib, scratch=(), smem=0):
    def run(*args, after=()):
        count = len(args)
        in_specs = [
            pl.BlockSpec(memory_space=pltpu.SMEM if i < smem else pltpu.VMEM) for i in range(count)
        ] + [pl.BlockSpec(memory_space=pl.ANY) for _ in after]

        def inner(*refs):
            body(*refs[:count], *refs[count + len(after) :])

        out = pl.pallas_call(
            inner,
            in_specs=in_specs,
            out_specs=[pl.BlockSpec(memory_space=pltpu.VMEM) for _ in outs],
            out_shape=[jax.ShapeDtypeStruct(s, t) for s, t in outs],
            scratch_shapes=list(scratch),
            cost_estimate=pl.CostEstimate(
                flops=int(micros * 1.1e9), bytes_accessed=int(micros * 3.6e6), transcendentals=0
            ),
            compiler_params=pltpu.CompilerParams(vmem_limit_bytes=mib * MIB),
        )(*args, *after)
        return out

    return run


def token(*arrays):
    return jnp.stack([a[(0,) * a.ndim].astype(F32) for a in arrays])


def hold(arrays, mark):
    count = len(arrays)

    def body(*refs):
        del refs

    return pl.pallas_call(
        body,
        in_specs=[pl.BlockSpec(memory_space=pl.ANY)] * (count + 1),
        out_specs=[pl.BlockSpec(memory_space=pl.ANY)] * count,
        out_shape=[jax.ShapeDtypeStruct(a.shape, a.dtype) for a in arrays],
        input_output_aliases={i: i for i in range(count)},
    )(*arrays, mark)


def lane(shape):
    return lax.broadcasted_iota(jnp.int32, shape, 1)


def normalise(x, gain):
    return x * lax.rsqrt(jnp.mean(x * x, axis=-1, keepdims=True) + EPS) * gain


def norm_back(x, gain, dy):
    r = lax.rsqrt(jnp.mean(x * x, axis=-1, keepdims=True) + EPS)
    cdy = gain * dy
    dx = r * cdy - x * (r * r * r) * jnp.mean(x * cdy, axis=-1, keepdims=True)
    dc = jnp.sum(dy * x * r, axis=0, keepdims=True)
    return dx, dc


def spin(tile, cosine, sine):
    first = (lane(tile.shape) % HEAD) < HEAD // 2
    swapped = jnp.where(first, pltpu.roll(tile, 96, 1), pltpu.roll(tile, 32, 1))
    return tile * cosine + swapped * sine


def project_body(count):
    def body(*refs):
        info, base = refs[:2]
        parts = refs[2 : 2 + count]
        gain, own, other, cosine, sine = refs[2 + count : 7 + count]
        if count:
            ahead_in = refs[7 + count : 10 + count]
            x_out, normed_out, q_out, kv_out, ahead_out, halves = refs[10 + count :]
            ahead_out[...] = jnp.zeros((ROWS, 2 * QP + D), BF)
            for i in range(3):
                ahead_out[:, i * QP : i * QP + D] = ahead_in[i][...]
        else:
            x_out, normed_out, q_out, kv_out, halves = refs[7:]
        side = info[0]
        x = base[...]
        for part in parts:
            x = x + part[...].astype(F32)
        x_out[...] = x
        normed = normalise(x, gain[...]).astype(BF)
        normed_out[...] = normed
        cos, sin = cosine[...], sine[...]
        halves[side] = dot(normed, own[:, :HALF])
        halves[1 - side] = dot(normed, other[:, :HALF])
        for j in range(8):
            tile = halves[0, :, j * 128 : (j + 1) * 128] if j < 7 else halves[1, :, 0:128]
            q_out[:, j * 128 : (j + 1) * 128] = (spin(tile, cos, sin) * (HEAD**-0.5)).astype(BF)
        for g in range(KV_HEADS):
            tile = halves[1, :, (g + 1) * 128 : (g + 2) * 128]
            tile = jnp.where(lane(tile.shape) < HEAD, spin(tile, cos, sin), tile)
            kv_out[:, g * 128 : (g + 1) * 128] = tile.astype(BF)

    return body


def project(info, base, parts, gain, weight, cosine, sine, ahead=()):
    outs = [((ROWS, D), F32), ((ROWS, D), BF), ((ROWS, QP), BF), ((ROWS, 2 * KW), BF)]
    if ahead:
        outs.append(((ROWS, 2 * QP + D), BF))
    scratch = [pltpu.VMEM((2, ROWS, HALF), F32)]
    return call(project_body(len(parts)), outs, 2.5, 16, scratch, smem=1)(
        info, base, *parts, gain, *weight, cosine, sine, *ahead
    )


def step_place(info, t):
    first, second = info[2], info[3]
    count = first // 4 + 1
    early = t < count
    block = jnp.where(early, 0, 1)
    chunk = jnp.where(early, t, t - count)
    place = jnp.where(early, first, second)
    return block, chunk, place


def causal(place, chunk):
    rows = lax.broadcasted_iota(jnp.int32, (BLK, CHUNK), 0) + place * BLK
    cols = lax.broadcasted_iota(jnp.int32, (BLK, CHUNK), 1) + chunk * CHUNK
    one = rows >= cols
    return jnp.concatenate([one] * GROUP, axis=0)


def head_tile(ref, block, head, upper):
    j = head // 2
    tile = ref[block * BLK : (block + 1) * BLK, j * 128 : (j + 1) * 128].astype(F32)
    if (head % 2 == 1) != upper:
        tile = pltpu.roll(tile, 64, 1)
    keep = (lane(tile.shape) >= HEAD) if upper else (lane(tile.shape) < HEAD)
    return jnp.where(keep, tile, 0.0)


def attend_body(count):
    def body(*refs):
        info, q_ref = refs[0], refs[1]
        pieces = refs[2 : 2 + count]
        (own, other, x_ref, gain, mixed_out, lse_out, kvs, resid_out, second_out) = refs[
            2 + count : 11 + count
        ]
        qh, top, total, acc, halves = refs[11 + count :]
        side = info[0]
        number = 0
        for piece in pieces:
            for b in range(piece.shape[0] // BLK):
                at = pl.multiple_of(info[4 + number] * BLK, BLK)
                kvs[pl.ds(at, BLK), :] = piece[b * BLK : (b + 1) * BLK, :]
                number += 1
        for i in range(2):
            for g in range(KV_HEADS):
                for r in range(GROUP):
                    qh[i, g, r * BLK : (r + 1) * BLK, :] = head_tile(
                        q_ref, i, g * GROUP + r, False
                    ).astype(BF)
        top[...] = jnp.full(top.shape, NEG, F32)
        total[...] = jnp.zeros(total.shape, F32)
        acc[...] = jnp.zeros(acc.shape, F32)

        def step(t, carry):
            block, chunk, place = step_place(info, t)
            allowed = causal(place, chunk)
            at = pl.multiple_of(chunk * CHUNK, CHUNK)
            for g in range(KV_HEADS):
                keys = kvs[pl.ds(at, CHUNK), g * 128 : (g + 1) * 128]
                scores = dot(qh[block, g], keys, NT)
                scores = jnp.where(allowed, scores, NEG)
                old = top[block, g]
                new = jnp.maximum(old, jnp.max(scores, axis=1, keepdims=True))
                probs = jnp.exp(scores - jnp.concatenate([new, new], axis=1))
                shrink = jnp.exp(old - new)
                top[block, g] = new
                total[block, g] = shrink * total[block, g] + jnp.sum(probs, axis=1, keepdims=True)
                acc[block, g] = shrink * acc[block, g] + dot(probs.astype(BF), keys)
            return carry

        lax.fori_loop(0, STEPS, step, 0)
        for i in range(2):
            heads = []
            for g in range(KV_HEADS):
                sums = total[i, g]
                result = acc[i, g] / sums
                lse_out[i, g] = top[i, g] + jnp.log(sums)
                for r in range(GROUP):
                    heads.append(result[r * BLK : (r + 1) * BLK, :])
            for j in range(8):
                low = pltpu.roll(heads[2 * j], 64, 1)
                rows = slice(i * BLK, (i + 1) * BLK)
                if j < 7:
                    tile = jnp.where(lane(low.shape) < HEAD, low, heads[2 * j + 1])
                    mixed_out[rows, j * 128 : (j + 1) * 128] = tile.astype(BF)
                else:
                    mixed_out[rows, 896:960] = low[:, :64].astype(BF)
        halves[side] = dot(mixed_out[...], own[:, HALF:])
        halves[1 - side] = dot(mixed_out[...], other[:, HALF:])
        resid = x_ref[...] + jnp.concatenate([halves[0], halves[1]], axis=1)
        resid_out[...] = resid
        second_out[...] = normalise(resid, gain[...]).astype(BF)

    return body


def attend(info, q, pieces, wo, x, gain, after=()):
    outs = [
        ((ROWS, D), BF),
        ((2, KV_HEADS, GROUP * BLK, 128), F32),
        ((SEQ, 2 * KW), BF),
        ((ROWS, D), F32),
        ((ROWS, D), BF),
    ]
    shape = (2, KV_HEADS, GROUP * BLK, 128)
    scratch = [pltpu.VMEM(shape, BF)] + [pltpu.VMEM(shape, F32)] * 3
    scratch.append(pltpu.VMEM((2, ROWS, D // 2), F32))
    return call(attend_body(len(pieces)), outs, 12.0, 18, scratch, smem=1)(
        info, q, *pieces, *wo, x, gain, after=after
    )


def feed_body(layer, info, second, own, other, wd, gu_out, hidden_out, part_out):
    side = info[0]
    columns = slice(layer * FF // 4, (layer + 1) * FF // 4)
    gu_out[side] = dot(second[...], own[...])
    gu_out[1 - side] = dot(second[...], other[:, columns])
    gate, up = gu_out[0], gu_out[1]
    hidden = (gate / (1.0 + jnp.exp(-gate)) * up).astype(BF)
    hidden_out[...] = hidden
    part_out[...] = dot(hidden, wd[...]).astype(BF)


def feed(layer, info, second, wgu, wd):
    outs = [((2, ROWS, FF // 4), F32), ((ROWS, FF // 4), BF), ((ROWS, D), BF)]
    body = partial(feed_body, layer)
    return call(body, outs, 1.0, 12, smem=1)(info, second, *wgu, wd)


def feed_back_body(layer, info, grad_low, gu, own, other, wd, dgu_out, part_out):
    side = info[0]
    columns = slice(layer * FF // 4, (layer + 1) * FF // 4)
    d_hidden = dot(grad_low[...], wd[...], NT)
    gate, up = gu[0], gu[1]
    sig = 1.0 / (1.0 + jnp.exp(-gate))
    d_gate = d_hidden * up * sig * (1.0 + gate * (1.0 - sig))
    d_up = d_hidden * gate * sig
    dgu_out[0] = d_gate.astype(BF)
    dgu_out[1] = d_up.astype(BF)
    part = dot(dgu_out[side], own[...], NT) + dot(dgu_out[1 - side], other[:, columns], NT)
    part_out[...] = part.astype(BF)


def feed_back(layer, info, grad_low, gu, wgu, wd):
    outs = [((2, ROWS, FF // 4), BF), ((ROWS, D), BF)]
    body = partial(feed_back_body, layer)
    return call(body, outs, 1.3, 12, smem=1)(info, grad_low, gu, *wgu, wd)


def feed_both_body(
    layer, info, second, grad_low, own, other, wd, dgu_out, hidden_out, part_out, back_out, gu
):
    feed_body(layer, info, second, own, other, wd, gu, hidden_out, part_out)
    feed_back_body(layer, info, grad_low, gu, own, other, wd, dgu_out, back_out)


def feed_both(layer, info, second, grad_low, wgu, wd):
    half = (2, ROWS, FF // 4)
    outs = [(half, BF), ((ROWS, FF // 4), BF), ((ROWS, D), BF), ((ROWS, D), BF)]
    body = partial(feed_both_body, layer)
    return call(body, outs, 2.5, 12, [pltpu.VMEM(half, F32)], smem=1)(
        info, second, grad_low, *wgu, wd
    )


def attend_back_body(
    info, p0, p1, p2, p3, grad, resid, gain, own, other, mixed, q_ref, lse, kvs, cosine, sine,
    d_resid_out, d_low_out, dc_out, dq_out, o0, o1, o2, o3,
    qd, qd_turned, delta, dq, dkv, placed, dm, mx, halves,
):
    d_second = p0[...].astype(F32) + p1[...].astype(F32) + p2[...].astype(F32) + p3[...].astype(F32)
    dx, dc = norm_back(resid[...], gain[...], d_second)
    dc_out[...] = dc
    d_resid = grad[...] + dx
    d_resid_out[...] = d_resid
    low = d_resid.astype(BF)
    d_low_out[...] = low
    side = info[0]
    halves[0] = d_resid[:, : D // 2].astype(BF)
    halves[1] = d_resid[:, D // 2 :].astype(BF)
    d_mixed = dot(halves[side], own[:, HALF:], NT) + dot(halves[1 - side], other[:, HALF:], NT)
    dm[:, :D] = d_mixed.astype(BF)
    dm[:, D:] = jnp.zeros((ROWS, QP - D), BF)
    mx[:, :D] = mixed[...]
    mx[:, D:] = jnp.zeros((ROWS, QP - D), BF)
    span = GROUP * BLK
    for i in range(2):
        for g in range(KV_HEADS):
            for r in range(GROUP):
                head = g * GROUP + r
                there = slice(r * BLK, (r + 1) * BLK)
                qd[i, g, there, :] = head_tile(q_ref, i, head, False).astype(BF)
                do = head_tile(dm, i, head, True)
                qd[i, g, span + r * BLK : span + (r + 1) * BLK, :] = do.astype(BF)
                dots = jnp.sum(do * head_tile(mx, i, head, True), axis=1, keepdims=True)
                delta[i, g, there, :] = jnp.broadcast_to(dots, (BLK, 128))
            qd_turned[i, g] = qd[i, g].astype(F32).T.astype(BF)
    dq[...] = jnp.zeros(dq.shape, F32)
    dkv[...] = jnp.zeros(dkv.shape, F32)

    def step(t, carry):
        block, chunk, place = step_place(info, t)
        allowed = causal(place, chunk)
        at = pl.multiple_of(chunk * CHUNK, CHUNK)
        for g in range(KV_HEADS):
            keys = kvs[pl.ds(at, CHUNK), g * 128 : (g + 1) * 128]
            both = dot(qd[block, g], keys, NT)
            scores, d_probs = both[:span], both[span:]
            total = lse[block, g]
            probs = jnp.exp(
                jnp.where(allowed, scores, NEG) - jnp.concatenate([total, total], axis=1)
            )
            shift = delta[block, g]
            d_scores = probs * (d_probs - jnp.concatenate([shift, shift], axis=1))
            d_low = d_scores.astype(BF)
            dq[block, g] += dot(d_low, keys)
            stacked = jnp.concatenate([d_low, probs.astype(BF)], axis=0)
            dkv[chunk, g] += dot(qd_turned[block, g], stacked)
        return carry

    lax.fori_loop(0, STEPS, step, 0)
    for i in range(2):
        rows = slice(i * BLK, (i + 1) * BLK)
        cos, sin = cosine[rows, :], sine[rows, :]
        heads = []
        for g in range(KV_HEADS):
            for r in range(GROUP):
                heads.append(dq[i, g, r * BLK : (r + 1) * BLK, :] * (HEAD**-0.5))
        for j in range(8):
            if j < 7:
                high = pltpu.roll(heads[2 * j + 1], 64, 1)
                tile = jnp.where(lane(high.shape) < HEAD, heads[2 * j], high)
                dq_out[rows, j * 128 : (j + 1) * 128] = spin(tile, cos, -sin).astype(BF)
            else:
                dq_out[rows, 896:960] = spin(heads[14], cos, -sin)[:, :64].astype(BF)
    for c in range(SEQ // CHUNK):
        for g in range(KV_HEADS):
            rows, columns = slice(c * CHUNK, (c + 1) * CHUNK), slice(g * 128, (g + 1) * 128)
            placed[rows, columns] = dkv[c, g].T.astype(BF)
    number = 0
    for out in (o0, o1, o2, o3):
        for b in range(out.shape[0] // BLK):
            at = pl.multiple_of(info[36 + number] * BLK, BLK)
            out[b * BLK : (b + 1) * BLK, :] = placed[pl.ds(at, BLK), :]
            number += 1


def attend_back(info, parts, grad, resid, gain, wo, mixed, q, lse, kvs, cosine, sine, after=()):
    outs = [
        ((ROWS, D), F32),
        ((ROWS, D), BF),
        ((1, D), F32),
        ((ROWS, D), BF),
    ] + [((4 * ROWS, 2 * KW), BF)] * 4
    shape = (2, KV_HEADS, GROUP * BLK, 128)
    scratch = [
        pltpu.VMEM((2, KV_HEADS, 2 * GROUP * BLK, 128), BF),
        pltpu.VMEM((2, KV_HEADS, 128, 2 * GROUP * BLK), BF),
        pltpu.VMEM(shape, F32),
        pltpu.VMEM(shape, F32),
        pltpu.VMEM((SEQ // CHUNK, KV_HEADS, 128, CHUNK), F32),
        pltpu.VMEM((SEQ, 2 * KW), BF),
        pltpu.VMEM((ROWS, QP), BF),
        pltpu.VMEM((ROWS, QP), BF),
        pltpu.VMEM((2, ROWS, D // 2), BF),
    ]
    return call(attend_back_body, outs, 20.0, 28, scratch, smem=1)(
        info, *parts, grad, resid, gain, *wo, mixed, q, lse, kvs, cosine, sine, after=after
    )


def project_back_body(
    info, k0, k1, k2, k3, dq, d_resid, d_low, x_ref, gain, own, other, cosine, sine,
    cut_out, grad_out, dc_out, halves, dkv,
):
    side, z = info[0], info[1]
    sums = k0[...].astype(F32) + k1[...].astype(F32) + k2[...].astype(F32) + k3[...].astype(F32)
    cos, sin = cosine[...], -sine[...]
    halves[0] = dq[:, :HALF]
    halves[1] = jnp.zeros((ROWS, HALF), BF)
    halves[1, :, :HEAD] = dq[:, HALF:]
    for g in range(KV_HEADS):
        tile = sums[:, g * 128 : (g + 1) * 128]
        tile = jnp.where(lane(tile.shape) < HEAD, spin(tile, cos, sin), tile)
        dkv[:, g * 128 : (g + 1) * 128] = tile
        halves[1, :, (g + 1) * 128 : (g + 2) * 128] = tile.astype(BF)
    d_normed = dot(halves[side], own[:, :HALF], NT) + dot(halves[1 - side], other[:, :HALF], NT)
    dx, dc = norm_back(x_ref[...], gain[...], d_normed)
    dc_out[...] = dc
    grad_out[...] = d_resid[...] + dx
    query, low = dq[...].astype(F32), d_low[...].astype(F32)
    quarters = (
        query[:, :640],
        jnp.concatenate([query[:, 640:], dkv[:, :320]], axis=1),
        jnp.concatenate([dkv[:, 320:], low[:, :320]], axis=1),
        low[:, 320:],
    )
    for place in range(4):
        cut_out[(place + 4 - z) % 4] = quarters[place].astype(BF)


def project_back(info, pieces, dq, d_resid, d_low, x, gain, weight, cosine, sine, after=()):
    outs = [((4, ROWS, 640), BF), ((ROWS, D), F32), ((1, D), F32)]
    scratch = [pltpu.VMEM((2, ROWS, HALF), BF), pltpu.VMEM((ROWS, 2 * KW), F32)]
    return call(project_back_body, outs, 3.2, 16, scratch, smem=1)(
        info, *pieces, dq, d_resid, d_low, x, gain, *weight, cosine, sine, after=after
    )


def slot_of(info, c, given):
    place = info[68 + c]
    return (place % 4) * 4 + place // 4 if given else place


def feed_grads_body(*refs):
    info = refs[0]
    seconds, dgus, hiddens, lows = (refs[1 + 4 * i : 5 + 4 * i] for i in range(4))
    keep_out, give_out, left, right, hidden, low, acc, down, group = refs[17:]
    side = info[0]
    for k in range(4):
        rows = slice(k * ROWS, (k + 1) * ROWS)
        left[rows, :] = seconds[k][...]
        hidden[rows, :] = hiddens[k][...]
        low[rows, :] = lows[k][...]
        for h in range(2):
            right[h, rows, :] = dgus[k][h]
    down[...] = dot(hidden[...], low[...], TN)
    group[90:, :] = jnp.zeros((6, 640), F32)
    for turn, out in ((0, keep_out), (1, give_out)):
        half = side if turn == 0 else 1 - side
        acc[...] = dot(left[...], right[half], TN)
        for h in range(2):

            @pl.when(half == h)
            def _():
                for c in range(16):
                    at = 40 * c + 20 * h
                    group[:60, :] = acc[60 * c : 60 * c + 60, :]
                    group[60:80, :] = down[at : at + 20, :640]
                    group[80:90, :320] = down[at : at + 10, 640:]
                    group[80:90, 320:] = down[at + 10 : at + 20, 640:]
                    out[slot_of(info, c, turn)] = group[...].astype(BF)


def feed_grads(info, seconds, dgus, hiddens, lows, after=()):
    rows = 4 * ROWS
    scratch = [
        pltpu.VMEM((rows, D), BF),
        pltpu.VMEM((2, rows, 640), BF),
        pltpu.VMEM((rows, 640), BF),
        pltpu.VMEM((rows, D), BF),
        pltpu.VMEM((D, 640), F32),
        pltpu.VMEM((640, D), F32),
        pltpu.VMEM((96, 640), F32),
    ]
    return call(feed_grads_body, [((16, 96, 640), BF)] * 2, 6.5, 20, scratch, smem=1)(
        info, *seconds, *dgus, *hiddens, *lows, after=after
    )


def attend_grads_body(*refs):
    info = refs[0]
    mines, ahead = refs[1:5], refs[5]
    dc_one, dc_two, keep_out, give_out, lhs, mine, acc, group = refs[6:]
    side, z = info[0], info[1]
    for k in range(4):
        rows = slice(k * ROWS, (k + 1) * ROWS)
        for h in range(2):
            mine[h, rows, :] = mines[k][:, h * 320 : (h + 1) * 320].astype(F32).astype(BF)
        lhs[0, rows, :] = ahead[(z + 4 - k) % 4, :, :D]
        lhs[1, rows, :] = ahead[(z + 4 - k) % 4, :, QP : QP + D]
    group[60:, :] = jnp.zeros((4, 384), F32)
    for turn, out in ((0, keep_out), (1, give_out)):
        h = side if turn == 0 else 1 - side
        which = jnp.where(z + h >= 3, 1, 0)
        acc[:, :320] = dot(lhs[which], mine[h], TN)
        gain_row = jnp.where(h == 0, dc_one[...], dc_two[...])
        first = lax.broadcasted_iota(jnp.int32, (8, D), 0) == 0
        spread = jnp.where(first, jnp.broadcast_to(gain_row, (8, D)), 0.0)
        acc[:, 320:] = dot(spread, jnp.ones((8, 64), F32), TN)
        for c in range(16):
            group[:60, :] = acc[60 * c : 60 * c + 60, :]
            out[slot_of(info, c, turn)] = group[...].astype(BF)


def attend_grads(info, mines, ahead, dc_one, dc_two, after=()):
    rows = 4 * ROWS
    scratch = [
        pltpu.VMEM((2, rows, D), BF),
        pltpu.VMEM((2, rows, 320), BF),
        pltpu.VMEM((D, 384), F32),
        pltpu.VMEM((64, 384), F32),
    ]
    return call(attend_grads_body, [((16, 64, 384), BF)] * 2, 3.0, 16, scratch, smem=1)(
        info, *mines, ahead, dc_one, dc_two, after=after
    )


def finish_body(info, p0, p1, p2, p3, *outs):
    n1, gq, gk, gv, go, n2, gate, up = outs[:8]
    placed = outs[8]
    z = info[1]
    for k, piece in enumerate((p0, p1, p2, p3)):
        placed[(z + 4 - k) % 4] = piece[...]
    att = []
    for place in range(4):
        gate[:, 0, place * 640 : (place + 1) * 640] = placed[place, :, :640]
        up[:, 0, place * 640 : (place + 1) * 640] = placed[place, :, 1024:1664]
        att += [placed[place, :, 640:960], placed[place, :, 1664:1984]]
    gq[:, 0, :] = jnp.concatenate(att[:3], axis=1)
    go[:, 0, :] = jnp.concatenate(att[5:], axis=1)
    both = jnp.concatenate(att[3:5], axis=1)
    gk[:, 0, :] = jnp.concatenate([both[:, g * 128 : g * 128 + 64] for g in range(KV_HEADS)], axis=1)
    gv[:, 0, :] = jnp.concatenate([both[:, g * 128 + 64 : g * 128 + 128] for g in range(KV_HEADS)], axis=1)
    total = placed[0] + placed[1] + placed[2] + placed[3]
    n1[...] = total[:, 960:1024]
    n2[...] = total[:, 1984:2048]


def finish(info, pieces):
    widths = [D, KW, KW, D, FF, FF]
    shapes = [(15, 1, width) for width in widths]
    shapes = [(15, 64)] + shapes[:4] + [(15, 64)] + shapes[4:]
    return call(
        finish_body, [(s, F32) for s in shapes], 1.5, 8, [pltpu.VMEM((4, 15, 2048), F32)], smem=1
    )(info, *pieces)


def z_shift(value, steps):
    return lax.ppermute(value, "wsh", [(i, (i + steps) % 4) for i in range(4)])


def ctx_shift(value, steps, core_along_x):
    pairs = []
    for core in range(2):
        for y in range(4):
            for x in range(4):
                to = (y, (x + steps) % 4) if core == core_along_x else ((y + steps) % 4, x)
                pairs.append((core * 16 + y * 4 + x, core * 16 + to[0] * 4 + to[1]))
    return lax.ppermute(value, ("section", "ctx"), pairs)


def gather_shift(value, steps):
    return ctx_shift(value, steps, 0)


def reduce_shift(value, steps):
    return ctx_shift(value, steps, 1)


def swap(value):
    return lax.ppermute(value, "section", [(0, 1), (1, 0)])


def add(first, *others):
    total = first.astype(F32)
    for other in others:
        total = total + other.astype(F32)
    return total


def in_order(pieces, rank):
    stacked = jnp.stack(pieces)
    return [lax.dynamic_index_in_dim(stacked, (rank - z) % 4, 0, False) for z in range(4)]


def shards(
    tokens, cotangent, block_order, norm_one, w_query, w_key, w_value, w_out, norm_two, w_gate, w_up, w_down
):
    section = lax.axis_index("section")
    rank = lax.axis_index("ctx")
    z_rank = lax.axis_index("wsh")
    first_core = section == 0
    quarter = FF // 4

    def both(value):
        other = swap(value)
        return jnp.where(first_core, value, other), jnp.where(first_core, other, value)

    key_value = jnp.concatenate(
        [w_key[0].reshape(-1, KV_HEADS, HEAD), w_value[0].reshape(-1, KV_HEADS, HEAD)], axis=2
    ).reshape(-1, 2 * KW)
    shard_rows = w_query.shape[1]
    low_half = jnp.concatenate([w_query[0][:, :HALF], w_out[0][:, : D // 2]], axis=1)
    high_half = jnp.concatenate(
        [
            w_query[0][:, HALF:],
            jnp.zeros((shard_rows, HEAD), BF),
            key_value,
            jnp.zeros((shard_rows, 128), BF),
            w_out[0][:, D // 2 :],
        ],
        axis=1,
    )
    got = swap(jnp.where(first_core, high_half, low_half))
    layer_half = (jnp.where(first_core, low_half, got), jnp.where(first_core, got, high_half))

    gains = jnp.stack([norm_one[0], norm_two[0]])
    gain_parts = [gains] + [z_shift(gains, k) for k in (1, 2, 3)]
    gains = jnp.concatenate(in_order(gain_parts, z_rank), axis=1)
    gain_pair = [g.astype(F32) for g in both(gains)]

    given = swap(jnp.where(first_core, w_up[0], w_gate[0]))
    kind = (jnp.where(first_core, w_gate[0], given), jnp.where(first_core, given, w_up[0]))

    def none_of(mark):
        return (mark != mark).astype(jnp.int32)

    def columns(z):
        start = z * quarter
        return jnp.concatenate(
            [lax.dynamic_slice_in_dim(k, start, quarter, 1) for k in kind], axis=1
        )

    feed_columns = [columns((z_rank + k) % 4) for k in range(4)]

    def send_feed_weights(early, late):
        after, before = hold([feed_columns[1], feed_columns[3]], early)
        (across,) = hold([feed_columns[2]], late)
        return [feed_columns[0], z_shift(after, 1), z_shift(across, 2), z_shift(before, 3)]

    def join_feed_weights(parts, mark):
        later = none_of(mark)
        ordered = jnp.concatenate(in_order(parts, z_rank + later), axis=0)
        other = swap(ordered)
        return [(ordered[:, layer * quarter : (layer + 1) * quarter], other) for layer in range(2)]

    own = lax.dynamic_slice_in_dim(block_order, 2 * rank, 2, 0)
    pairs = block_order.reshape(4, 4, 2)
    y, x = rank // 4, rank % 4
    step = jnp.arange(4, dtype=jnp.int32)

    def by_core(table):
        return jnp.where(first_core, table, jnp.swapaxes(table, 0, 1))

    came = by_core(pairs[(y - step) % 4][:, (x - step) % 4]).reshape(32)
    goes = by_core(pairs[(y + step) % 4][:, (x + step) % 4]).reshape(32)
    ahead_y = ((step - y) % 4)[:, None]
    ahead_x = ((step - x) % 4)[None, :]
    slot = jnp.where(first_core, ahead_y * 4 + ahead_x, ahead_x * 4 + ahead_y).reshape(16)
    place = jnp.stack([section, z_rank]).astype(jnp.int32)
    info = jnp.concatenate([place, own, came, goes, slot]).astype(jnp.int32)
    offsets = jnp.arange(BLK, dtype=jnp.int32)
    local_pos = (own[:, None] * BLK + offsets[None, :]).reshape(ROWS)
    frequency = jnp.exp(
        jnp.arange(HEAD // 2).astype(F32) * (-2.0 * math.log(ROPE_BASE) / HEAD)
    )
    angle = local_pos.astype(F32)[:, None] * frequency[None, :]
    cos32, sin32 = jnp.cos(angle), jnp.sin(angle)
    cosine = jnp.concatenate([cos32] * 4, axis=1)
    sine = jnp.concatenate([-sin32, sin32, -sin32, sin32], axis=1)

    own_tokens = lax.dynamic_index_in_dim(tokens, section, 0, False)[0]
    own_cotangent = lax.dynamic_index_in_dim(cotangent, section, 0, False)[0]

    def z_gather(value):
        return [value] + [z_shift(value, k) for k in (1, 2, 3)]

    last_low = own_cotangent.astype(BF)

    def whole(part):
        full = lax.all_gather(part, "wsh", axis=0, tiled=True)
        return full, swap(full)

    gathered = tuple(whole(part) for part in layer_half)
    saved = []
    base, parts = own_tokens, []
    for layer in range(2):
        gain_one = gain_pair[layer][0:1]
        gain_two = gain_pair[layer][1:2]
        ahead = (saved[0]["normed"], saved[0]["mixed"], last_low) if layer else ()
        x_in, normed, q, kv, *ahead = project(
            place, base, parts, gain_one, gathered[layer], cosine, sine, ahead
        )
        if layer:
            first_ahead = lax.all_gather(ahead[0], "wsh")
        row = jnp.concatenate([kv] + [gather_shift(kv, k) for k in (1, 2, 3)], axis=0)
        pieces = [row] + [reduce_shift(row, k) for k in (1, 2, 3)]
        if layer == 0:
            sent = send_feed_weights(token(row), token(pieces[1]))
            wd = both(hold([w_down[0]], token(kv))[0])
        mixed, lse, kvs, resid, second = attend(
            info, q, pieces, gathered[layer], x_in, gain_two, after=() if layer else (token(wd[0]),)
        )
        seconds = z_gather(second)
        if layer == 0:
            wgu = join_feed_weights(sent, second[0, 0])
        if layer:
            lows = [last_low] + [
                lax.dynamic_index_in_dim(first_ahead, (z_rank - k) % 4, 0, False)[:, 2 * QP :]
                for k in (1, 2, 3)
            ]
            fed = [
                feed_both(layer, place, seconds[k], lows[k], wgu[layer], wd[layer])
                for k in range(4)
            ]
        else:
            fed = [feed(layer, place, s, wgu[layer], wd[layer]) for s in seconds]
        parts = [fed[0][2]] + [z_shift(fed[k][2], -k) for k in (1, 2, 3)]
        base = resid
        saved.append(
            dict(
                x=x_in, q=q, mixed=mixed, lse=lse, kvs=kvs, resid=resid,
                normed=normed,
                seconds=seconds, gu=[f[0] for f in fed], hidden=[f[1] for f in fed],
            )
        )
    outputs = [saved[1]["x"], add(base, *parts)]

    grad = own_cotangent
    input_grads = [None, None]
    feed_halves = [None, None]
    kept = [None, None]

    def stage_one(half):
        cut = [half[4 * k : 4 * k + 4] for k in range(4)]
        return add(cut[0], *[reduce_shift(cut[k], k) for k in (1, 2, 3)])

    def stage_two(stage):
        low = stage.astype(BF)
        return add(stage[0], *[gather_shift(low[k], k) for k in (1, 2, 3)])

    for layer in (1, 0):
        s = saved[layer]
        gain_one = gain_pair[layer][0:1]
        gain_two = gain_pair[layer][1:2]
        if layer:
            back = [(f[0], f[3]) for f in fed]
        else:
            back = [
                feed_back(layer, place, lows[k], s["gu"][k], wgu[layer], wd[layer]) for k in range(4)
            ]
        parts = [back[0][1]] + [z_shift(back[k][1], -k) for k in (1, 2, 3)]
        keep, give = feed_grads(info, s["seconds"], [b[0] for b in back], s["hidden"], lows)
        mark = token(keep)
        d_resid, d_low, dc_two, dq, *goes_out = attend_back(
            info, parts, grad, s["resid"], gain_two, gathered[layer], s["mixed"], s["q"],
            s["lse"], s["kvs"], cosine, sine, after=(mark,),
        )
        feed_halves[layer] = add(keep, swap(give)).astype(BF)
        row = add(goes_out[0], *[reduce_shift(goes_out[k], k) for k in (1, 2, 3)])
        row = row.astype(BF).reshape(4, ROWS, 2 * KW)
        own_pieces = [row[0]] + [gather_shift(row[k], k) for k in (1, 2, 3)]
        ahead = first_ahead
        if layer:
            gap = jnp.zeros((ROWS, QP - D), BF)
            ahead = jnp.concatenate([s["normed"], gap, s["mixed"]], axis=1)
            ahead = lax.all_gather(hold([ahead], mark)[0], "wsh")
        if layer == 0:
            kept[1] = attention_grads(none_of(d_low[0, 0]))
        cut, grad, dc_one = project_back(
            info, own_pieces, dq, d_resid, d_low, s["x"], gain_one, gathered[layer], cosine, sine,
            after=(token(ahead),) if layer else (),
        )
        input_grads[layer] = grad
        if layer:
            lows = z_gather(grad.astype(BF))

        def attention_grads(later, after=(), cut=cut, ahead=ahead, dc_one=dc_one, dc_two=dc_two):
            mines = [lax.dynamic_index_in_dim(cut, k + later, 0, False) for k in range(4)]
            mines = [mines[0]] + [z_shift(mines[k], k) for k in (1, 2, 3)]
            keep, give = attend_grads(info, mines, ahead, dc_one, dc_two, after)
            return add(keep, swap(give)).astype(BF)

        if layer == 0:
            feed_stage = stage_one(jnp.concatenate(hold(feed_halves, token(row)), axis=1))
            kept[0] = attention_grads(0, (token(feed_stage),))
    attend_stage = stage_one(jnp.concatenate(kept, axis=2))
    both_sums = stage_two(
        jnp.concatenate(
            [feed_stage[:, :96], feed_stage[:, 96:], jnp.pad(attend_stage, ((0, 0), (0, 32), (0, 0)))],
            axis=2,
        )
    )
    feed_sums = (both_sums[:, :640], both_sums[:, 640:1280])
    attend_sum = both_sums[:64, 1280:]
    sums = [
        jnp.concatenate(
            [feed_sums[layer], jnp.pad(attend_sum[:, layer * 384 : (layer + 1) * 384], ((0, 32), (0, 0)))],
            axis=1,
        )
        for layer in range(2)
    ]

    mine = jnp.where(first_core, sums[0], sums[1])
    other = swap(jnp.where(first_core, sums[1], sums[0]))
    halves = (jnp.where(first_core, mine, other), jnp.where(first_core, other, mine))
    joined = jnp.concatenate([h[:60] for h in halves], axis=1).reshape(4, 15, 2048)
    pieces = [lax.dynamic_index_in_dim(joined, z_rank, 0, False)] + [
        z_shift(lax.dynamic_index_in_dim(joined, (z_rank + k) % 4, 0, False), k) for k in (1, 2, 3)
    ]
    down = jnp.concatenate(
        [
            jnp.concatenate(
                [h[60:80, :640], jnp.concatenate([h[80:90, :320], h[80:90, 320:640]], axis=0)], axis=1
            )
            for h in halves
        ],
        axis=0,
    )
    moves = [(c * 4 + z, (4 * z + c // 4) * 4 + c % 4) for c in range(16) for z in range(4)]
    grad_down = lax.ppermute(down, ("ctx", "wsh"), moves)[None]
    sum_one, gq, gk, gv, go, sum_two, gate, up = finish(info, pieces)
    grad_query, grad_key, grad_value, grad_out, grad_gate, grad_up = (
        jnp.swapaxes(g, 0, 1) for g in (gq, gk, gv, go, gate, up)
    )

    def arranged(pair):
        mine = jnp.where(first_core, pair[0], pair[1])
        other = swap(jnp.where(first_core, pair[1], pair[0]))
        first = jnp.where(first_core, mine, other)
        last = jnp.where(first_core, other, mine)
        return jnp.stack([first, last])[None, :, None]

    return (
        arranged(outputs),
        arranged(input_grads),
        sum_one[:, 0][None],
        grad_query,
        grad_key,
        grad_value,
        grad_out,
        sum_two[:, 0][None],
        grad_gate,
        grad_up,
        grad_down,
    )


def solution(mesh):
    rows = P(None, "wsh", "ctx", None)
    gain = P("section", "wsh")
    weight = P("section", "wsh", None)
    in_specs = (rows, rows, P(), gain, weight, weight, weight, weight, gain, weight, weight, weight)
    result = P("section", None, "wsh", "ctx", None)
    gain_out = P("section", ("ctx", "wsh"))
    weight_out = P("section", ("ctx", "wsh"), None)
    out_specs = (
        result, result, gain_out, weight_out, weight_out, weight_out, weight_out, gain_out,
        weight_out, weight_out, weight_out,
    )
    return jax.shard_map(shards, mesh=mesh, in_specs=in_specs, out_specs=out_specs, check_vma=False)
```
